32 devices in a mesh: seq: 4 (over y, x), dp: 8 (over z, core).
Axes of the slice: x: 2, y: 2, z: 4, core: 2. Of those that a mesh axis runs over, the one named last changes fastest.
Arguments:
- inputs: bfloat16 [24, 512, 768], P('dp', 'seq'), may hold values from -6 to 6
- masked_positions: int32 [24, 76], P('dp'), may hold values from 0 to 511, as said below
- masked_grads: bfloat16 [24, 76, 768], P('dp'), may hold values from -6 to 6
- kernel_paths: int32 [24, 2], P('dp'), may hold values from 0 to 2, as said below
- attn_weight: float32 [2, 768, 2304], P(None, ('seq', 'dp')), may hold values from -0.21875 to 0.21875
- out_weight: float32 [2, 768, 768], P(None, ('seq', 'dp')), may hold values from -1.75 to 1.75
- point_weight: float32 [2, 768, 768], P(None, ('seq', 'dp')), may hold values from -0.21875 to 0.21875
- depth_weight: float32 [2, 7, 768], P(None, None, ('seq', 'dp')), may hold values from -2 to 2
- gains: float32 [2, 2, 768], P(None, None, ('seq', 'dp')), may hold values from 0.5 to 1.5
- shifts: float32 [2, 5, 768], P(None, None, ('seq', 'dp')), may hold values from -1.2 to 1.2
- first_attn: float32 [2, 768, 2304], P(None, ('seq', 'dp')), may hold values from -160 to 160
- first_out: float32 [2, 768, 768], P(None, ('seq', 'dp')), may hold values from -20 to 20
- first_point: float32 [2, 768, 768], P(None, ('seq', 'dp')), may hold values from -224 to 224
- first_depth: float32 [2, 7, 768], P(None, None, ('seq', 'dp')), may hold values from -320 to 320
- first_gains: float32 [2, 2, 768], P(None, None, ('seq', 'dp')), may hold values from -320 to 320
- first_shifts: float32 [2, 5, 768], P(None, None, ('seq', 'dp')), may hold values from -192 to 192
- second_attn: float32 [2, 768, 2304], P(None, ('seq', 'dp')), may hold values from 307.2 to 1228.8
- second_out: float32 [2, 768, 768], P(None, ('seq', 'dp')), may hold values from 6.144 to 24.576
- second_point: float32 [2, 768, 768], P(None, ('seq', 'dp')), may hold values from 614.4 to 2457.6
- second_depth: float32 [2, 7, 768], P(None, None, ('seq', 'dp')), may hold values from 1228.8 to 4915.2
- second_gains: float32 [2, 2, 768], P(None, None, ('seq', 'dp')), may hold values from 1228.8 to 4915.2
- second_shifts: float32 [2, 5, 768], P(None, None, ('seq', 'dp')), may hold values from 491.52 to 1966.08
Outputs:
- result: bfloat16 [24, 512, 768], P('dp', 'seq')
- input_grad: float32 [24, 512, 768], P('dp', 'seq')
- new_attn: float32 [2, 768, 2304], P(None, ('seq', 'dp'))
- new_out: float32 [2, 768, 768], P(None, ('seq', 'dp'))
- new_point: float32 [2, 768, 768], P(None, ('seq', 'dp'))
- new_depth: float32 [2, 7, 768], P(None, None, ('seq', 'dp'))
- new_gains: float32 [2, 2, 768], P(None, None, ('seq', 'dp'))
- new_shifts: float32 [2, 5, 768], P(None, None, ('seq', 'dp'))
- moment_attn: float32 [2, 768, 2304], P(None, ('seq', 'dp'))
- moment_out: float32 [2, 768, 768], P(None, ('seq', 'dp'))
- moment_point: float32 [2, 768, 768], P(None, ('seq', 'dp'))
- moment_depth: float32 [2, 7, 768], P(None, None, ('seq', 'dp'))
- moment_gains: float32 [2, 2, 768], P(None, None, ('seq', 'dp'))
- moment_shifts: float32 [2, 5, 768], P(None, None, ('seq', 'dp'))
- square_attn: float32 [2, 768, 2304], P(None, ('seq', 'dp'))
- square_out: float32 [2, 768, 768], P(None, ('seq', 'dp'))
- square_point: float32 [2, 768, 768], P(None, ('seq', 'dp'))
- square_depth: float32 [2, 7, 768], P(None, None, ('seq', 'dp'))
- square_gains: float32 [2, 2, 768], P(None, None, ('seq', 'dp'))
- square_shifts: float32 [2, 5, 768], P(None, None, ('seq', 'dp'))
- copy_attn: bfloat16 [2, 768, 2304], P(None, ('seq', 'dp'))
- copy_out: bfloat16 [2, 768, 768], P(None, ('seq', 'dp'))
- copy_point: bfloat16 [2, 768, 768], P(None, ('seq', 'dp'))
- copy_depth: bfloat16 [2, 7, 768], P(None, None, ('seq', 'dp'))
- copy_gains: bfloat16 [2, 2, 768], P(None, None, ('seq', 'dp'))
- copy_shifts: bfloat16 [2, 5, 768], P(None, None, ('seq', 'dp'))
The draws below stay inside these ranges and needn't reach their ends.
Inputs may be any that keep to these rules, and one draw needn't show every extreme that they name: `masked_positions`: each row holds 76 distinct token positions of its sequence. Sequence s in block b uses a centred kernel of 2 kernel_paths[s, b] + 3 taps.
All inputs are finite; a program needn't handle non-finite values.
Results may differ from the reference program's by a relative error of at most 0.034.
Values may be sent and summed in bfloat16 or wider, within the bound.
No kernel may reach another device: no remote copies, remote signals or barrier semaphores. Data moves between devices by JAX's collectives and lax.ppermute only.
A program may use at most 192 MiB of HBM per device.

```python
import math
from functools import partial
import jax
import jax.numpy as jnp
from jax import lax

D = 768
HEADS = 12
TAPS = 7
BLOCKS = 2
STEP = 10
SEQ_LEN = 512
SEQS = 24
MASKED = 76


def draw_masked_positions(key, part):
    key = jax.random.fold_in(key, 11)
    row_keys = jax.random.split(key, SEQS)
    rows = jax.vmap(lambda row_key: jax.random.permutation(row_key, SEQ_LEN)[:MASKED])(row_keys)
    return rows.astype(jnp.int32)


def draw_kernel_paths(key, part):
    key = jax.random.fold_in(key, 13)
    value_key, row_key = jax.random.split(key)
    values = jax.random.randint(value_key, (SEQS, BLOCKS), 0, 3, dtype=jnp.int32)
    chosen = jax.random.randint(row_key, (), 0, SEQS, dtype=jnp.int32)
    pattern = 2 - 2 * (jnp.arange(BLOCKS, dtype=jnp.int32) % 2)
    values = values.at[chosen].set(pattern)
    return values.astype(jnp.int32)


def block_scale(rng, dims, cuts, least, largest):
    level, own = 1.0, jax.random.fold_in(rng, 6)
    for dim, shards_of in cuts:
        steps = jnp.exp(jax.random.uniform(jax.random.fold_in(own, dim), (shards_of,), jnp.float32, least / len(cuts), largest / len(cuts)))
        level = level * jnp.repeat(steps, dims[dim] // shards_of).reshape([-1 if axis == dim else 1 for axis in range(len(dims))])
    return level


def noise(key, extent, deviation, bound, cuts=(), held_as=jnp.bfloat16):
    level = block_scale(key, extent, cuts, -0.22, 0.18) if cuts else 1.0
    values = jax.random.normal(key, extent, jnp.float32) * deviation * level
    return jnp.minimum(jnp.maximum(values, -bound), bound).astype(held_as)


def setup_inputs(seed: int = 0) -> dict:
    key_list = jax.random.split(jax.random.key(seed), 23)
    return {
        "inputs": noise(key_list[0], (SEQS, SEQ_LEN, D), 1.0, 6.0, ((0, 8), (1, 4))),
        "masked_positions": draw_masked_positions(jax.random.fold_in(key_list[22], 71), 0),
        "masked_grads": noise(key_list[2], (SEQS, MASKED, D), 1.0, 6.0, ((0, 8),)),
        "kernel_paths": draw_kernel_paths(jax.random.fold_in(key_list[22], 71), 0),
        "attn_weight": noise(key_list[4], (BLOCKS, D, 3 * D), D ** -0.5, 0.21875, ((1, 32),), jnp.float32),
        "out_weight": noise(key_list[5], (BLOCKS, D, D), (D // 64) ** -0.5, 1.75, ((1, 32),), jnp.float32),
        "point_weight": noise(key_list[6], (BLOCKS, D, D), D ** -0.5, 0.21875, ((1, 32),), jnp.float32),
        "depth_weight": noise(key_list[7], (BLOCKS, TAPS, D), TAPS ** -0.5, 2.0, ((2, 32),), jnp.float32),
        "gains": jnp.clip(1.0 + 0.1 * jax.random.normal(key_list[8], (BLOCKS, 2, D), jnp.float32), 0.5, 1.5),
        "shifts": noise(key_list[9], (BLOCKS, 5, D), 0.2, 1.2, ((2, 32),), jnp.float32),
        "first_attn": noise(key_list[10], (BLOCKS, D, 3 * D), ((0.05 * SEQS * SEQ_LEN) ** 0.5), 160.0, ((1, 32),), jnp.float32),
        "first_out": noise(key_list[11], (BLOCKS, D, D), ((0.001 * SEQS * SEQ_LEN) ** 0.5), 20.0, ((1, 32),), jnp.float32),
        "first_point": noise(key_list[12], (BLOCKS, D, D), ((0.1 * SEQS * SEQ_LEN) ** 0.5), 224.0, ((1, 32),), jnp.float32),
        "first_depth": noise(key_list[13], (BLOCKS, TAPS, D), ((0.2 * SEQS * SEQ_LEN) ** 0.5), 320.0, ((2, 32),), jnp.float32),
        "first_gains": noise(key_list[14], (BLOCKS, 2, D), ((0.2 * SEQS * SEQ_LEN) ** 0.5), 320.0, ((2, 32),), jnp.float32),
        "first_shifts": noise(key_list[15], (BLOCKS, 5, D), ((0.08 * SEQS * SEQ_LEN) ** 0.5), 192.0, ((2, 32),), jnp.float32),
        "second_attn": jnp.clip(jnp.exp(math.log(1228.8) - 1.3862944 * jax.random.uniform(key_list[16], (BLOCKS, D, 3 * D), jnp.float32) ** block_scale(key_list[16], (BLOCKS, D, 3 * D), ((1, 32),), -0.2, 0.2)), 307.2, 1228.8),
        "second_out": jnp.clip(jnp.exp(math.log(24.576) - 1.3862944 * jax.random.uniform(key_list[17], (BLOCKS, D, D), jnp.float32) ** block_scale(key_list[17], (BLOCKS, D, D), ((1, 32),), -0.2, 0.2)), 6.144, 24.576),
        "second_point": jnp.clip(jnp.exp(math.log(2457.6) - 1.3862944 * jax.random.uniform(key_list[18], (BLOCKS, D, D), jnp.float32) ** block_scale(key_list[18], (BLOCKS, D, D), ((1, 32),), -0.2, 0.2)), 614.4, 2457.6),
        "second_depth": jnp.clip(jnp.exp(math.log(4915.2) - 1.3862944 * jax.random.uniform(key_list[19], (BLOCKS, TAPS, D), jnp.float32) ** block_scale(key_list[19], (BLOCKS, TAPS, D), ((2, 32),), -0.2, 0.2)), 1228.8, 4915.2),
        "second_gains": jnp.clip(jnp.exp(math.log(4915.2) - 1.3862944 * jax.random.uniform(key_list[20], (BLOCKS, 2, D), jnp.float32) ** block_scale(key_list[20], (BLOCKS, 2, D), ((2, 32),), -0.2, 0.2)), 1228.8, 4915.2),
        "second_shifts": jnp.clip(jnp.exp(math.log(1966.08) - 1.3862944 * jax.random.uniform(key_list[21], (BLOCKS, 5, D), jnp.float32) ** block_scale(key_list[21], (BLOCKS, 5, D), ((2, 32),), -0.2, 0.2)), 491.52, 1966.08),
    }


@jax.custom_vjp
def low(v):
    return lax.optimization_barrier(v.astype(jnp.bfloat16)).astype(jnp.float32)

@jax.custom_vjp
def low_back(v):
    return v

def low_keep(v):
    return (low(v), None)

def low_pass(kept, grad):
    return (grad,)

def back_keep(v):
    return (v, None)

def back_low(kept, grad):
    return (low(grad),)
low.defvjp(low_keep, low_pass)
low_back.defvjp(back_keep, back_low)
norm_eps = 1e-05
beta_first = 0.5
beta_second = 0.5
adam_eps = 1e-08
weight_decay = 0.01
rate_attn = 0.03
rate_out = 0.25
rate_point = 0.03
rate_depth = 0.3
rate_gain = 0.45
rate_vector = 0.2

def layer_norm(stream, gain_row, shift_row):
    center = stream - lax.optimization_barrier(jnp.mean(stream, axis=-1, keepdims=True))
    variance = lax.optimization_barrier(jnp.mean(center * center, axis=-1, keepdims=True))
    inverse = lax.rsqrt(variance + norm_eps)
    normed = center * inverse
    return normed * gain_row + shift_row

def tap_mask(paths, taps):
    offsets = jnp.abs(jnp.arange(taps, dtype=jnp.int32) - taps // 2)
    return (offsets[None, :] <= paths[:, None] + 1).astype(jnp.float32)

def attend(parts, head_count, score_scale):
    queries, key_rows, value_rows = parts
    length, model_width = queries.shape
    head_size = model_width // head_count
    query_heads = queries.reshape(length, head_count, head_size)
    key_heads = key_rows.reshape(length, head_count, head_size)
    value_heads = value_rows.reshape(length, head_count, head_size)
    scores = low_back(jnp.einsum('the,lhe->htl', query_heads, key_heads, precision=lax.Precision.HIGHEST) * score_scale)
    maxima = lax.optimization_barrier(jnp.max(scores, axis=-1, keepdims=True))
    exponent = jnp.exp(scores - maxima)
    attn_probs = low(exponent / lax.optimization_barrier(jnp.sum(exponent, axis=-1, keepdims=True)))
    mixture = jnp.einsum('htl,lhe->the', attn_probs, value_heads, precision=lax.Precision.HIGHEST)
    return mixture.reshape(length, model_width)

def block_forward(stream, attention_matrix, output_matrix, pointwise_matrix, depth_mat, gain_rows, shifted_rows, paths):
    seq_count, length, model_width = stream.shape
    head_count = HEADS
    score_scale = (model_width // head_count) ** (-0.5)
    half_width = depth_mat.shape[0] // 2
    flowing_lowered = low(stream)
    project_output = jnp.einsum('nck,kf->ncf', flowing_lowered, attention_matrix, precision=lax.Precision.HIGHEST)
    proj_bias = jnp.concatenate([shifted_rows[2], jnp.zeros((2 * model_width,), jnp.float32)])
    project_output = low(low_back(project_output + proj_bias))
    queries = project_output[..., :model_width]
    key_rows = project_output[..., model_width:2 * model_width]
    value_rows = project_output[..., 2 * model_width:]
    mixture = lax.map(jax.checkpoint(partial(attend, head_count=head_count, score_scale=score_scale)), (queries, key_rows, value_rows))
    mixed_lowered = low(low_back(mixture))
    branch_output = low_back(jnp.einsum('nck,kf->ncf', mixed_lowered, output_matrix, precision=lax.Precision.HIGHEST) + shifted_rows[3])
    middle = layer_norm(stream + branch_output, gain_rows[0], shifted_rows[0])
    middle_low = low(middle)
    padded = jnp.pad(middle_low, ((0, 0), (half_width, half_width), (0, 0)))
    tap_weights = depth_mat[None, :, :] * tap_mask(paths, depth_mat.shape[0])[:, :, None]
    convolved = jnp.zeros_like(middle)
    for offset in range(2 * half_width + 1):
        convolved = convolved + tap_weights[:, offset][:, None, :] * padded[:, offset:offset + length]
    convolution_lowered = low(low_back(convolved))
    pointwise_mixing = low_back(jnp.einsum('nck,kf->ncf', convolution_lowered, pointwise_matrix, precision=lax.Precision.HIGHEST) + shifted_rows[4])
    return layer_norm(middle + pointwise_mixing, gain_rows[1], shifted_rows[1])

def forward(stream, weight_set, paths):
    for block_num in range(weight_set[0].shape[0]):
        stream = block_forward(stream, weight_set[0][block_num], weight_set[1][block_num], weight_set[2][block_num], weight_set[3][block_num], weight_set[4][block_num], weight_set[5][block_num], paths[:, block_num])
    return stream

def adam_update(master, first, second, gradient, step_rate):
    first_new = beta_first * first + (1.0 - beta_first) * gradient
    second_new = beta_second * second + (1.0 - beta_second) * gradient * gradient
    first_hat = first_new / (1.0 - beta_first ** STEP)
    second_hat = second_new / (1.0 - beta_second ** STEP)
    updated = master - step_rate * (first_hat / (jnp.sqrt(second_hat) + adam_eps) + weight_decay * master)
    return (updated, first_new, second_new, updated.astype(jnp.bfloat16))

def reference(inputs, masked_positions, masked_grads, kernel_paths, attn_weight, out_weight, point_weight, depth_weight, gains, shifts, first_attn, first_out, first_point, first_depth, first_gains, first_shifts, second_attn, second_out, second_point, second_depth, second_gains, second_shifts):
    seq_count, length, model_width = inputs.shape
    masters = (attn_weight, out_weight, point_weight, depth_weight, gains, shifts)
    weight_set = tuple((master.astype(jnp.bfloat16).astype(jnp.float32) for master in masters))
    group_size = math.gcd(seq_count, 8)
    batches = seq_count // group_size

    def step_group(totals, batch):
        stream, places, incoming_gradients, paths = batch

        def run_forward(flowing, weight_tuple):
            return forward(flowing, weight_tuple, paths)
        output, pullback = jax.vjp(run_forward, stream.astype(jnp.float32), weight_set)
        branch_picks = (places[:, None, :] == jnp.arange(length, dtype=jnp.int32)[None, :, None]).astype(jnp.float32)
        output_gradient = jnp.einsum('guq,gqy->guy', branch_picks, incoming_gradients.astype(jnp.float32), precision=lax.Precision.HIGHEST)
        grad_input, grad_weights = pullback(output_gradient)
        totals = jax.tree.map(lambda left, right: left + right, totals, grad_weights)
        return (totals, (output.astype(jnp.bfloat16), grad_input))
    zero_set = jax.tree.map(jnp.zeros_like, weight_set)
    grouped_inputs = inputs.reshape(batches, group_size, length, model_width)
    grouped_places = masked_positions.reshape(batches, group_size, masked_positions.shape[1])
    grouped_grads = masked_grads.reshape(batches, group_size, masked_grads.shape[1], model_width)
    grouped_paths = kernel_paths.reshape(batches, group_size, kernel_paths.shape[1])
    totals, (outputs, input_grads) = lax.scan(step_group, zero_set, (grouped_inputs, grouped_places, grouped_grads, grouped_paths))
    firsts = (first_attn, first_out, first_point, first_depth, first_gains, first_shifts)
    seconds = (second_attn, second_out, second_point, second_depth, second_gains, second_shifts)
    rates = (rate_attn, rate_out, rate_point, rate_depth, rate_gain, rate_vector)
    updates = [adam_update(masters[member], firsts[member], seconds[member], totals[member], rates[member]) for member in range(6)]
    result = outputs.reshape(seq_count, length, model_width)
    input_grad = input_grads.reshape(seq_count, length, model_width)
    return (result, input_grad, updates[0][0], updates[1][0], updates[2][0], updates[3][0], updates[4][0], updates[5][0], updates[0][1], updates[1][1], updates[2][1], updates[3][1], updates[4][1], updates[5][1], updates[0][2], updates[1][2], updates[2][2], updates[3][2], updates[4][2], updates[5][2], updates[0][3], updates[1][3], updates[2][3], updates[3][3], updates[4][3], updates[5][3])
```

```python
from functools import partial

import jax
import jax.numpy as jnp
from jax import lax
from jax.experimental import pallas as pl
from jax.experimental.pallas import tpu as pltpu
from jax.sharding import PartitionSpec as P

HEADS = 12
STEP = 10

norm_eps = 1e-05
beta_first = 0.5
beta_second = 0.5
adam_eps = 1e-08
weight_decay = 0.01
rate_attn = 0.03
rate_out = 0.25
rate_point = 0.03
rate_depth = 0.3
rate_gain = 0.45
rate_vector = 0.2

f32 = jnp.float32
bf16 = jnp.bfloat16
AXES = ("seq", "dp")
VMEM_BYTES = 56 * 2**20
GROUP = 256
ROWS = 64
PAD = 8

GAIN = 7
SHIFT = 9
SMALL = 14


def dot_nn(a, b):
    return lax.dot_general(a, b, (((1,), (0,)), ((), ())), preferred_element_type=f32)


def dot_nt(a, b):
    return lax.dot_general(a, b, (((1,), (1,)), ((), ())), preferred_element_type=f32)


def dot_tn(a, b):
    return lax.dot_general(a, b, (((0,), (0,)), ((), ())), preferred_element_type=f32)


def vmem_spec():
    return pl.BlockSpec(memory_space=pltpu.VMEM)


def smem_spec():
    return pl.BlockSpec(memory_space=pltpu.SMEM)


def any_spec():
    return pl.BlockSpec(memory_space=pl.ANY)


def call(body, outs, in_specs, scratch, cost, name):
    return pl.pallas_call(
        body,
        out_shape=outs,
        in_specs=in_specs,
        out_specs=jax.tree.map(lambda _: vmem_spec(), outs),
        scratch_shapes=scratch,
        compiler_params=pltpu.CompilerParams(vmem_limit_bytes=VMEM_BYTES),
        cost_estimate=pl.CostEstimate(flops=cost, bytes_accessed=4 * 2**20, transcendentals=0),
        name=name,
    )


def row_loop(total, body, rows=ROWS):
    def step(i, carry):
        body(pl.multiple_of(i * rows, rows))
        return carry

    lax.fori_loop(0, total // rows, step, 0)


def weight_copies(meta, pieces, dest, sem, columns=None):
    s, z, c = meta[0], meta[1], meta[2]
    seqs = len(pieces) // 2
    copies = []
    for j in range(2):
        for k in range(seqs):
            piece = pieces[j * seqs + k]
            subs, rows, width = piece.shape
            first, half = columns if columns else (0, width)
            for m in range(subs):
                row = pl.multiple_of(((k ^ s) * subs + (m ^ z)) * rows, rows)
                col = pl.multiple_of((j ^ c) * half, 128)
                copies.append(
                    pltpu.make_async_copy(
                        piece.at[m, :, pl.ds(first, half)] if columns else piece.at[m],
                        dest.at[pl.ds(row, rows), pl.ds(col, half)],
                        sem,
                    )
                )
    return copies


def head_masks(scale):
    lane = lax.broadcasted_iota(jnp.int32, (1, GROUP), 1) // (GROUP // 4)
    return [jnp.where(lane == h, f32(scale), f32(0)).astype(bf16) for h in range(4)]


def attend_kernel(x_parts, seqs, scale, meta, small, *refs):
    x_refs, pieces = refs[:x_parts], refs[x_parts : x_parts + 2 * seqs]
    x_out, xt_out, qkv, o_out, ot_out, lse_out, weight, x_sem, w_sem = refs[x_parts + 2 * seqs :]
    copies = weight_copies(meta, pieces, weight, w_sem)
    for copy in copies:
        copy.start()
    if x_parts > 1:
        part_rows = x_refs[0].shape[0]
        x_copies = [
            pltpu.make_async_copy(
                x_refs[k],
                x_out.at[pl.ds(pl.multiple_of((k ^ meta[0]) * part_rows, part_rows), part_rows)],
                x_sem,
            )
            for k in range(x_parts)
        ]
        for copy in x_copies:
            copy.start()
        for copy in x_copies:
            copy.wait()
    else:
        x_out[...] = x_refs[0][...]
    xt_out[...] = x_out[...].T
    for copy in copies:
        copy.wait()
    tokens, width = x_out.shape
    scaled, plain = head_masks(scale), head_masks(1.0)
    lane = lax.broadcasted_iota(jnp.int32, (tokens, 128), 1)
    sums = jnp.zeros((tokens, 128), f32)
    for g in range(width // GROUP):
        cols = slice(g * GROUP, (g + 1) * GROUP)
        cols_k = slice(width + g * GROUP, width + (g + 1) * GROUP)
        cols_v = slice(2 * width + g * GROUP, 2 * width + (g + 1) * GROUP)
        bias = small[SHIFT + 2 : SHIFT + 3, cols]
        qkv[:, cols] = (dot_nn(x_out[...], weight[:, cols]) + bias).astype(bf16)
        qkv[:, cols_k] = dot_nn(x_out[...], weight[:, cols_k]).astype(bf16)
        qkv[:, cols_v] = dot_nn(x_out[...], weight[:, cols_v]).astype(bf16)
        mixed = jnp.zeros((tokens, GROUP), f32)
        for h in range(4):
            scores = dot_nt(qkv[:, cols] * scaled[h], qkv[:, cols_k])
            top = jnp.max(scores, axis=-1, keepdims=True)
            weights = jnp.exp(scores - top)
            total = jnp.sum(weights, axis=-1, keepdims=True)
            part = dot_nn(weights.astype(bf16), qkv[:, cols_v] * plain[h])
            mixed = mixed + part * (1.0 / total)
            sums = jnp.where(lane == g * 4 + h, top + jnp.log(total), sums)
        o_out[:, cols] = mixed.astype(bf16)
    ot_out[...] = o_out[...].T
    lse_out[...] = sums.T


def tap_rows(meta, small, block, taps):
    path = meta[3 + block]
    half = taps // 2
    return [
        small[j : j + 1, :] * jnp.where(path + 1 >= abs(j - half), f32(1), f32(0))
        for j in range(taps)
    ]


def norm_rows(r, gain, shift):
    center = r - jnp.mean(r, axis=-1, keepdims=True)
    inverse = lax.rsqrt(jnp.mean(center * center, axis=-1, keepdims=True) + norm_eps)
    normed = center * inverse
    return normed * gain + shift, normed, inverse


def mix_kernel(block, seqs, taps, relative, meta, small, x_ref, o_ref, *refs):
    pieces = refs[: 2 * seqs]
    y_out, y_low, xh1, inv1, xh2, inv2, hct, w_out, w_point, acc, y1, zpad, hc, sem = refs[2 * seqs :]
    tokens, width = o_ref.shape
    half = width // 2
    copies = weight_copies(meta, pieces, w_out, sem, (0, half)) + weight_copies(
        meta, pieces, w_point, sem, (half, half)
    )
    for copy in copies:
        copy.start()
    for copy in copies:
        copy.wait()
    zpad[0:PAD, :] = jnp.zeros((PAD, width), f32)
    zpad[tokens + PAD :, :] = jnp.zeros((PAD, width), f32)
    for n in range(width // GROUP):
        cols = slice(n * GROUP, (n + 1) * GROUP)
        acc[:, cols] = dot_nn(o_ref[...], w_out[:, cols])

    def first_norm(row):
        rows = pl.ds(row, ROWS)
        stream = x_ref[rows, :].astype(f32) + (acc[rows, :] + small[SHIFT + 3 : SHIFT + 4, :])
        out, normed, inverse = norm_rows(
            stream, small[GAIN : GAIN + 1, :], small[SHIFT : SHIFT + 1, :]
        )
        y1[rows, :] = out
        xh1[rows, :] = normed
        inv1[rows, :] = inverse
        zpad[pl.ds(row + PAD, ROWS), :] = out.astype(bf16).astype(f32)

    row_loop(tokens, first_norm)
    weights = tap_rows(meta, small, block, taps)
    reach = taps // 2

    def convolve(row):
        window = zpad[pl.ds(row, ROWS + 2 * PAD), :]
        total = jnp.zeros((ROWS, width), f32)
        for j in range(taps):
            start = PAD - reach + j
            total = total + weights[j] * window[start : start + ROWS]
        hc[pl.ds(row, ROWS), :] = total.astype(bf16)

    row_loop(tokens, convolve)
    for n in range(width // GROUP):
        cols = slice(n * GROUP, (n + 1) * GROUP)
        acc[:, cols] = dot_nn(hc[...], w_point[:, cols])

    def second_norm(row):
        rows = pl.ds(row, ROWS)
        stream = y1[rows, :] + (acc[rows, :] + small[SHIFT + 4 : SHIFT + 5, :])
        out, normed, inverse = norm_rows(
            stream, small[GAIN + 1 : GAIN + 2, :], small[SHIFT + 1 : SHIFT + 2, :]
        )
        xh2[rows, :] = normed
        inv2[rows, :] = inverse
        if not relative:
            y_out[rows, :] = out
            y_low[rows, :] = out.astype(bf16)
        else:
            part = tokens // relative
            y_low[(row // part) ^ meta[0], pl.ds(row % part, ROWS), :] = out.astype(bf16)

    row_loop(tokens, second_norm)
    hct[...] = hc[...].T


def norm_rows_back(upstream, normed, inverse, gain):
    scaled = upstream * gain
    inner = (
        scaled
        - jnp.mean(scaled, axis=-1, keepdims=True)
        - normed * jnp.mean(scaled * normed, axis=-1, keepdims=True)
    )
    return inverse * inner


def column_sum(a):
    return jnp.sum(a, axis=0, keepdims=True)


def store_parts(out, columns, value, meta):
    seqs, subs, rows, _ = out.shape
    for k in range(seqs):
        for m in range(subs):
            start = (k * subs + m) * rows
            out[k ^ meta[0], m ^ meta[1], :, columns] = value[start : start + rows].astype(bf16)


def unmix_kernel(block, seqs, taps, last, meta, small, *refs):
    if last:
        places, grads = refs[:2]
        refs = refs[2:]
    else:
        dy_ref = refs[0]
        refs = refs[1:]
    xh2, inv2, xh1, inv1, hct, ot = refs[:6]
    pieces = refs[6 : 6 + 2 * seqs]
    dr1, do_out, keep, send, sums, w_out, w_point, dr2, du, dpad, zpad, sem = refs[6 + 2 * seqs :]
    tokens, width = dr1.shape
    half = width // 2
    copies = weight_copies(meta, pieces, w_point, sem, (half, half)) + weight_copies(
        meta, pieces, w_out, sem, (0, half)
    )
    for copy in copies:
        copy.start()
    sums[...] = jnp.zeros_like(sums)
    if last:
        picked = places.shape[1]
        token = lax.broadcasted_iota(jnp.int32, (tokens, picked), 0)
        live = jnp.where(meta[5] > 0, f32(1), f32(0))
        picks = jnp.where(token == places[...], live, f32(0)).astype(bf16)
        dr2[...] = dot_nn(picks, grads[...])
    for pad in (dpad, zpad):
        pad[0:PAD, :] = jnp.zeros((PAD, width), f32)
        pad[tokens + PAD :, :] = jnp.zeros((PAD, width), f32)

    def second_norm(row):
        rows = pl.ds(row, ROWS)
        dy = dr2[rows, :] if last else dy_ref[rows, :]
        normed = xh2[rows, :]
        back = norm_rows_back(dy, normed, inv2[rows, :], small[GAIN + 1 : GAIN + 2, :])
        low = back.astype(bf16)
        dr2[rows, :] = back
        du[rows, :] = low
        sums[GAIN + 1 : GAIN + 2, :] += column_sum(dy * normed)
        sums[SHIFT + 1 : SHIFT + 2, :] += column_sum(dy)
        sums[SHIFT + 4 : SHIFT + 5, :] += column_sum(low.astype(f32))
        z = xh1[rows, :] * small[GAIN : GAIN + 1, :] + small[SHIFT : SHIFT + 1, :]
        zpad[pl.ds(row + PAD, ROWS), :] = z.astype(bf16).astype(f32)

    row_loop(tokens, second_norm)
    for copy in copies:
        copy.wait()
    c = meta[2]
    mine = pl.ds(pl.multiple_of(c * half, 128), half)
    other = pl.ds(pl.multiple_of((1 - c) * half, 128), half)
    point_cols, out_cols = slice(half, width), slice(0, half)
    for n in range(width // GROUP):
        cols = slice(n * GROUP, (n + 1) * GROUP)
        back = dot_nt(du[...], w_point[cols, :])
        dpad[PAD : PAD + tokens, cols] = back.astype(bf16).astype(f32)
    store_parts(send, point_cols, dot_nn(hct[...], du[:, other]), meta)
    store_parts(keep, point_cols, dot_nn(hct[...], du[:, mine]), meta)
    weights = tap_rows(meta, small, block, taps)
    path = meta[3 + block]
    reach = taps // 2

    def unconvolve(row):
        rows = pl.ds(row, ROWS)
        window = dpad[pl.ds(row, ROWS + 2 * PAD), :]
        z_window = zpad[pl.ds(row, ROWS + 2 * PAD), :]
        here = window[PAD : PAD + ROWS]
        total = dr2[rows, :]
        for j in range(taps):
            start = PAD + reach - j
            total = total + weights[j] * window[start : start + ROWS]
            z_start = PAD - reach + j
            sums[j : j + 1, :] += column_sum(here * z_window[z_start : z_start + ROWS])
        normed = xh1[rows, :]
        back = norm_rows_back(total, normed, inv1[rows, :], small[GAIN : GAIN + 1, :])
        low = back.astype(bf16)
        dr1[rows, :] = back
        du[rows, :] = low
        sums[GAIN : GAIN + 1, :] += column_sum(total * normed)
        sums[SHIFT : SHIFT + 1, :] += column_sum(total)
        sums[SHIFT + 3 : SHIFT + 4, :] += column_sum(low.astype(f32))

    row_loop(tokens, unconvolve)
    for j in range(taps):
        used = jnp.where(path + 1 >= abs(j - reach), f32(1), f32(0))
        sums[j : j + 1, :] = sums[j : j + 1, :] * used
    for n in range(width // GROUP):
        cols = slice(n * GROUP, (n + 1) * GROUP)
        do_out[:, cols] = dot_nt(du[...], w_out[cols, :]).astype(bf16)
    store_parts(send, out_cols, dot_nn(ot[...], du[:, other]), meta)
    store_parts(keep, out_cols, dot_nn(ot[...], du[:, mine]), meta)


def unattend_kernel(scale, meta, qkv, do_ref, lse, xt, dqkv, keep, send, bias):
    tokens, width = do_ref.shape
    scaled, plain = head_masks(scale), head_masks(1.0)
    for g in range(width // GROUP):
        cols = slice(g * GROUP, (g + 1) * GROUP)
        cols_k = slice(width + g * GROUP, width + (g + 1) * GROUP)
        cols_v = slice(2 * width + g * GROUP, 2 * width + (g + 1) * GROUP)
        dq = jnp.zeros((tokens, GROUP), f32)
        dk = jnp.zeros((tokens, GROUP), f32)
        dv = jnp.zeros((tokens, GROUP), f32)
        for h in range(4):
            q = qkv[:, cols] * scaled[h]
            do = do_ref[:, cols] * plain[h]
            scores = dot_nt(qkv[:, cols_k], q)
            probs = jnp.exp(scores - lse[g * 4 + h : g * 4 + h + 1, :])
            dp = dot_nt(qkv[:, cols_v], do)
            weighted = probs * dp
            ds = (weighted - probs * column_sum(weighted)).astype(bf16)
            dv = dv + dot_nn(probs.astype(bf16), do)
            dk = dk + dot_nn(ds, q)
            dq = dq + dot_tn(ds, qkv[:, cols_k] * scaled[h])
        low = dq.astype(bf16)
        dqkv[:, cols] = low
        bias[:, cols] = column_sum(low.astype(f32))
        dqkv[:, cols_k] = dk.astype(bf16)
        dqkv[:, cols_v] = dv.astype(bf16)
    half = 3 * width // 2
    part = half // 3
    for out, j in ((send, 1 - meta[2]), (keep, meta[2])):
        for t in range(3):
            cols = pl.ds(pl.multiple_of(j * half + t * part, 128), part)
            store_parts(out, slice(t * part, (t + 1) * part), dot_nn(xt[...], dqkv[:, cols]), meta)


def unproject_kernel(seqs, relative, meta, dqkv, dr1, *refs):
    pieces = refs[: 2 * seqs]
    out, weight, sem = refs[2 * seqs :]
    copies = weight_copies(meta, pieces, weight, sem)
    for copy in copies:
        copy.start()
    for copy in copies:
        copy.wait()
    tokens, width = dr1.shape
    for n in range(width // GROUP):
        cols = slice(n * GROUP, (n + 1) * GROUP)
        value = dr1[:, cols] + dot_nt(dqkv[...], weight[cols, :])
        if not relative:
            out[:, cols] = value
        else:
            part = tokens // relative
            for t in range(relative):
                out[t ^ meta[0], :, cols] = value[t * part : (t + 1) * part].astype(bf16)


def adam_update(master, first, second, gradient, step_rate):
    first_new = beta_first * first + (1.0 - beta_first) * gradient
    second_new = beta_second * second + (1.0 - beta_second) * gradient * gradient
    first_hat = first_new / (1.0 - beta_first**STEP)
    second_hat = second_new / (1.0 - beta_second**STEP)
    updated = master - step_rate * (
        first_hat / (jnp.sqrt(second_hat) + adam_eps) + weight_decay * master
    )
    return (updated, first_new, second_new, updated.astype(jnp.bfloat16))


class Links:
    def __init__(self, seqs, copies):
        self.seqs, self.copies, self.ring = seqs, copies, copies // 2
        self.s = lax.axis_index("seq")
        position = lax.axis_index("dp")
        self.z, self.c = position // 2, position % 2

    def swap(self, array, seq=0, ring=0, core=0):
        pairs = [
            (s * self.copies + d, (s ^ seq) * self.copies + (d ^ (2 * ring + core)))
            for s in range(self.seqs)
            for d in range(self.copies)
        ]
        return lax.ppermute(array, AXES, pairs)

    def by_core(self, first, second):
        return (
            jnp.where(self.c == 0, first, second),
            jnp.where(self.c == 0, second, first),
        )

    def aligned(self, rows):
        return (2 * rows) % 16 == 0

    def gather(self, first, second):
        rows, half = first.shape
        own, other = self.by_core(first, second)
        given = self.swap(other, core=1)
        unit = jnp.concatenate(self.by_core(own, given), axis=0)
        units = [unit] + [self.swap(unit, ring=m) for m in range(1, self.ring)]
        if self.aligned(rows):
            block = jnp.stack(units)
        else:
            block = jnp.zeros((self.ring, 2 * rows, half), unit.dtype)
            for m, piece in enumerate(units):
                block = lax.dynamic_update_slice(
                    block, piece[None], (self.z ^ m, jnp.int32(0), jnp.int32(0))
                )
            block = block.reshape(1, self.ring * 2 * rows, half)
        blocks = [block] + [self.swap(block, seq=k) for k in range(1, self.seqs)]
        return blocks + [self.swap(piece, core=1) for piece in blocks]

    def reduce(self, keep, send, rows):
        given = self.swap(send, core=1)
        half = keep.shape[-1]
        sums = [keep[k].astype(f32) + given[k].astype(f32) for k in range(self.seqs)]
        total = sums[0]
        for k in range(1, self.seqs):
            total = total + self.swap(sums[k].astype(bf16), seq=k).astype(f32)
        total = total.reshape(self.ring, 2 * rows, half)
        if self.aligned(rows):
            units = [total[m] for m in range(self.ring)]
        else:
            units = [
                lax.dynamic_index_in_dim(total, self.z ^ m, 0, keepdims=False)
                for m in range(self.ring)
            ]
        unit = units[0]
        for m in range(1, self.ring):
            unit = unit + self.swap(units[m].astype(bf16), ring=m).astype(f32)
        own, other = self.by_core(unit[:rows], unit[rows:])
        given = self.swap(other.astype(bf16), core=1).astype(f32)
        return jnp.concatenate(self.by_core(own, given), axis=1)


def shards(
    inputs,
    masked_positions,
    masked_grads,
    kernel_paths,
    attn_weight,
    out_weight,
    point_weight,
    depth_weight,
    gains,
    shifts,
    first_attn,
    first_out,
    first_point,
    first_depth,
    first_gains,
    first_shifts,
    second_attn,
    second_out,
    second_point,
    second_depth,
    second_gains,
    second_shifts,
):
    seq_count, part_tokens, width = inputs.shape
    seqs, copies = lax.axis_size("seq"), lax.axis_size("dp")
    devices = seqs * copies
    tokens = seqs * part_tokens
    blocks, rows, _ = attn_weight.shape
    taps = depth_weight.shape[1]
    scale = (width // HEADS) ** (-0.5)
    links = Links(seqs, copies)
    subs = links.ring if links.aligned(rows) else 1
    part_rows = width // (seqs * subs)
    half = 3 * width // 2
    place = links.s
    mine = jnp.minimum(place, seq_count - 1)
    live = (place < seq_count).astype(jnp.int32)
    own_paths = lax.dynamic_index_in_dim(kernel_paths, mine, 0, keepdims=False)
    meta = jnp.concatenate(
        [
            jnp.stack([place, links.z if subs > 1 else jnp.zeros_like(links.z), links.c]),
            own_paths,
            live[None],
        ]
    ).astype(jnp.int32)
    own_places = lax.dynamic_index_in_dim(masked_positions, mine, 0, keepdims=True)
    own_grads = lax.dynamic_index_in_dim(masked_grads, mine, 0, keepdims=False)

    small_local = jnp.concatenate([depth_weight, gains, shifts], axis=1).astype(bf16)
    small_all = lax.all_gather(small_local, AXES, axis=0, tiled=False)
    small_all = jnp.moveaxis(small_all, 0, 2).reshape(blocks, SMALL, width).astype(f32)
    small_all = jnp.pad(small_all, ((0, 0), (0, 2), (0, 0)))

    def sent_to(k):
        return lax.dynamic_index_in_dim(
            inputs, jnp.minimum(place ^ k, seq_count - 1), 0, keepdims=False
        )

    x_parts = [sent_to(0)] + [links.swap(sent_to(k), seq=k) for k in range(1, seqs)]

    attn_pieces, mix_pieces = [], []
    for b in range(blocks):
        low = attn_weight[b].astype(bf16)
        attn_pieces.append(links.gather(low[:, :half], low[:, half:]))
        low_out, low_point = out_weight[b].astype(bf16), point_weight[b].astype(bf16)
        cut = width // 2
        mix_pieces.append(
            links.gather(
                jnp.concatenate([low_out[:, :cut], low_point[:, :cut]], axis=1),
                jnp.concatenate([low_out[:, cut:], low_point[:, cut:]], axis=1),
            )
        )

    def shape(*dims, dtype=f32):
        return jax.ShapeDtypeStruct(dims, dtype)

    dma = pltpu.SemaphoreType.DMA
    square = (width, width)
    x_low, x_full = None, None
    saved = []
    for b in range(blocks):
        parts = x_parts if b == 0 else [x_low]
        x16, xt, qkv, o, ot, lse = call(
            partial(attend_kernel, len(parts), seqs, scale),
            (
                shape(tokens, width, dtype=bf16),
                shape(width, tokens, dtype=bf16),
                shape(tokens, 3 * width, dtype=bf16),
                shape(tokens, width, dtype=bf16),
                shape(width, tokens, dtype=bf16),
                shape(128, tokens),
            ),
            [smem_spec(), vmem_spec()]
            + [any_spec() if b == 0 else vmem_spec()] * len(parts)
            + [any_spec()] * (2 * seqs),
            [pltpu.VMEM((width, 3 * width), bf16), dma, dma],
            8 * 10**9,
            f"attend_{b}",
        )(meta, small_all[b], *parts, *attn_pieces[b])
        final = b == blocks - 1
        y, y_low, xh1, inv1, xh2, inv2, hct = call(
            partial(mix_kernel, b, seqs, taps, seqs if final else 0),
            (
                shape(8, 128) if final else shape(tokens, width),
                shape(seqs, part_tokens, width, dtype=bf16)
                if final
                else shape(tokens, width, dtype=bf16),
                shape(tokens, width),
                shape(tokens, 1),
                shape(tokens, width),
                shape(tokens, 1),
                shape(width, tokens, dtype=bf16),
            ),
            [smem_spec()] + [vmem_spec()] * 3 + [any_spec()] * (2 * seqs),
            [
                pltpu.VMEM(square, bf16),
                pltpu.VMEM(square, bf16),
                pltpu.VMEM((tokens, width), f32),
                pltpu.VMEM((tokens, width), f32),
                pltpu.VMEM((tokens + 2 * PAD, width), f32),
                pltpu.VMEM((tokens, width), bf16),
                dma,
            ],
            8 * 10**9,
            f"mix_{b}",
        )(meta, small_all[b], x16 if b == 0 else x_full, o, *mix_pieces[b])
        saved.append((xt, qkv, ot, lse, xh1, inv1, xh2, inv2, hct))
        x_low, x_full = y_low, y

    def sent_back(array):
        stacked = [array[0]] + [links.swap(array[k], seq=k) for k in range(1, seqs)]
        stacked = jnp.stack(stacked)
        return jnp.stack(
            [
                lax.dynamic_index_in_dim(stacked, place ^ i, 0, keepdims=False)
                for i in range(seq_count)
            ]
        )

    result = sent_back(x_low)
    dy = None
    big = [None] * blocks
    small_grads = [None] * blocks
    for b in reversed(range(blocks)):
        xt, qkv, ot, lse, xh1, inv1, xh2, inv2, hct = saved[b]
        last = b == blocks - 1
        upstream = (own_places, own_grads) if last else (dy,)
        dr1, do, keep, send, sums = call(
            partial(unmix_kernel, b, seqs, taps, last),
            (
                shape(tokens, width),
                shape(tokens, width, dtype=bf16),
                shape(seqs, subs, part_rows, width, dtype=bf16),
                shape(seqs, subs, part_rows, width, dtype=bf16),
                shape(16, width),
            ),
            [smem_spec()] + [vmem_spec()] * (len(upstream) + 7) + [any_spec()] * (2 * seqs),
            [
                pltpu.VMEM(square, bf16),
                pltpu.VMEM(square, bf16),
                pltpu.VMEM((tokens, width), f32),
                pltpu.VMEM((tokens, width), bf16),
                pltpu.VMEM((tokens + 2 * PAD, width), f32),
                pltpu.VMEM((tokens + 2 * PAD, width), f32),
                dma,
            ],
            12 * 10**9,
            f"unmix_{b}",
        )(meta, small_all[b], *upstream, xh2, inv2, xh1, inv1, hct, ot, *mix_pieces[b])
        grad_mix = links.reduce(keep, send, rows)
        dqkv, keep, send, bias = call(
            partial(unattend_kernel, scale),
            (
                shape(tokens, 3 * width, dtype=bf16),
                shape(seqs, subs, part_rows, half, dtype=bf16),
                shape(seqs, subs, part_rows, half, dtype=bf16),
                shape(1, width),
            ),
            [smem_spec()] + [vmem_spec()] * 4,
            [],
            16 * 10**9,
            f"unattend_{b}",
        )(meta, qkv, do, lse, xt)
        grad_attn = links.reduce(keep, send, rows)
        dy = call(
            partial(unproject_kernel, seqs, 0 if b else seqs),
            shape(tokens, width) if b else shape(seqs, part_tokens, width, dtype=bf16),
            [smem_spec()] + [vmem_spec()] * 2 + [any_spec()] * (2 * seqs),
            [pltpu.VMEM((width, 3 * width), bf16), dma],
            6 * 10**9,
            f"unproject_{b}",
        )(meta, dqkv, dr1, *attn_pieces[b])
        cut = width // 2
        big[b] = (
            grad_attn,
            jnp.concatenate([grad_mix[:, :cut], grad_mix[:, width : width + cut]], axis=1),
            jnp.concatenate([grad_mix[:, cut:width], grad_mix[:, width + cut :]], axis=1),
        )
        small_grads[b] = jnp.concatenate([sums[: SHIFT + 2], bias, sums[SHIFT + 3 : SMALL]])
    input_grad = sent_back(dy).astype(f32)

    small_sum = jnp.stack(small_grads).reshape(blocks * SMALL, devices, width // devices)
    small_sum = lax.psum_scatter(
        jnp.moveaxis(small_sum, 1, 0).reshape(devices, -1), AXES, scatter_dimension=0, tiled=True
    ).reshape(blocks, SMALL, width // devices)
    reduced = (
        jnp.stack([big[b][0] for b in range(blocks)]),
        jnp.stack([big[b][1] for b in range(blocks)]),
        jnp.stack([big[b][2] for b in range(blocks)]),
        small_sum[:, :taps],
        small_sum[:, GAIN:SHIFT],
        small_sum[:, SHIFT:SMALL],
    )
    masters = (attn_weight, out_weight, point_weight, depth_weight, gains, shifts)
    firsts = (first_attn, first_out, first_point, first_depth, first_gains, first_shifts)
    seconds = (second_attn, second_out, second_point, second_depth, second_gains, second_shifts)
    rates = (rate_attn, rate_out, rate_point, rate_depth, rate_gain, rate_vector)
    updates = [
        adam_update(
            masters[member], firsts[member], seconds[member], reduced[member], rates[member]
        )
        for member in range(6)
    ]
    return (
        (result, input_grad)
        + tuple((entry[0] for entry in updates))
        + tuple((entry[1] for entry in updates))
        + tuple((entry[2] for entry in updates))
        + tuple((entry[3] for entry in updates))
    )


def solution(mesh):
    sequence = P("dp", "seq", None)
    matrix = P(None, AXES, None)
    vector = P(None, None, AXES)
    weights = (matrix,) * 3 + (vector,) * 3
    return jax.shard_map(
        shards,
        mesh=mesh,
        in_specs=(sequence, P("dp", None), P("dp", None, None), P("dp", None)) + weights * 3,
        out_specs=(sequence, sequence) + weights * 4,
        check_vma=False,
    )
```

```python
from functools import partial

import jax
import jax.numpy as jnp
from jax import lax
from jax.experimental import pallas as pl
from jax.experimental.pallas import tpu as pltpu
from jax.sharding import PartitionSpec as P

HEADS = 12
STEP = 10

norm_eps = 1e-05
beta_first = 0.5
beta_second = 0.5
adam_eps = 1e-08
weight_decay = 0.01
rate_attn = 0.03
rate_out = 0.25
rate_point = 0.03
rate_depth = 0.3
rate_gain = 0.45
rate_vector = 0.2

f32 = jnp.float32
bf16 = jnp.bfloat16
AXES = ("seq", "dp")
VMEM_BYTES = 24 * 2**20
GROUP = 256
ROWS = 64
PAD = 8

GAIN = 7
SHIFT = 9
SMALL = 14
SLOT = 16
LANES = 128


def dot_nn(a, b):
    return lax.dot_general(a, b, (((1,), (0,)), ((), ())), preferred_element_type=f32)


def dot_nt(a, b):
    return lax.dot_general(a, b, (((1,), (1,)), ((), ())), preferred_element_type=f32)


def dot_tn(a, b):
    return lax.dot_general(a, b, (((0,), (0,)), ((), ())), preferred_element_type=f32)


def vmem_spec():
    return pl.BlockSpec(memory_space=pltpu.VMEM)


def smem_spec():
    return pl.BlockSpec(memory_space=pltpu.SMEM)


def any_spec():
    return pl.BlockSpec(memory_space=pl.ANY)


def hbm_spec():
    return pl.BlockSpec(memory_space=pltpu.HBM)


class Stored(jax.ShapeDtypeStruct):
    pass


def call(body, outs, in_specs, args, scratch, cost, name, after=(), carry=()):
    n_in, n_after, n_carry, n_out = len(in_specs), len(after), len(carry), len(outs)

    def kernel(*refs):
        tail = n_in + n_after + n_carry
        body(*refs[:n_in], *refs[tail : tail + n_out], *refs[tail + n_out + n_carry :])

    args = [
        pltpu.with_memory_space_constraint(arg, pltpu.HBM)
        if spec.memory_space == pltpu.HBM
        else arg
        for arg, spec in zip(args, in_specs, strict=True)
    ]
    results = pl.pallas_call(
        kernel,
        out_shape=tuple(
            pltpu.HBM(out.shape, out.dtype) if isinstance(out, Stored) else out for out in outs
        )
        + tuple(jax.ShapeDtypeStruct(a.shape, a.dtype) for a in carry),
        in_specs=list(in_specs) + [vmem_spec()] * n_after + [any_spec()] * n_carry,
        out_specs=tuple(hbm_spec() if isinstance(out, Stored) else vmem_spec() for out in outs)
        + (any_spec(),) * n_carry,
        scratch_shapes=scratch,
        input_output_aliases={n_in + n_after + i: n_out + i for i in range(n_carry)},
        compiler_params=pltpu.CompilerParams(vmem_limit_bytes=VMEM_BYTES),
        cost_estimate=pl.CostEstimate(flops=cost, bytes_accessed=2**18, transcendentals=0),
        name=name,
    )(*args, *after, *carry)
    return (results[:n_out], results[n_out:]) if n_carry else results


TOKEN = jax.ShapeDtypeStruct((8, 128), f32)


def small_call(body, outs, args, name, after=(), scratch=()):
    specs = [vmem_spec()] * len(args)
    return call(body, outs, specs, args, list(scratch), 10**8, name, after)


def join(parts, after=()):
    def kernel(*refs):
        start, (out, mark) = 0, refs[len(parts) :]
        for part in refs[: len(parts)]:
            count = part.shape[0]
            out[start : start + count] = part[...]
            start += count
        mark[...] = jnp.zeros_like(mark)

    rows = sum(part.shape[0] for part in parts)
    out = jax.ShapeDtypeStruct((rows,) + parts[0].shape[1:], parts[0].dtype)
    return small_call(kernel, (out, TOKEN), parts, "join", after)


def fold(groups, after=()):
    terms = [term for group in groups for term in group]
    widths = [group[0].shape[-1] for group in groups]
    lead = terms[0].shape[:-2]
    rows, half = terms[0].shape[-2], lead[0] // 2

    def kernel(*refs):
        ins, (kept, sent, mark) = refs[: len(terms)], refs[len(terms) :]

        def block(out, to, at):
            start, used = 0, 0
            for group, width in zip(groups, widths, strict=True):
                total = ins[used][at].astype(f32)
                for term in ins[used + 1 : used + len(group)]:
                    total = total + term[at].astype(f32)
                out[(*to, slice(None), slice(start, start + width))] = total.astype(bf16)
                start, used = start + width, used + len(group)

        for n in range(half):
            if len(lead) == 1:
                block(kept, (n,), (n,))
                block(sent, (n,), (half + n,))
            else:

                def step(m, carry, n=n):
                    block(kept, (n, m), (n, m))
                    block(sent, (n, m), (half + n, m))
                    return carry

                lax.fori_loop(0, lead[1], step, 0)
        mark[...] = jnp.zeros_like(mark)

    out = jax.ShapeDtypeStruct((half,) + lead[1:] + (rows, sum(widths)), bf16)
    return small_call(kernel, (out, out, TOKEN), terms, "fold", after)


def touch(*arrays):
    def kernel(*refs):
        refs[-1][...] = jnp.zeros_like(refs[-1])

    return small_call(kernel, (TOKEN,), arrays, "touch")[0]


def chunk_copies(source, dest, sem, count=4):
    rows = source.shape[0] // count
    return [
        pltpu.make_async_copy(
            source.at[pl.ds(n * rows, rows)], dest.at[pl.ds(n * rows, rows)], sem
        )
        for n in range(count)
    ]


def row_loop(total, body, rows=ROWS):
    def step(i, carry):
        body(pl.multiple_of(i * rows, rows))
        return carry

    lax.fori_loop(0, total // rows, step, 0, unroll=True)


def flipped(index, count):
    bits, out = count.bit_length() - 1, 0
    for bit in range(bits):
        out = out | (((index >> bit) & 1) << (bits - 1 - bit))
    return out


def weight_copies(meta, pieces, dest, sem, first, half, ring_last=False, whole=False):
    s, z, c = meta[0], meta[1], meta[2]
    copies, first_late = [], pieces[0].shape[0]
    late_count = first_late + pieces[1].shape[0]
    for n, piece in enumerate(pieces):
        late, early, rows, width = piece.shape
        core = (n // 2) ^ c
        for a in range(late):
            for b in range(early):
                outer, inner = (n % 2) * first_late + a, b
                if 2 * first_late == late_count:
                    outer = jnp.where(core == 0, outer, flipped(outer, late_count))
                inner = jnp.where(core == 0, inner, flipped(inner, early))
                if ring_last:
                    row = ((inner ^ s) * late_count + (outer ^ z)) * rows
                else:
                    row = ((outer ^ s) * early + (inner ^ z)) * rows
                row = pl.multiple_of(row, rows)
                source = piece.at[a, b]
                if (first, half) != (0, width):
                    source = piece.at[a, b, :, pl.ds(first, half)]
                if whole:
                    target = dest.at[core, pl.ds(row, rows)]
                else:
                    col = pl.multiple_of(core * half, 128)
                    target = dest.at[pl.ds(row, rows), pl.ds(col, half)]
                copies.append(pltpu.make_async_copy(source, target, sem))
    return copies


def head_masks(scale):
    lane = lax.broadcasted_iota(jnp.int32, (1, GROUP), 1) // (GROUP // 4)
    return [jnp.where(lane == h, f32(scale), f32(0)).astype(bf16) for h in range(4)]


def attend_kernel(block, x_parts, scale, meta, *refs):
    if block:
        table, refs = refs[0], refs[1:]
    x_refs, pieces = refs[:x_parts], refs[x_parts : x_parts + 4]
    refs = refs[x_parts + 4 :]
    if block == 0:
        table, x_far, refs = refs[0], refs[1], refs[2:]
    w_far, xt_far, qkv_far, o_out, ot_far, lse_far, weight, xt, qkv, ot, lse, sems = refs[:12]
    half = weight.shape[1] // 2
    if block == 0:
        extra, x = refs[12:]
        smalls = weight_copies(meta, pieces, extra, sems.at[0], half, LANES, whole=True)
        for copy in smalls:
            copy.start()
        part_rows = x_refs[0].shape[0]
        x_copies = [
            pltpu.make_async_copy(
                x_refs[k],
                x.at[pl.ds(pl.multiple_of((k ^ meta[0]) * part_rows, part_rows), part_rows)],
                sems.at[1],
            )
            for k in range(x_parts)
        ]
        for copy in x_copies:
            copy.start()
    else:
        x = x_refs[0]
    copies = weight_copies(meta, pieces, weight, sems.at[2], 0, half)
    for copy in copies:
        copy.start()
    if block == 0:
        for copy in x_copies:
            copy.wait()
        x_store = pltpu.make_async_copy(x, x_far, sems.at[1])
        x_store.start()
        for copy in smalls:
            copy.wait()
        table[...] = extra[0].astype(f32).T[: table.shape[0]]
    small = table.at[pl.ds(SLOT * block, SLOT)]
    xt[...] = x[...].T
    xt_store = pltpu.make_async_copy(xt, xt_far, sems.at[3])
    xt_store.start()
    for copy in copies:
        copy.wait()
    w_stores = chunk_copies(weight, w_far, sems.at[2])
    for copy in w_stores:
        copy.start()
    tokens, width = x.shape
    scaled, plain = head_masks(scale), head_masks(1.0)
    lane = lax.broadcasted_iota(jnp.int32, (tokens, 128), 1)
    sums = jnp.zeros((tokens, 128), f32)
    for g in range(width // GROUP):
        cols = slice(g * GROUP, (g + 1) * GROUP)
        cols_k = slice(width + g * GROUP, width + (g + 1) * GROUP)
        cols_v = slice(2 * width + g * GROUP, 2 * width + (g + 1) * GROUP)
        bias = small[SHIFT + 2 : SHIFT + 3, cols]
        qkv[:, cols] = (dot_nn(x[...], weight[:, cols]) + bias).astype(bf16)
        qkv[:, cols_k] = dot_nn(x[...], weight[:, cols_k]).astype(bf16)
        qkv[:, cols_v] = dot_nn(x[...], weight[:, cols_v]).astype(bf16)
        for part in (cols, cols_k, cols_v):
            pltpu.make_async_copy(qkv.at[:, part], qkv_far.at[:, part], sems.at[4]).start()
        mixed = jnp.zeros((tokens, GROUP), f32)
        for h in range(4):
            scores = dot_nt(qkv[:, cols] * scaled[h], qkv[:, cols_k])
            top = jnp.max(scores, axis=-1, keepdims=True)
            weights = jnp.exp(scores - top)
            total = jnp.sum(weights, axis=-1, keepdims=True)
            part = dot_nn(weights.astype(bf16), qkv[:, cols_v] * plain[h])
            mixed = mixed + part * (1.0 / total)
            sums = jnp.where(lane == g * 4 + h, top + jnp.log(total), sums)
        o_out[:, cols] = mixed.astype(bf16)
        ot[cols, :] = o_out[:, cols].T
        pltpu.make_async_copy(ot.at[cols], ot_far.at[cols], sems.at[5]).start()
    lse[...] = sums.T
    lse_store = pltpu.make_async_copy(lse, lse_far, sems.at[6])
    lse_store.start()
    if block == 0:
        x_store.wait()
    for copy in w_stores + [lse_store]:
        copy.wait()
    xt_store.wait()
    pltpu.make_async_copy(qkv, qkv_far, sems.at[4]).wait()
    pltpu.make_async_copy(ot, ot_far, sems.at[5]).wait()


def tap_rows(meta, small, block, taps):
    path = meta[3 + block]
    half = taps // 2
    return [
        small[j : j + 1, :] * jnp.where(path + 1 >= abs(j - half), f32(1), f32(0))
        for j in range(taps)
    ]


def norm_rows(r, gain, shift):
    center = r - jnp.mean(r, axis=-1, keepdims=True)
    inverse = lax.rsqrt(jnp.mean(center * center, axis=-1, keepdims=True) + norm_eps)
    normed = center * inverse
    return normed * gain + shift, normed, inverse


def mix_kernel(block, count, ring_last, taps, relative, meta, table, x_ref, o_ref, *refs):
    pieces = refs[:count]
    refs = refs[count:]
    y_far, refs = (None, refs) if relative else (refs[0], refs[1:])
    *outs, x, xh1, xh2, hct, stats, w_out, w_point, acc, y1, zpad, hc, sems = refs
    xh1_far, xh2_far, hct_far, stats_far, w_out_far, w_point_far = outs[-6:]
    y_low = outs[0]
    small = table.at[pl.ds(SLOT * block, SLOT)]
    tokens, width = o_ref.shape
    half = width // 2
    copies = weight_copies(meta, pieces, w_out, sems.at[0], 0, half, ring_last)
    late_copies = weight_copies(meta, pieces, w_point, sems.at[1], half, half, ring_last)
    x_copy = pltpu.make_async_copy(x_ref, x, sems.at[2])
    for copy in copies + [x_copy] + late_copies:
        copy.start()
    zpad[0:PAD, :] = jnp.zeros((PAD, width), f32)
    zpad[tokens + PAD :, :] = jnp.zeros((PAD, width), f32)
    for copy in copies:
        copy.wait()
    stores = chunk_copies(w_out, w_out_far, sems.at[0], 2)
    for copy in stores:
        copy.start()
    for n in range(width // GROUP):
        cols = slice(n * GROUP, (n + 1) * GROUP)
        acc[:, cols] = dot_nn(o_ref[...], w_out[:, cols])
    x_copy.wait()

    def first_norm(row):
        rows = pl.ds(row, ROWS)
        stream = x[rows, :].astype(f32) + (acc[rows, :] + small[SHIFT + 3 : SHIFT + 4, :])
        out, normed, inverse = norm_rows(
            stream, small[GAIN : GAIN + 1, :], small[SHIFT : SHIFT + 1, :]
        )
        y1[rows, :] = out
        xh1[rows, :] = normed
        stats[rows, 0:1] = inverse
        zpad[pl.ds(row + PAD, ROWS), :] = out.astype(bf16).astype(f32)

    row_loop(tokens, first_norm)
    xh1_store = pltpu.make_async_copy(xh1, xh1_far, sems.at[3])
    xh1_store.start()
    weights = tap_rows(meta, small, block, taps)
    reach = taps // 2

    def convolve(row):
        window = zpad[pl.ds(row, ROWS + 2 * PAD), :]
        total = jnp.zeros((ROWS, width), f32)
        for j in range(taps):
            start = PAD - reach + j
            total = total + weights[j] * window[start : start + ROWS]
        hc[pl.ds(row, ROWS), :] = total.astype(bf16)

    row_loop(tokens, convolve)
    hct[...] = hc[...].T
    hct_store = pltpu.make_async_copy(hct, hct_far, sems.at[4])
    hct_store.start()
    for copy in late_copies:
        copy.wait()
    late_stores = chunk_copies(w_point, w_point_far, sems.at[1], 2)
    for copy in late_stores:
        copy.start()
    for n in range(width // GROUP):
        cols = slice(n * GROUP, (n + 1) * GROUP)
        acc[:, cols] = dot_nn(hc[...], w_point[:, cols])

    def second_norm(row):
        rows = pl.ds(row, ROWS)
        stream = y1[rows, :] + (acc[rows, :] + small[SHIFT + 4 : SHIFT + 5, :])
        out, normed, inverse = norm_rows(
            stream, small[GAIN + 1 : GAIN + 2, :], small[SHIFT + 1 : SHIFT + 2, :]
        )
        xh2[rows, :] = normed
        stats[rows, 1:2] = inverse
        pltpu.make_async_copy(xh2.at[rows], xh2_far.at[rows], sems.at[5]).start()
        if not relative:
            y1[rows, :] = out
            pltpu.make_async_copy(y1.at[rows], y_far.at[rows], sems.at[6]).start()
            y_low[rows, :] = out.astype(bf16)
        else:
            y1[rows, :] = out

    row_loop(tokens, second_norm)
    stats_store = pltpu.make_async_copy(stats, stats_far, sems.at[7])
    stats_store.start()
    for k in range(relative):
        part = tokens // relative
        first = pl.multiple_of((k ^ meta[0]) * part, part)
        outs[k][0] = y1[pl.ds(first, part), :].astype(bf16)
    for copy in [xh1_store, hct_store, stats_store] + stores + late_stores:
        copy.wait()
    pltpu.make_async_copy(xh2, xh2_far, sems.at[5]).wait()
    if not relative:
        pltpu.make_async_copy(y1, y_far, sems.at[6]).wait()


def norm_rows_back(upstream, normed, inverse, gain):
    scaled = upstream * gain
    inner = (
        scaled
        - jnp.mean(scaled, axis=-1, keepdims=True)
        - normed * jnp.mean(scaled * normed, axis=-1, keepdims=True)
    )
    return inverse * inner


def column_sum(a):
    return jnp.sum(a, axis=0, keepdims=True)


def store_parts(out, columns, value, meta, core):
    seqs, subs, rows, _ = out.shape
    for k in range(seqs):
        for m in range(subs):
            start = (k * subs + m) * rows
            seq, ring = k ^ meta[0], m ^ meta[1]
            seq = jnp.where(core == 0, flipped(seq, seqs), seq)
            ring = jnp.where(core == 0, flipped(ring, subs), ring)
            out[seq, ring, :, columns] = value[start : start + rows].astype(bf16)


def unmix_kernel(block, taps, last, meta, table, *refs):
    small = table.at[pl.ds(SLOT * block, SLOT)]
    if last:
        places, grads = refs[:2]
        refs = refs[2:]
    else:
        dy_ref = refs[0]
        refs = refs[1:]
    xh1_far, xh2_far, hct_far, stats_far, w_out_far, w_point_far, ot_far, *refs = refs
    dr1, do_out, sums, keep, send, xh2, xh1, hct, ot, stats, *refs = refs
    w_out, w_point, dr2, du, dpad, zpad, sems = refs
    tokens, width = dr1.shape
    half = width // 2
    xh2_copy = pltpu.make_async_copy(xh2_far, xh2, sems.at[0])
    xh1_copy = pltpu.make_async_copy(xh1_far, xh1, sems.at[1])
    hct_copy = pltpu.make_async_copy(hct_far, hct, sems.at[2])
    ot_copy = pltpu.make_async_copy(ot_far, ot, sems.at[3])
    stats_copy = pltpu.make_async_copy(stats_far, stats, sems.at[6])
    copies = chunk_copies(w_point_far, w_point, sems.at[4], 2)
    late_copies = chunk_copies(w_out_far, w_out, sems.at[5], 2)
    for copy in [stats_copy, xh2_copy, xh1_copy, *copies, hct_copy, *late_copies, ot_copy]:
        copy.start()
    sums[...] = jnp.zeros_like(sums)
    if last:
        mine = jnp.minimum(meta[0], places.shape[0] - 1)
        picked = places.shape[2]
        token = lax.broadcasted_iota(jnp.int32, (tokens, picked), 0)
        live = jnp.where(meta[5] > 0, f32(1), f32(0))
        picks = jnp.where(token == places[mine], live, f32(0)).astype(bf16)
        dr2[...] = dot_nn(picks, grads[mine])
    for pad in (dpad, zpad):
        pad[0:PAD, :] = jnp.zeros((PAD, width), f32)
        pad[tokens + PAD :, :] = jnp.zeros((PAD, width), f32)
    stats_copy.wait()
    xh2_copy.wait()
    xh1_copy.wait()

    def second_norm(row):
        rows = pl.ds(row, ROWS)
        dy = dr2[rows, :] if last else dy_ref[rows, :]
        normed = xh2[rows, :]
        back = norm_rows_back(dy, normed, stats[rows, 1:2], small[GAIN + 1 : GAIN + 2, :])
        low = back.astype(bf16)
        dr2[rows, :] = back
        du[rows, :] = low
        sums[GAIN + 1 : GAIN + 2, :] += column_sum(dy * normed)
        sums[SHIFT + 1 : SHIFT + 2, :] += column_sum(dy)
        sums[SHIFT + 4 : SHIFT + 5, :] += column_sum(low.astype(f32))
        z = xh1[rows, :] * small[GAIN : GAIN + 1, :] + small[SHIFT : SHIFT + 1, :]
        zpad[pl.ds(row + PAD, ROWS), :] = z.astype(bf16).astype(f32)

    row_loop(tokens, second_norm)
    for copy in copies:
        copy.wait()
    c = meta[2]
    mine = pl.ds(pl.multiple_of(c * half, 128), half)
    other = pl.ds(pl.multiple_of((1 - c) * half, 128), half)
    point_cols, out_cols = slice(half, width), slice(0, half)
    for n in range(width // GROUP):
        cols = slice(n * GROUP, (n + 1) * GROUP)
        back = dot_nt(du[...], w_point[cols, :])
        dpad[PAD : PAD + tokens, cols] = back.astype(bf16).astype(f32)
    hct_copy.wait()
    store_parts(send, point_cols, dot_nn(hct[...], du[:, other]), meta, 1 - c)
    store_parts(keep, point_cols, dot_nn(hct[...], du[:, mine]), meta, c)
    weights = tap_rows(meta, small, block, taps)
    path = meta[3 + block]
    reach = taps // 2

    def unconvolve(row):
        rows = pl.ds(row, ROWS)
        window = dpad[pl.ds(row, ROWS + 2 * PAD), :]
        z_window = zpad[pl.ds(row, ROWS + 2 * PAD), :]
        here = window[PAD : PAD + ROWS]
        total = dr2[rows, :]
        for j in range(taps):
            start = PAD + reach - j
            total = total + weights[j] * window[start : start + ROWS]
            z_start = PAD - reach + j
            sums[j : j + 1, :] += column_sum(here * z_window[z_start : z_start + ROWS])
        normed = xh1[rows, :]
        back = norm_rows_back(total, normed, stats[rows, 0:1], small[GAIN : GAIN + 1, :])
        low = back.astype(bf16)
        dr1[rows, :] = back
        du[rows, :] = low
        sums[GAIN : GAIN + 1, :] += column_sum(total * normed)
        sums[SHIFT : SHIFT + 1, :] += column_sum(total)
        sums[SHIFT + 3 : SHIFT + 4, :] += column_sum(low.astype(f32))

    row_loop(tokens, unconvolve)
    for j in range(taps):
        used = jnp.where(path + 1 >= abs(j - reach), f32(1), f32(0))
        sums[j : j + 1, :] = sums[j : j + 1, :] * used
    for copy in late_copies:
        copy.wait()
    ot_copy.wait()
    for n in range(width // GROUP):
        cols = slice(n * GROUP, (n + 1) * GROUP)
        do_out[:, cols] = dot_nt(du[...], w_out[cols, :]).astype(bf16)
    store_parts(send, out_cols, dot_nn(ot[...], du[:, other]), meta, 1 - c)
    store_parts(keep, out_cols, dot_nn(ot[...], du[:, mine]), meta, c)


def unattend_kernel(scale, meta, qkv_far, do_ref, lse_far, dqkv, bias, qkv, lse, sems):
    tokens, width = do_ref.shape
    copies = []
    for g in range(width // GROUP):
        for first in (0, width, 2 * width):
            part = slice(first + g * GROUP, first + (g + 1) * GROUP)
            copies.append(
                pltpu.make_async_copy(qkv_far.at[:, part], qkv.at[:, part], sems.at[g])
            )
    lse_copy = pltpu.make_async_copy(lse_far, lse, sems.at[width // GROUP])
    for copy in [lse_copy] + copies:
        copy.start()
    lse_copy.wait()
    scaled, plain = head_masks(scale), head_masks(1.0)
    for g in range(width // GROUP):
        cols = slice(g * GROUP, (g + 1) * GROUP)
        cols_k = slice(width + g * GROUP, width + (g + 1) * GROUP)
        cols_v = slice(2 * width + g * GROUP, 2 * width + (g + 1) * GROUP)
        for copy in copies[3 * g : 3 * g + 3]:
            copy.wait()
        dq = jnp.zeros((tokens, GROUP), f32)
        dk = jnp.zeros((tokens, GROUP), f32)
        dv = jnp.zeros((tokens, GROUP), f32)
        for h in range(4):
            q = qkv[:, cols] * scaled[h]
            do = do_ref[:, cols] * plain[h]
            scores = dot_nt(qkv[:, cols_k], q)
            probs = jnp.exp(scores - lse[g * 4 + h : g * 4 + h + 1, :])
            dp = dot_nt(qkv[:, cols_v], do)
            weighted = probs * dp
            ds = (weighted - probs * column_sum(weighted)).astype(bf16)
            dv = dv + dot_nn(probs.astype(bf16), do)
            dk = dk + dot_nn(ds, q)
            dq = dq + dot_tn(ds, qkv[:, cols_k] * scaled[h])
        low = dq.astype(bf16)
        dqkv[:, cols] = low
        bias[:, cols] = column_sum(low.astype(f32))
        dqkv[:, cols_k] = dk.astype(bf16)
        dqkv[:, cols_v] = dv.astype(bf16)


def attn_grad_kernel(blocks, meta, dqkv, xt_far, *refs):
    count = max(0, 2 * blocks)
    tables = refs[:count]
    keep, send, xt, sem = refs[count : count + 4]
    copies = chunk_copies(xt_far, xt, sem, 2)
    for copy in copies:
        copy.start()
    for copy in copies:
        copy.wait()
    width = xt.shape[0]
    half = 3 * width // 2
    part = half // 3
    for out, j in ((send, 1 - meta[2]), (keep, meta[2])):
        for t in range(3):
            cols = pl.ds(pl.multiple_of(j * half + t * part, 128), part)
            value = dot_nn(xt[...], dqkv[:, cols])
            store_parts(out, slice(t * part, (t + 1) * part), value, meta, j)
    if blocks:
        small = refs[count + 4]
        small[...] = jnp.zeros_like(small)
        for b in range(blocks):
            small[b * SLOT : (b + 1) * SLOT, :] = tables[2 * b][...]
            small[b * SLOT + SHIFT + 2 : b * SLOT + SHIFT + 3, :] = tables[2 * b + 1][...]
        extra = small[...].T
        zero = (meta[2] == 0).astype(f32)
        store_parts(keep, slice(half, half + LANES), extra * zero, meta, meta[2])
        store_parts(send, slice(half, half + LANES), extra * (1 - zero), meta, 1 - meta[2])


def unproject_kernel(relative, meta, dqkv, dr1, w_far, *refs):
    outs, weight, dx, sem = refs[:-3], refs[-3], refs[-2], refs[-1]
    copies = chunk_copies(w_far, weight, sem)
    for copy in copies:
        copy.start()
    for copy in copies:
        copy.wait()
    tokens, width = dr1.shape
    target = dx if relative else outs[0]
    for n in range(width // GROUP):
        cols = slice(n * GROUP, (n + 1) * GROUP)
        target[:, cols] = dr1[:, cols] + dot_nt(dqkv[...], weight[cols, :])
    for k in range(relative):
        part = tokens // relative
        first = pl.multiple_of((k ^ meta[0]) * part, part)
        outs[k][0] = dx[pl.ds(first, part), :].astype(bf16)


def prepare_kernel(ends, meta, inputs, attn, out, point, depth, gains, shifts, *refs):
    own, other, *x_parts, table = refs
    seq_count, blocks = inputs.shape[0], attn.shape[0]
    rows, half, cut = attn.shape[1], attn.shape[2] // 2, out.shape[2] // 2
    for k, part in enumerate(x_parts):
        part[...] = inputs[jnp.minimum(meta[0] ^ k, seq_count - 1)]
    table[...] = jnp.zeros_like(table)
    for b in range(blocks):
        start = b * SLOT
        for array in (depth, gains, shifts):
            table[start : start + array.shape[1], :rows] = array[b]
            start += array.shape[1]
    small = table[...].T[:rows]
    for to, core in ((own, meta[2]), (other, 1 - meta[2])):
        wide = pl.ds(pl.multiple_of(core * half, 128), half)
        narrow = pl.ds(pl.multiple_of(core * cut, 128), cut)
        to[:, half : half + LANES] = (small * (core == 0).astype(f32)).astype(bf16)
        for b in range(blocks):
            start = 0 if b == 0 else ends[2 * b - 1]
            to[:, start : start + half] = attn[b, :, wide].astype(bf16)
            start = ends[2 * b]
            to[:, start : start + cut] = out[b, :, narrow].astype(bf16)
            to[:, start + cut : start + 2 * cut] = point[b, :, narrow].astype(bf16)


def pair_kernel(meta, own, given, *refs):
    outs, (rows_ref,) = refs[:-1], refs[-1:]
    rows = own.shape[0]
    mine, theirs = own[...].astype(f32), given[...].astype(f32)
    rows_ref[0:rows, :] = jnp.where(meta[2] == 0, mine, theirs)
    rows_ref[rows : 2 * rows, :] = jnp.where(meta[2] == 0, theirs, mine)
    start = 0
    for out in outs:
        stop = start + out.shape[-1]
        out[0] = rows_ref[:, start:stop].astype(bf16)
        start = stop


def end_kernel(meta, kept, got, own, other, rows_ref):
    rows = own.shape[0]
    rows_ref[...] = kept[0].astype(f32) + got[0].astype(f32)
    first, second = rows_ref[0:rows, :], rows_ref[rows : 2 * rows, :]
    own[...] = jnp.where(meta[2] == 0, first, second)
    other[...] = jnp.where(meta[2] == 0, second, first).astype(bf16)


def settle_kernel(seqs, meta, *refs):
    parts, out, all_parts = refs[: len(refs) - 2], refs[-2], refs[-1]
    at = 0
    for part in parts:
        for n in range(part.shape[0]):
            all_parts[at] = part[n]
            at += 1
    for i in range(out.shape[0]):
        out[i] = all_parts[i ^ meta[0]].astype(out.dtype)


def adam_update(master, first, second, gradient, step_rate):
    first_new = beta_first * first + (1.0 - beta_first) * gradient
    second_new = beta_second * second + (1.0 - beta_second) * gradient * gradient
    first_hat = first_new / (1.0 - beta_first**STEP)
    second_hat = second_new / (1.0 - beta_second**STEP)
    updated = master - step_rate * (
        first_hat / (jnp.sqrt(second_hat) + adam_eps) + weight_decay * master
    )
    return (updated, first_new, second_new, updated.astype(jnp.bfloat16))


def adam_kernel(places, rates, smalls, meta, *refs):
    count = 2 * (1 + max(index for spots in places for index, _ in spots))
    grads, refs = refs[:count], refs[count:]
    arrays = len(places) + len(smalls)
    states = [refs[3 * n : 3 * n + 3] for n in range(arrays)]
    outs = [refs[3 * arrays + 4 * n : 3 * arrays + 4 * n + 4] for n in range(arrays)]

    def pick(index, half, lanes):
        own, given = grads[2 * index][:, lanes], grads[2 * index + 1][:, lanes].astype(f32)
        return jnp.where(meta[2] == half, own, given)

    for spots, state, out, rate in zip(places, states, outs, rates):
        width = state[0].shape[2] // 2
        for b, (index, start) in enumerate(spots):
            for half in range(2):
                cols = slice(half * width, (half + 1) * width)
                gradient = pick(index, half, slice(start, start + width))
                values = adam_update(*[ref[b, :, cols] for ref in state], gradient, rate)
                for ref, value in zip(out, values):
                    ref[b, :, cols] = value
    if smalls:
        table = refs[-1]
        index, start = places[0][0]
        start += states[0][0].shape[2] // 2
        rows = grads[2 * index].shape[0]
        table[...] = jnp.zeros_like(table)
        table[:rows, :] = pick(index, 0, slice(start, start + LANES))
        sums = table[...].T
        for n, (row, rate) in enumerate(smalls):
            state, out = states[len(places) + n], outs[len(places) + n]
            for b in range(state[0].shape[0]):
                first = b * SLOT + row
                gradient = sums[first : first + state[0].shape[1], :rows]
                values = adam_update(*[ref[b] for ref in state], gradient, rate)
                for ref, value in zip(out, values):
                    ref[b] = value


class Links:
    def __init__(self, seqs, copies):
        self.seqs, self.copies, self.ring = seqs, copies, copies // 2
        self.s = lax.axis_index("seq")
        position = lax.axis_index("dp")
        self.z, self.c = position // 2, position % 2

    def swap(self, array, seq=0, ring=0, core=0):
        pairs = [
            (s * self.copies + d, (s ^ seq) * self.copies + (d ^ (2 * ring + core)))
            for s in range(self.seqs)
            for d in range(self.copies)
        ]
        return lax.ppermute(array, AXES, pairs)

    def hop(self, array, axis, step):
        count = self.seqs if axis == "seq" else self.ring
        last = count.bit_length() - 2
        pairs = []
        for s in range(self.seqs):
            for d in range(self.copies):
                bit = 1 << (step if d % 2 == 0 else last - step)
                to_s, to_d = (s ^ bit, d) if axis == "seq" else (s, d ^ (2 * bit))
                pairs.append((s * self.copies + d, to_s * self.copies + to_d))
        return lax.ppermute(array, AXES, pairs)

    def steps(self, axis):
        return range((self.seqs if axis == "seq" else self.ring).bit_length() - 1)

    def place(self, m):
        return self.z ^ jnp.where(self.c == 0, m, flipped(m, self.ring))

    def around(self, block, axis, start=0, stop=None):
        for step in self.steps(axis)[start:stop]:
            block = join([block, self.hop(block, axis, step)])[0]
        return block

    def ring_block(self, block):
        _, rows, half = block.shape
        if rows % 16 == 0:
            return block
        placed = jnp.zeros_like(block)
        for m in range(self.ring):
            placed = lax.dynamic_update_slice(
                placed, block[m : m + 1], (self.place(m), jnp.int32(0), jnp.int32(0))
            )
        return placed.reshape(1, self.ring * rows, half)

    def both_cores(self, blocks):
        return blocks + [self.swap(one, core=1) for one in blocks]

    def finish(self, block, axis):
        return self.both_cores([block, self.hop(block, axis, self.steps(axis)[-1])])

    def ring_terms(self, terms):
        terms = [term[0] for term in terms]
        if terms[0].shape[0] > 1:
            return terms
        total = terms[0][0].astype(f32)
        for term in terms[1:]:
            total = total + term[0].astype(f32)
        total = total.reshape(self.ring, total.shape[0] // self.ring, total.shape[1])
        units = []
        for m in range(self.ring):
            at = self.z ^ jnp.where(self.c == 0, flipped(m, self.ring), m)
            units.append(lax.dynamic_index_in_dim(total, at, 0, keepdims=False))
        return [jnp.stack(units).astype(bf16)]


def shards(
    inputs,
    masked_positions,
    masked_grads,
    kernel_paths,
    attn_weight,
    out_weight,
    point_weight,
    depth_weight,
    gains,
    shifts,
    first_attn,
    first_out,
    first_point,
    first_depth,
    first_gains,
    first_shifts,
    second_attn,
    second_out,
    second_point,
    second_depth,
    second_gains,
    second_shifts,
):
    seq_count, part_tokens, width = inputs.shape
    seqs, copies = lax.axis_size("seq"), lax.axis_size("dp")
    devices = seqs * copies
    tokens = seqs * part_tokens
    blocks, rows, _ = attn_weight.shape
    taps = depth_weight.shape[1]
    scale = (width // HEADS) ** (-0.5)
    links = Links(seqs, copies)
    aligned = (2 * rows) % 16 == 0
    subs = links.ring if aligned else 1
    part_rows = width // (seqs * subs)
    half = 3 * width // 2
    place = links.s
    mine = jnp.minimum(place, seq_count - 1)
    live = (place < seq_count).astype(jnp.int32)
    own_paths = lax.dynamic_index_in_dim(kernel_paths, mine, 0, keepdims=False)
    meta = jnp.concatenate(
        [
            jnp.stack([place, links.z if subs > 1 else jnp.zeros_like(links.z), links.c]),
            own_paths,
            live[None],
        ]
    ).astype(jnp.int32)
    cut = width // 2
    ends = [half + LANES, half + LANES + width]
    ends += [ends[1] + half, ends[1] + half + width]

    def shape(*dims, dtype=f32):
        return jax.ShapeDtypeStruct(dims, dtype)

    dma = pltpu.SemaphoreType.DMA
    square = (width, width)
    wide = (width, 3 * width)

    def attend(b, parts, pieces, table, after=(), carry=()):
        outs = (
            Stored(wide, bf16),
            Stored((width, tokens), bf16),
            Stored((tokens, 3 * width), bf16),
            shape(tokens, width, dtype=bf16),
            Stored((width, tokens), bf16),
            Stored((LANES, tokens), f32),
        )
        scratch = [
            pltpu.VMEM(wide, bf16),
            pltpu.VMEM((width, tokens), bf16),
            pltpu.VMEM((tokens, 3 * width), bf16),
            pltpu.VMEM((width, tokens), bf16),
            pltpu.VMEM((LANES, tokens), f32),
            dma((7,)),
        ]
        if b == 0:
            outs = (shape(blocks * SLOT, width), Stored((tokens, width), bf16)) + outs
            scratch += [pltpu.VMEM((2, width, LANES), bf16), pltpu.VMEM((tokens, width), bf16)]
        return call(
            partial(attend_kernel, b, len(parts), scale),
            outs,
            [smem_spec()]
            + ([vmem_spec()] if b else [])
            + [vmem_spec()] * (len(parts) + len(pieces)),
            [meta] + ([table] if b else []) + list(parts) + list(pieces),
            scratch,
            11 * 10**9,
            f"attend_{b}",
            after,
            carry,
        )

    def mix(b, table, x, o, pieces, after=(), carry=()):
        final = b == blocks - 1
        return call(
            partial(mix_kernel, b, len(pieces), final and aligned, taps, seqs if final else 0),
            (
                (shape(1, part_tokens, width, dtype=bf16),) * seqs
                if final
                else (Stored((tokens, width), f32), shape(tokens, width, dtype=bf16))
            )
            + (
                Stored((tokens, width), f32),
                Stored((tokens, width), f32),
                Stored((width, tokens), bf16),
                Stored((tokens, LANES), f32),
                Stored(square, bf16),
                Stored(square, bf16),
            ),
            [smem_spec(), vmem_spec(), hbm_spec(), vmem_spec()] + [vmem_spec()] * len(pieces),
            [meta, table, x, o, *pieces],
            [
                pltpu.VMEM((tokens, width), x.dtype),
                pltpu.VMEM((tokens, width), f32),
                pltpu.VMEM((tokens, width), f32),
                pltpu.VMEM((width, tokens), bf16),
                pltpu.VMEM((tokens, LANES), f32),
                pltpu.VMEM(square, bf16),
                pltpu.VMEM(square, bf16),
                pltpu.VMEM((tokens, width), f32),
                pltpu.VMEM((tokens, width), f32),
                pltpu.VMEM((tokens + 2 * PAD, width), f32),
                pltpu.VMEM((tokens, width), bf16),
                dma((8,)),
            ],
            7 * 10**9,
            f"mix_{b}",
            after,
            carry,
        )

    def unmix(b, table, upstream, saved, ot, after=(), carry=()):
        last = b == blocks - 1
        parts = shape(seqs, subs, part_rows, width, dtype=bf16)
        return call(
            partial(unmix_kernel, b, taps, last),
            (
                shape(tokens, width),
                shape(tokens, width, dtype=bf16),
                shape(SLOT, width),
                parts,
                parts,
            ),
            [smem_spec()] + [vmem_spec()] * (len(upstream) + 1) + [hbm_spec()] * 7,
            [meta, table, *upstream, *saved, ot],
            [
                pltpu.VMEM((tokens, width), f32),
                pltpu.VMEM((tokens, width), f32),
                pltpu.VMEM((width, tokens), bf16),
                pltpu.VMEM((width, tokens), bf16),
                pltpu.VMEM((tokens, LANES), f32),
                pltpu.VMEM(square, bf16),
                pltpu.VMEM(square, bf16),
                pltpu.VMEM((tokens, width), f32),
                pltpu.VMEM((tokens, width), bf16),
                pltpu.VMEM((tokens + 2 * PAD, width), f32),
                pltpu.VMEM((tokens + 2 * PAD, width), f32),
                dma((7,)),
            ],
            10 * 10**9,
            f"unmix_{b}",
            after,
            carry,
        )

    def unattend(b, qkv, do, lse, after=(), carry=()):
        return call(
            partial(unattend_kernel, scale),
            (shape(tokens, 3 * width, dtype=bf16), shape(1, width)),
            [smem_spec(), hbm_spec(), vmem_spec(), hbm_spec()],
            [meta, qkv, do, lse],
            [
                pltpu.VMEM((tokens, 3 * width), bf16),
                pltpu.VMEM((LANES, tokens), f32),
                dma((width // GROUP + 1,)),
            ],
            13 * 10**9,
            f"unattend_{b}",
            after,
            carry,
        )

    def attn_grad(b, dqkv, xt, tables, after=(), carry=()):
        span = half + (0 if b else LANES)
        parts = shape(seqs, subs, part_rows, span, dtype=bf16)
        return call(
            partial(attn_grad_kernel, len(tables) // 2),
            (parts, parts),
            [smem_spec(), vmem_spec(), hbm_spec()] + [vmem_spec()] * len(tables),
            [meta, dqkv, xt, *tables],
            [pltpu.VMEM((width, tokens), bf16), dma]
            + ([pltpu.VMEM((LANES, width), f32)] if tables else []),
            3 * 10**9,
            f"attn_grad_{b}",
            after,
            carry,
        )

    def unproject(b, dqkv, dr1, weight, after=(), carry=()):
        return call(
            partial(unproject_kernel, 0 if b else seqs),
            (shape(tokens, width),) if b else (shape(1, part_tokens, width, dtype=bf16),) * seqs,
            [smem_spec()] + [vmem_spec()] * 2 + [hbm_spec()],
            [meta, dqkv, dr1, weight],
            [pltpu.VMEM(wide, bf16), pltpu.VMEM((tokens, width), f32), dma],
            4 * 10**9,
            f"unproject_{b}",
            after,
            carry,
        )

    def settle(parts, dtype, after=()):
        return call(
            partial(settle_kernel, seqs),
            (shape(seq_count, part_tokens, width, dtype=dtype),),
            [smem_spec()] + [vmem_spec()] * len(parts),
            [meta, *parts],
            [pltpu.VMEM((seqs, part_tokens, width), bf16)],
            10**8,
            "settle",
            after,
        )[0]

    def end(kept, got):
        span = kept.shape[-1]
        own, other = call(
            end_kernel,
            (shape(rows, span), shape(rows, span, dtype=bf16)),
            [smem_spec(), vmem_spec(), vmem_spec()],
            [meta, kept, got],
            [pltpu.VMEM((2 * rows, span), f32)],
            10**8,
            "end",
        )
        return own, links.swap(other, core=1)

    def adam(places, rates, smalls, grads, states):
        outs = []
        for state in states:
            outs += [shape(*state[0].shape)] * 3 + [shape(*state[0].shape, dtype=bf16)]
        flat = [array for state in states for array in state]
        results = call(
            partial(adam_kernel, places, rates, smalls),
            tuple(outs),
            [smem_spec()] + [vmem_spec()] * (len(grads) + len(flat)),
            [meta, *grads, *flat],
            [pltpu.VMEM((LANES, LANES), f32)],
            10**8,
            "adam",
        )
        return [results[4 * n : 4 * n + 4] for n in range(len(states))]

    own, other, *x_parts = call(
        partial(prepare_kernel, ends),
        (shape(rows, ends[3], dtype=bf16),) * 2
        + (shape(part_tokens, width, dtype=bf16),) * seqs,
        [smem_spec()] + [vmem_spec()] * 7,
        [meta, inputs, attn_weight, out_weight, point_weight, depth_weight, gains, shifts],
        [pltpu.VMEM((LANES, LANES), f32)],
        10**8,
        "prepare",
    )
    given = links.swap(other, core=1)
    widths = (ends[0], ends[2] - ends[0], width)
    unit_a0, unit_mid, unit_m1 = call(
        pair_kernel,
        tuple(shape(1, 2 * rows, span, dtype=bf16) for span in widths),
        [smem_spec(), vmem_spec(), vmem_spec()],
        [meta, own, given],
        [pltpu.VMEM((2 * rows, ends[3]), f32)],
        10**8,
        "pair",
    )
    x_parts = [x_parts[0]] + [links.swap(x_parts[k], seq=k) for k in range(1, seqs)]
    last_seq, last_ring = links.steps("seq")[-1], links.steps("ring")[-1]
    block_a0 = links.around(unit_a0, "ring", stop=-1)
    got_a0 = links.hop(block_a0, "ring", last_ring)
    plane_m1 = links.around(unit_m1, "seq") if aligned else unit_m1
    ring_a0, done = join([block_a0, got_a0], after=(*x_parts[1:], plane_m1))
    ring_a0 = links.ring_block(ring_a0)
    got_a0 = links.hop(ring_a0[None], "seq", 0)
    unit_mid, _ = join([unit_mid], after=(done,))
    got_mid = links.hop(unit_mid, "ring", 0)
    part_mid, done = join([unit_mid, got_mid])
    plane_a0, _ = join([ring_a0[None], got_a0], after=(done,))
    pieces_a0 = links.finish(plane_a0, "seq")
    ring_mid = links.ring_block(links.around(part_mid, "ring", 1))
    ring_m0, ring_a1 = ring_mid[..., :width], ring_mid[..., width:]
    got_m0 = [links.swap(ring_m0[None], seq=k) for k in range(1, seqs)]
    got_a1 = links.hop(ring_a1[None], "seq", 0)
    got_m1 = links.hop(plane_m1[None], "ring", 0) if aligned else None
    table, x16, w_0, xt_0, qkv_0, o_0, ot_0, lse_0 = attend(
        0, x_parts, pieces_a0, None, after=(ring_m0, ring_a1)
    )
    got_m0, _ = join(got_m0, after=(table,))
    pieces_m0 = links.both_cores([ring_m0[None], got_m0])
    plane_a1, done_a1 = join([ring_a1[None], got_a1], after=(table,))
    marks = [done_a1]
    if aligned:
        plane_m1, done_m1 = join([plane_m1[None], got_m1], after=(table,))
        marks.append(done_m1)
    got_a1 = links.hop(plane_a1, "seq", last_seq)
    y_0, x_1, *saved_0 = mix(0, table, x16, o_0, pieces_m0, after=marks)
    pieces_a1 = links.both_cores([plane_a1, got_a1])
    if aligned:
        got_m1, _ = join([links.hop(plane_m1, "ring", last_ring)], after=(x_1,))
        pieces_m1 = links.both_cores([plane_m1, got_m1])
    else:
        ring_m1 = links.ring_block(links.around(unit_m1, "ring"))
        pieces_m1 = links.finish(links.around(ring_m1[None], "seq", stop=-1), "seq")
    w_1, xt_1, qkv_1, o_1, ot_1, lse_1 = attend(1, [x_1], pieces_a1, table)
    *y_1, xh1, xh2, hct, stats, w_out, w_point = mix(1, table, y_0, o_1, pieces_m1)
    saved_1 = (xh1, xh2, hct, stats, w_out, w_point)

    y_back = [links.swap(y_1[k], seq=k) for k in range(1, seqs)]
    places = masked_positions[:, None, :]
    dr1, do, sums_1, keep, send = unmix(1, table, (places, masked_grads), saved_1, ot_1)
    y_back, done = join(y_back, after=(sums_1,))
    given_m1 = links.swap(send, core=1)
    terms_m1 = [keep, given_m1]
    dqkv, bias_1 = unattend(1, qkv_1, do, lse_1, after=(done,))
    keep, send = attn_grad(1, dqkv, xt_1, ())
    terms_a1 = [keep, links.swap(send, core=1)]
    late, sent, done = fold([terms_m1, terms_a1])
    got = links.hop(sent, "seq", 0)
    (dy,) = unproject(1, dqkv, dr1, w_1, after=(done,))
    dr1, do, sums_0, keep, send = unmix(0, table, (dy,), saved_0, ot_0)
    late, sent, done = fold([[late, got]], after=(sums_0,))
    got = links.hop(sent, "seq", 1)
    mixed, sent, done_mixed = fold([[keep, links.swap(send, core=1)]])
    got_mixed = links.hop(sent, "seq", 0)
    dqkv, bias_0 = unattend(0, qkv_0, do, lse_0, after=(done, done_mixed))
    mixed, sent, done_mixed = fold([[mixed, got_mixed]], after=(bias_0,))
    got_mixed = links.hop(sent, "seq", 1)
    keep, send = attn_grad(
        0, dqkv, xt_0, (sums_0, bias_0, sums_1, bias_1), after=(done_mixed, touch(got))
    )
    final, sent, done = fold([[keep, links.swap(send, core=1)]])
    got_final = links.hop(sent, "seq", 0)
    dx = unproject(0, dqkv, dr1, w_0, after=(done,))
    final, sent, done = fold([[final, got_final]], after=(dx[0],))
    got_final = links.hop(sent, "seq", 1)
    late, sent, _ = fold(
        [links.ring_terms([late, got]), links.ring_terms([mixed, got_mixed])], after=(done,)
    )
    got = links.hop(sent, "ring", 0)
    final, sent, done_final = fold([links.ring_terms([final, got_final])], after=(touch(got),))
    got_final = links.hop(sent, "ring", 0)
    dx_sent, _ = join(dx[1:], after=(done_final,))
    x_back = [links.swap(dx_sent[k - 1], seq=k) for k in range(1, seqs)]
    for step in links.steps("ring")[1:]:
        late, sent, _ = fold([[late, got]])
        got = links.hop(sent, "ring", step)
    x_back, done = join([one[None] for one in x_back])
    for step in links.steps("ring")[1:]:
        final, sent, _ = fold([[final, got_final]], after=(done,))
        got_final = links.hop(sent, "ring", step)
    result = settle([y_1[0], y_back], bf16)
    input_grad = settle([dx[0], x_back], f32)
    grads = end(late, got)
    last = width + half
    new_out, new_point = adam(
        (((0, last), (0, 0)), ((0, last + cut), (0, cut))),
        (rate_out, rate_point),
        (),
        grads,
        (
            (out_weight, first_out, second_out),
            (point_weight, first_point, second_point),
        ),
    )
    new_attn, new_depth, new_gains, new_shifts = adam(
        (((0, 0), (1, width)),),
        (rate_attn,),
        ((0, rate_depth), (GAIN, rate_gain), (SHIFT, rate_vector)),
        end(final, got_final) + grads,
        (
            (attn_weight, first_attn, second_attn),
            (depth_weight, first_depth, second_depth),
            (gains, first_gains, second_gains),
            (shifts, first_shifts, second_shifts),
        ),
    )
    updates = (new_attn, new_out, new_point, new_depth, new_gains, new_shifts)
    return (
        (result, input_grad)
        + tuple((entry[0] for entry in updates))
        + tuple((entry[1] for entry in updates))
        + tuple((entry[2] for entry in updates))
        + tuple((entry[3] for entry in updates))
    )


def solution(mesh):
    sequence = P("dp", "seq", None)
    matrix = P(None, AXES, None)
    vector = P(None, None, AXES)
    weights = (matrix,) * 3 + (vector,) * 3
    return jax.shard_map(
        shards,
        mesh=mesh,
        in_specs=(sequence, P("dp", None), P("dp", None, None), P("dp", None)) + weights * 3,
        out_specs=(sequence, sequence) + weights * 4,
        check_vma=False,
    )
```

```python
from functools import partial

import jax
import jax.numpy as jnp
from jax import lax
from jax.experimental import pallas as pl
from jax.experimental.pallas import tpu as pltpu
from jax.sharding import PartitionSpec as P

HEADS = 12
STEP = 10

norm_eps = 1e-05
beta_first = 0.5
beta_second = 0.5
adam_eps = 1e-08
weight_decay = 0.01
rate_attn = 0.03
rate_out = 0.25
rate_point = 0.03
rate_depth = 0.3
rate_gain = 0.45
rate_vector = 0.2

f32 = jnp.float32
bf16 = jnp.bfloat16
AXES = ("seq", "dp")
VMEM_BYTES = 24 * 2**20
GROUP = 256
ROWS = 64
PAD = 8

GAIN = 7
SHIFT = 9
SMALL = 14
SLOT = 16
LANES = 128


def dot_nn(a, b):
    return lax.dot_general(a, b, (((1,), (0,)), ((), ())), preferred_element_type=f32)


def dot_nt(a, b):
    return lax.dot_general(a, b, (((1,), (1,)), ((), ())), preferred_element_type=f32)


def dot_tn(a, b):
    return lax.dot_general(a, b, (((0,), (0,)), ((), ())), preferred_element_type=f32)


def vmem_spec():
    return pl.BlockSpec(memory_space=pltpu.VMEM)


def smem_spec():
    return pl.BlockSpec(memory_space=pltpu.SMEM)


def any_spec():
    return pl.BlockSpec(memory_space=pl.ANY)


def hbm_spec():
    return pl.BlockSpec(memory_space=pltpu.HBM)


class Stored(jax.ShapeDtypeStruct):
    pass


def call(body, outs, in_specs, args, scratch, cost, name, after=(), fetch=()):
    n_in, n_after, n_out, n_fetch = len(in_specs), len(after), len(outs), len(fetch)

    def kernel(*refs):
        first = n_in + n_after
        far, refs = refs[first : first + n_fetch], refs[:n_in] + refs[first + n_fetch :]
        near = refs[n_in + n_out : n_in + n_out + n_fetch]
        refs = refs[: n_in + n_out] + refs[n_in + n_out + n_fetch :]
        copies = []
        if n_fetch:
            for n in range(n_fetch):
                count = 4 if far[n].shape[0] % 64 == 0 else 1
                copies += chunk_copies(far[n], near[n], refs[-1].at[n], count)
            refs = refs[:-1]
        for copy in copies:
            copy.start()
        body(*refs)
        for copy in copies:
            copy.wait()

    args = [
        pltpu.with_memory_space_constraint(arg, pltpu.HBM)
        if spec.memory_space == pltpu.HBM
        else arg
        for arg, spec in zip(args, in_specs, strict=True)
    ]
    fetch = [pltpu.with_memory_space_constraint(arg, pltpu.HBM) for arg in fetch]
    results = pl.pallas_call(
        kernel,
        out_shape=tuple(
            pltpu.HBM(out.shape, out.dtype) if isinstance(out, Stored) else out for out in outs
        )
        + tuple(jax.ShapeDtypeStruct(a.shape, a.dtype) for a in fetch),
        in_specs=list(in_specs) + [vmem_spec()] * n_after + [hbm_spec()] * n_fetch,
        out_specs=tuple(hbm_spec() if isinstance(out, Stored) else vmem_spec() for out in outs)
        + (vmem_spec(),) * n_fetch,
        scratch_shapes=list(scratch) + ([pltpu.SemaphoreType.DMA((n_fetch,))] if fetch else []),
        compiler_params=pltpu.CompilerParams(vmem_limit_bytes=VMEM_BYTES),
        cost_estimate=pl.CostEstimate(flops=cost, bytes_accessed=2**18, transcendentals=0),
        name=name,
    )(*args, *after, *fetch)
    return (results[:n_out], results[n_out:]) if n_fetch else results


TOKEN = jax.ShapeDtypeStruct((8, 128), f32)


def small_call(body, outs, args, name, after=(), scratch=()):
    specs = [vmem_spec()] * len(args)
    return call(body, outs, specs, args, list(scratch), 10**8, name, after)


def joins(groups, after=()):
    def kernel(*refs):
        used = 0
        for group, out in zip(groups, refs[sum(map(len, groups)) :]):
            start = 0
            for part in refs[used : used + len(group)]:
                count = part.shape[0]
                out[start : start + count] = part[...]
                start += count
            used += len(group)
        refs[-1][...] = jnp.zeros_like(refs[-1])

    outs = [
        jax.ShapeDtypeStruct((sum(p.shape[0] for p in group),) + group[0].shape[1:], group[0].dtype)
        for group in groups
    ]
    parts = [part for group in groups for part in group]
    return small_call(kernel, (*outs, TOKEN), parts, "join", after)


def join(parts, after=()):
    return joins([parts], after)


def fold(groups, after=()):
    terms = [term for group in groups for term in group]
    widths = [group[0].shape[-1] for group in groups]
    lead = terms[0].shape[:-2]
    rows, half = terms[0].shape[-2], lead[0] // 2

    def kernel(*refs):
        ins, (kept, sent, mark) = refs[: len(terms)], refs[len(terms) :]

        def block(out, to, at):
            start, used = 0, 0
            for group, width in zip(groups, widths, strict=True):
                total = ins[used][at].astype(f32)
                for term in ins[used + 1 : used + len(group)]:
                    total = total + term[at].astype(f32)
                out[(*to, slice(None), slice(start, start + width))] = total.astype(bf16)
                start, used = start + width, used + len(group)

        for n in range(half):
            if len(lead) == 1:
                block(kept, (n,), (n,))
                block(sent, (n,), (half + n,))
            else:

                def step(m, carry, n=n):
                    block(kept, (n, m), (n, m))
                    block(sent, (n, m), (half + n, m))
                    return carry

                lax.fori_loop(0, lead[1], step, 0)
        mark[...] = jnp.zeros_like(mark)

    out = jax.ShapeDtypeStruct((half,) + lead[1:] + (rows, sum(widths)), bf16)
    return small_call(kernel, (out, out, TOKEN), terms, "fold", after)


def touch(*arrays):
    def kernel(*refs):
        refs[-1][...] = jnp.zeros_like(refs[-1])

    return small_call(kernel, (TOKEN,), arrays, "touch")[0]


def chunk_copies(source, dest, sem, count=4):
    rows = source.shape[0] // count
    return [
        pltpu.make_async_copy(
            source.at[pl.ds(n * rows, rows)], dest.at[pl.ds(n * rows, rows)], sem
        )
        for n in range(count)
    ]


def group_loop(width, body):
    def step(g, carry):
        first = pl.multiple_of(g * GROUP, GROUP)
        return body(g, [pl.ds(part * width + first, GROUP) for part in range(3)], carry)

    return partial(lax.fori_loop, 0, width // GROUP, step)


def row_loop(total, body, rows=ROWS):
    def step(i, carry):
        body(pl.multiple_of(i * rows, rows))
        return carry

    lax.fori_loop(0, total // rows, step, 0, unroll=True)


def flipped(index, count):
    bits, out = count.bit_length() - 1, 0
    for bit in range(bits):
        out = out | (((index >> bit) & 1) << (bits - 1 - bit))
    return out


def weight_copies(meta, pieces, dest, sem, first, half, ring_last=False, whole=False):
    s, z, c = meta[0], meta[1], meta[2]
    copies, first_late = [], pieces[0].shape[0]
    late_count = first_late + pieces[1].shape[0]
    for n, piece in enumerate(pieces):
        late, early, rows, width = piece.shape
        core = (n // 2) ^ c
        for a in range(late):
            for b in range(early):
                outer, inner = (n % 2) * first_late + a, b
                if 2 * first_late == late_count:
                    outer = jnp.where(core == 0, outer, flipped(outer, late_count))
                inner = jnp.where(core == 0, inner, flipped(inner, early))
                if ring_last:
                    row = ((inner ^ s) * late_count + (outer ^ z)) * rows
                else:
                    row = ((outer ^ s) * early + (inner ^ z)) * rows
                row = pl.multiple_of(row, rows)
                source = piece.at[a, b]
                if (first, half) != (0, width):
                    source = piece.at[a, b, :, pl.ds(first, half)]
                if whole:
                    target = dest.at[core, pl.ds(row, rows)]
                else:
                    col = pl.multiple_of(core * half, 128)
                    target = dest.at[pl.ds(row, rows), pl.ds(col, half)]
                copies.append(pltpu.make_async_copy(source, target, sem))
    return copies


def head_masks(scale):
    lane = lax.broadcasted_iota(jnp.int32, (1, GROUP), 1) // (GROUP // 4)
    return [jnp.where(lane == h, f32(scale), f32(0)).astype(bf16) for h in range(4)]


def attend_kernel(block, near, x_parts, scale, meta, *refs):
    if block:
        table, refs = refs[0], refs[1:]
    x_refs, pieces = refs[:x_parts], refs[x_parts : x_parts + 4]
    refs = refs[x_parts + 4 :]
    if block == 0:
        table, x, refs = refs[0], refs[1], refs[2:]
    w_far, xt_far, qkv_far, o_out, ot_far, lse_far, *refs = refs
    if near:
        ot = ot_far
    else:
        ot, refs = refs[0], refs[1:]
    weight, xt, qkv, lse, sems = refs[:5]
    half = weight.shape[1] // 2
    if block == 0:
        (extra,) = refs[5:]
        smalls = weight_copies(meta, pieces, extra, sems.at[0], half, LANES, whole=True)
        for copy in smalls:
            copy.start()
        part_rows = x_refs[0].shape[0]
        x_copies = [
            pltpu.make_async_copy(
                x_refs[k],
                x.at[pl.ds(pl.multiple_of((k ^ meta[0]) * part_rows, part_rows), part_rows)],
                sems.at[1],
            )
            for k in range(x_parts)
        ]
        for copy in x_copies:
            copy.start()
    else:
        x = x_refs[0]
    copies = weight_copies(meta, pieces, weight, sems.at[2], 0, half)
    for copy in copies:
        copy.start()
    if block == 0:
        for copy in x_copies:
            copy.wait()
        for copy in smalls:
            copy.wait()
        table[...] = extra[0].astype(f32).T[: table.shape[0]]
    small = table.at[pl.ds(SLOT * block, SLOT)]
    xt[...] = x[...].T
    xt_store = pltpu.make_async_copy(xt, xt_far, sems.at[3])
    xt_store.start()
    for copy in copies:
        copy.wait()
    w_stores = chunk_copies(weight, w_far, sems.at[2])
    for copy in w_stores:
        copy.start()
    tokens, width = x.shape
    scaled, plain = head_masks(scale), head_masks(1.0)
    lane = lax.broadcasted_iota(jnp.int32, (tokens, 128), 1)
    sums = jnp.zeros((tokens, 128), f32)
    for g in range(width // GROUP):
        cols = slice(g * GROUP, (g + 1) * GROUP)
        cols_k = slice(width + g * GROUP, width + (g + 1) * GROUP)
        cols_v = slice(2 * width + g * GROUP, 2 * width + (g + 1) * GROUP)
        bias = small[SHIFT + 2 : SHIFT + 3, cols]
        qkv[:, cols] = (dot_nn(x[...], weight[:, cols]) + bias).astype(bf16)
        qkv[:, cols_k] = dot_nn(x[...], weight[:, cols_k]).astype(bf16)
        qkv[:, cols_v] = dot_nn(x[...], weight[:, cols_v]).astype(bf16)
        for part in (cols, cols_k, cols_v):
            pltpu.make_async_copy(qkv.at[:, part], qkv_far.at[:, part], sems.at[4]).start()
        mixed = jnp.zeros((tokens, GROUP), f32)
        for h in range(4):
            scores = dot_nt(qkv[:, cols] * scaled[h], qkv[:, cols_k])
            top = jnp.max(scores, axis=-1, keepdims=True)
            weights = jnp.exp(scores - top)
            total = jnp.sum(weights, axis=-1, keepdims=True)
            part = dot_nn(weights.astype(bf16), qkv[:, cols_v] * plain[h])
            mixed = mixed + part * (1.0 / total)
            sums = jnp.where(lane == g * 4 + h, top + jnp.log(total), sums)
        o_out[:, cols] = mixed.astype(bf16)
        ot[cols, :] = o_out[:, cols].T
        if not near:
            pltpu.make_async_copy(ot.at[cols], ot_far.at[cols], sems.at[5]).start()
    lse[...] = sums.T
    lse_store = pltpu.make_async_copy(lse, lse_far, sems.at[6])
    lse_store.start()
    for copy in w_stores + [lse_store]:
        copy.wait()
    xt_store.wait()
    pltpu.make_async_copy(qkv, qkv_far, sems.at[4]).wait()
    if not near:
        pltpu.make_async_copy(ot, ot_far, sems.at[5]).wait()


def tap_rows(meta, small, block, taps):
    path = meta[3 + block]
    half = taps // 2
    return [
        small[j : j + 1, :] * jnp.where(path + 1 >= abs(j - half), f32(1), f32(0))
        for j in range(taps)
    ]


def norm_rows(r, gain, shift):
    center = r - jnp.mean(r, axis=-1, keepdims=True)
    inverse = lax.rsqrt(jnp.mean(center * center, axis=-1, keepdims=True) + norm_eps)
    normed = center * inverse
    return normed * gain + shift, normed, inverse


def mix_kernel(block, count, ring_last, taps, near, relative, meta, table, x, o_ref, *refs):
    pieces = refs[:count]
    refs = refs[count:]
    y_out, refs = (None, refs) if relative else (refs[0], refs[1:])
    *refs, acc, y1, zpad, hc, sems = refs
    if near:
        outs, kept = refs[:-6], refs[-6:]
    else:
        outs, far, kept = refs[:-12], refs[-12:-6], refs[-6:]
    xh1, xh2, hct, stats, w_out, w_point = kept
    y_low = outs[0]
    stores = []

    def store(n, rows=None):
        if not near:
            source, target = kept[n], far[n]
            if rows is not None:
                source, target = source.at[rows], target.at[rows]
            copy = pltpu.make_async_copy(source, target, sems.at[4 + n])
            copy.start()
            if rows is None:
                stores.append(copy)

    small = table.at[pl.ds(SLOT * block, SLOT)]
    tokens, width = o_ref.shape
    half = width // 2
    copies = weight_copies(meta, pieces, w_out, sems.at[0], 0, half, ring_last)
    late_copies = weight_copies(meta, pieces, w_point, sems.at[1], half, half, ring_last)
    for copy in copies + late_copies:
        copy.start()
    zpad[0:PAD, :] = jnp.zeros((PAD, width), f32)
    zpad[tokens + PAD :, :] = jnp.zeros((PAD, width), f32)
    for copy in copies:
        copy.wait()
    store(4)
    for n in range(width // GROUP):
        cols = slice(n * GROUP, (n + 1) * GROUP)
        acc[:, cols] = dot_nn(o_ref[...], w_out[:, cols])

    def first_norm(row):
        rows = pl.ds(row, ROWS)
        stream = x[rows, :].astype(f32) + (acc[rows, :] + small[SHIFT + 3 : SHIFT + 4, :])
        out, normed, inverse = norm_rows(
            stream, small[GAIN : GAIN + 1, :], small[SHIFT : SHIFT + 1, :]
        )
        y1[rows, :] = out
        xh1[rows, :] = normed
        stats[rows, 0:1] = inverse
        zpad[pl.ds(row + PAD, ROWS), :] = out.astype(bf16).astype(f32)

    row_loop(tokens, first_norm)
    store(0)
    weights = tap_rows(meta, small, block, taps)
    reach = taps // 2

    def convolve(row):
        window = zpad[pl.ds(row, ROWS + 2 * PAD), :]
        total = jnp.zeros((ROWS, width), f32)
        for j in range(taps):
            start = PAD - reach + j
            total = total + weights[j] * window[start : start + ROWS]
        hc[pl.ds(row, ROWS), :] = total.astype(bf16)

    row_loop(tokens, convolve)
    hct[...] = hc[...].T
    store(2)
    for copy in late_copies:
        copy.wait()
    store(5)
    for n in range(width // GROUP):
        cols = slice(n * GROUP, (n + 1) * GROUP)
        acc[:, cols] = dot_nn(hc[...], w_point[:, cols])

    def second_norm(row):
        rows = pl.ds(row, ROWS)
        stream = y1[rows, :] + (acc[rows, :] + small[SHIFT + 4 : SHIFT + 5, :])
        out, normed, inverse = norm_rows(
            stream, small[GAIN + 1 : GAIN + 2, :], small[SHIFT + 1 : SHIFT + 2, :]
        )
        xh2[rows, :] = normed
        stats[rows, 1:2] = inverse
        store(1, rows)
        if not relative:
            y_out[rows, :] = out
            y_low[rows, :] = out.astype(bf16)
        else:
            y1[rows, :] = out

    row_loop(tokens, second_norm)
    store(3)
    for k in range(relative):
        part = tokens // relative
        first = pl.multiple_of((k ^ meta[0]) * part, part)
        outs[k][0] = y1[pl.ds(first, part), :].astype(bf16)
    for copy in stores:
        copy.wait()
    if not near:
        pltpu.make_async_copy(xh2, far[1], sems.at[5]).wait()


def norm_rows_back(upstream, normed, inverse, gain):
    scaled = upstream * gain
    inner = (
        scaled
        - jnp.mean(scaled, axis=-1, keepdims=True)
        - normed * jnp.mean(scaled * normed, axis=-1, keepdims=True)
    )
    return inverse * inner


def column_sum(a):
    return jnp.sum(a, axis=0, keepdims=True)


def store_parts(out, columns, value, meta, core):
    seqs, subs, rows, _ = out.shape
    for k in range(seqs):
        for m in range(subs):
            start = (k * subs + m) * rows
            seq, ring = k ^ meta[0], m ^ meta[1]
            seq = jnp.where(core == 0, flipped(seq, seqs), seq)
            ring = jnp.where(core == 0, flipped(ring, subs), ring)
            out[seq, ring, :, columns] = value[start : start + rows].astype(bf16)


def unmix_kernel(block, taps, last, meta, table, *refs):
    small = table.at[pl.ds(SLOT * block, SLOT)]
    if last:
        places, grads = refs[:2]
        refs = refs[2:]
    else:
        dy_ref = refs[0]
        refs = refs[1:]
    xh1, xh2, hct, stats, w_out, w_point, ot, *refs = refs
    dr1, do_out, sums, inner, keep, send, dr2, du, dpad, zpad = refs
    tokens, width = dr1.shape
    half = width // 2
    sums[...] = jnp.zeros_like(sums)
    if last:
        mine = jnp.minimum(meta[0], places.shape[0] - 1)
        picked = places.shape[2]
        token = lax.broadcasted_iota(jnp.int32, (tokens, picked), 0)
        live = jnp.where(meta[5] > 0, f32(1), f32(0))
        picks = jnp.where(token == places[mine], live, f32(0)).astype(bf16)
        dr2[...] = dot_nn(picks, grads[mine])
    for pad in (dpad, zpad):
        pad[0:PAD, :] = jnp.zeros((PAD, width), f32)
        pad[tokens + PAD :, :] = jnp.zeros((PAD, width), f32)

    def second_norm(row):
        rows = pl.ds(row, ROWS)
        dy = dr2[rows, :] if last else dy_ref[rows, :]
        normed = xh2[rows, :]
        back = norm_rows_back(dy, normed, stats[rows, 1:2], small[GAIN + 1 : GAIN + 2, :])
        low = back.astype(bf16)
        dr2[rows, :] = back
        du[rows, :] = low
        sums[GAIN + 1 : GAIN + 2, :] += column_sum(dy * normed)
        sums[SHIFT + 1 : SHIFT + 2, :] += column_sum(dy)
        sums[SHIFT + 4 : SHIFT + 5, :] += column_sum(low.astype(f32))
        z = xh1[rows, :] * small[GAIN : GAIN + 1, :] + small[SHIFT : SHIFT + 1, :]
        zpad[pl.ds(row + PAD, ROWS), :] = z.astype(bf16).astype(f32)

    row_loop(tokens, second_norm)
    c = meta[2]
    mine = pl.ds(pl.multiple_of(c * half, 128), half)
    other = pl.ds(pl.multiple_of((1 - c) * half, 128), half)
    point_cols, out_cols = slice(half, width), slice(0, half)
    for n in range(width // GROUP):
        cols = slice(n * GROUP, (n + 1) * GROUP)
        back = dot_nt(du[...], w_point[cols, :])
        dpad[PAD : PAD + tokens, cols] = back.astype(bf16).astype(f32)
    store_parts(send, point_cols, dot_nn(hct[...], du[:, other]), meta, 1 - c)
    store_parts(keep, point_cols, dot_nn(hct[...], du[:, mine]), meta, c)
    weights = tap_rows(meta, small, block, taps)
    path = meta[3 + block]
    reach = taps // 2

    def unconvolve(row):
        rows = pl.ds(row, ROWS)
        window = dpad[pl.ds(row, ROWS + 2 * PAD), :]
        z_window = zpad[pl.ds(row, ROWS + 2 * PAD), :]
        here = window[PAD : PAD + ROWS]
        total = dr2[rows, :]
        for j in range(taps):
            start = PAD + reach - j
            total = total + weights[j] * window[start : start + ROWS]
            z_start = PAD - reach + j
            sums[j : j + 1, :] += column_sum(here * z_window[z_start : z_start + ROWS])
        normed = xh1[rows, :]
        back = norm_rows_back(total, normed, stats[rows, 0:1], small[GAIN : GAIN + 1, :])
        low = back.astype(bf16)
        dr1[rows, :] = back
        du[rows, :] = low
        sums[GAIN : GAIN + 1, :] += column_sum(total * normed)
        sums[SHIFT : SHIFT + 1, :] += column_sum(total)
        sums[SHIFT + 3 : SHIFT + 4, :] += column_sum(low.astype(f32))

    row_loop(tokens, unconvolve)
    for j in range(taps):
        used = jnp.where(path + 1 >= abs(j - reach), f32(1), f32(0))
        sums[j : j + 1, :] = sums[j : j + 1, :] * used
    for n in range(width // GROUP):
        cols = slice(n * GROUP, (n + 1) * GROUP)
        do_out[:, cols] = dot_nt(du[...], w_out[cols, :]).astype(bf16)
        both = do_out[:, cols].T.astype(f32) * ot[cols, :].astype(f32)
        for h in range(4):
            size = GROUP // 4
            inner[n * 4 + h : n * 4 + h + 1, :] = column_sum(both[h * size : (h + 1) * size])
    store_parts(send, out_cols, dot_nn(ot[...], du[:, other]), meta, 1 - c)
    store_parts(keep, out_cols, dot_nn(ot[...], du[:, mine]), meta, c)


def unattend_kernel(scale, meta, qkv, do_ref, lse, inner, dqkv, bias):
    tokens, width = do_ref.shape
    scaled, plain = head_masks(scale), head_masks(1.0)

    def unattend_group(g, columns, carry):
        cols, cols_k, cols_v = columns
        dq = jnp.zeros((tokens, GROUP), f32)
        dk = jnp.zeros((tokens, GROUP), f32)
        dv = jnp.zeros((tokens, GROUP), f32)
        for h in range(4):
            row = pl.ds(g * 4 + h, 1)
            q = qkv[:, cols] * scaled[h]
            do = do_ref[:, cols] * plain[h]
            scores = dot_nt(qkv[:, cols_k], q)
            probs = jnp.exp(scores - lse[row, :])
            dp = dot_nt(qkv[:, cols_v], do)
            ds = (probs * (dp - inner[row, :])).astype(bf16)
            dv = dv + dot_nn(probs.astype(bf16), do)
            dk = dk + dot_nn(ds, q)
            dq = dq + dot_tn(ds, qkv[:, cols_k] * scaled[h])
        low = dq.astype(bf16)
        dqkv[:, cols] = low
        bias[:, cols] = column_sum(low.astype(f32))
        dqkv[:, cols_k] = dk.astype(bf16)
        dqkv[:, cols_v] = dv.astype(bf16)
        return carry

    group_loop(width, unattend_group)(0)


def attn_grad_kernel(blocks, keep, meta, dqkv, xt, *refs):
    tables, (out, mark, *refs) = refs[: 2 * blocks], refs[2 * blocks :]
    mark[...] = jnp.zeros_like(mark)
    width = xt.shape[0]
    half = 3 * width // 2
    part = half // 3
    core = meta[2] if keep else 1 - meta[2]
    for t in range(3):
        cols = pl.ds(pl.multiple_of(core * half + t * part, 128), part)
        value = dot_nn(xt[...], dqkv[:, cols])
        store_parts(out, slice(t * part, (t + 1) * part), value, meta, core)
    if blocks:
        small = refs[0]
        small[...] = jnp.zeros_like(small)
        for b in range(blocks):
            small[b * SLOT : (b + 1) * SLOT, :] = tables[2 * b][...]
            small[b * SLOT + SHIFT + 2 : b * SLOT + SHIFT + 3, :] = tables[2 * b + 1][...]
        extra = small[...].T * (core == 0).astype(f32)
        store_parts(out, slice(half, half + LANES), extra, meta, core)


def unproject_kernel(relative, meta, dqkv, dr1, weight, *refs):
    outs, dx = refs[:-1], refs[-1]
    tokens, width = dr1.shape
    target = dx if relative else outs[0]
    for n in range(width // GROUP):
        cols = slice(n * GROUP, (n + 1) * GROUP)
        target[:, cols] = dr1[:, cols] + dot_nt(dqkv[...], weight[cols, :])
    for k in range(relative):
        part = tokens // relative
        first = pl.multiple_of((k ^ meta[0]) * part, part)
        outs[k][0] = dx[pl.ds(first, part), :].astype(bf16)


def prepare_kernel(ends, meta, *refs):
    fars, (own, other, *refs) = refs[:7], refs[7:]
    *x_parts, table, inputs, attn, out, point, depth, gains, shifts, sems = refs
    nears = (inputs, attn, out, point, depth, gains, shifts)
    copies = [
        pltpu.make_async_copy(fars[n].at[m], nears[n].at[m], sems.at[n])
        for n in range(4)
        for m in range(nears[n].shape[0])
    ]
    copies += [pltpu.make_async_copy(fars[n], nears[n], sems.at[n]) for n in range(4, 7)]
    for copy in copies:
        copy.start()
    seq_count, blocks = inputs.shape[0], attn.shape[0]
    rows, half, cut = attn.shape[1], attn.shape[2] // 2, out.shape[2] // 2
    table[...] = jnp.zeros_like(table)
    for copy in copies:
        copy.wait()
    for b in range(blocks):
        start = b * SLOT
        for j in range(depth.shape[0]):
            table[start + j : start + j + 1, :rows] = depth[j, b : b + 1, :]
        table[start + GAIN : start + SHIFT, :rows] = gains[b]
        for j in range(shifts.shape[0]):
            at = start + SHIFT + j
            table[at : at + 1, :rows] = shifts[j, b : b + 1, :]
    small = table[...].T[:rows]
    for k, part in enumerate(x_parts):
        part[...] = inputs[jnp.minimum(meta[0] ^ k, seq_count - 1)]
    for to, core in ((own, meta[2]), (other, 1 - meta[2])):
        wide = pl.ds(pl.multiple_of(core * half, 128), half)
        narrow = pl.ds(pl.multiple_of(core * cut, 128), cut)
        to[:, half : half + LANES] = (small * (core == 0).astype(f32)).astype(bf16)
        for b in range(blocks):
            start = 0 if b == 0 else ends[2 * b - 1]
            to[:, start : start + half] = attn[b, :, wide].astype(bf16)
            start = ends[2 * b]
            to[:, start : start + cut] = out[b, :, narrow].astype(bf16)
            to[:, start + cut : start + 2 * cut] = point[b, :, narrow].astype(bf16)


def pair_kernel(meta, own, given, *refs):
    outs, (rows_ref,) = refs[:-1], refs[-1:]
    rows = own.shape[0]
    mine, theirs = own[...].astype(f32), given[...].astype(f32)
    rows_ref[0:rows, :] = jnp.where(meta[2] == 0, mine, theirs)
    rows_ref[rows : 2 * rows, :] = jnp.where(meta[2] == 0, theirs, mine)
    start = 0
    for out in outs:
        stop = start + out.shape[-1]
        out[0] = rows_ref[:, start:stop].astype(bf16)
        start = stop


def end_kernel(meta, kept, got, own, other, rows_ref):
    rows = own.shape[0]
    rows_ref[...] = kept[0].astype(f32) + got[0].astype(f32)
    first, second = rows_ref[0:rows, :], rows_ref[rows : 2 * rows, :]
    own[...] = jnp.where(meta[2] == 0, first, second)
    other[...] = jnp.where(meta[2] == 0, second, first).astype(bf16)


def settle_kernel(seqs, meta, *refs):
    *parts, out, mark, all_parts = refs
    mark[...] = jnp.zeros_like(mark)
    at = 0
    for part in parts:
        for n in range(part.shape[0]):
            all_parts[at] = part[n]
            at += 1
    for i in range(out.shape[0]):
        out[i] = all_parts[i ^ meta[0]].astype(out.dtype)


def adam_update(master, first, second, gradient, step_rate):
    first_new = beta_first * first + (1.0 - beta_first) * gradient
    second_new = beta_second * second + (1.0 - beta_second) * gradient * gradient
    first_hat = first_new / (1.0 - beta_first**STEP)
    second_hat = second_new / (1.0 - beta_second**STEP)
    updated = master - step_rate * (
        first_hat / (jnp.sqrt(second_hat) + adam_eps) + weight_decay * master
    )
    return (updated, first_new, second_new, updated.astype(jnp.bfloat16))


def adam_kernel(places, rates, smalls, meta, *refs):
    count = 2 * (1 + max(index for spots in places for index, _ in spots))
    grads, refs = refs[:count], refs[count:]
    arrays = len(places) + len(smalls)
    states = [refs[3 * n : 3 * n + 3] for n in range(arrays)]
    outs = [refs[3 * arrays + 4 * n : 3 * arrays + 4 * n + 4] for n in range(arrays)]
    mark, table = refs[7 * arrays :]
    mark[...] = jnp.zeros_like(mark)

    def pick(index, half, lanes):
        own, given = grads[2 * index][:, lanes], grads[2 * index + 1][:, lanes].astype(f32)
        return jnp.where(meta[2] == half, own, given)

    for spots, state, out, rate in zip(places, states, outs, rates):
        width = state[0].shape[2] // 2
        for b, (index, start) in enumerate(spots):
            for half in range(2):
                cols = slice(half * width, (half + 1) * width)
                gradient = pick(index, half, slice(start, start + width))
                values = adam_update(*[ref[b, :, cols] for ref in state], gradient, rate)
                for ref, value in zip(out, values):
                    ref[b, :, cols] = value
    if smalls:
        index, start = places[0][0]
        start += states[0][0].shape[2] // 2
        rows = grads[2 * index].shape[0]
        table[...] = jnp.zeros_like(table)
        table[:rows, :] = pick(index, 0, slice(start, start + LANES))
        sums = table[...].T
        for n, (row, rows_first, rate) in enumerate(smalls):
            state, out = states[len(places) + n], outs[len(places) + n]
            for i in range(state[0].shape[0]):
                if rows_first:
                    parts = [sums[b * SLOT + row + i :][:1] for b in range(state[0].shape[1])]
                    gradient = jnp.concatenate(parts)[:, :rows]
                else:
                    first = i * SLOT + row
                    gradient = sums[first : first + state[0].shape[1], :rows]
                values = adam_update(*[ref[i] for ref in state], gradient, rate)
                for ref, value in zip(out, values):
                    ref[i] = value


class Links:
    def __init__(self, seqs, copies):
        self.seqs, self.copies, self.ring = seqs, copies, copies // 2
        self.s = lax.axis_index("seq")
        position = lax.axis_index("dp")
        self.z, self.c = position // 2, position % 2

    def swap(self, array, seq=0, ring=0, core=0):
        pairs = [
            (s * self.copies + d, (s ^ seq) * self.copies + (d ^ (2 * ring + core)))
            for s in range(self.seqs)
            for d in range(self.copies)
        ]
        return lax.ppermute(array, AXES, pairs)

    def hop(self, array, axis, step):
        count = self.seqs if axis == "seq" else self.ring
        last = count.bit_length() - 2
        pairs = []
        for s in range(self.seqs):
            for d in range(self.copies):
                bit = 1 << (step if d % 2 == 0 else last - step)
                to_s, to_d = (s ^ bit, d) if axis == "seq" else (s, d ^ (2 * bit))
                pairs.append((s * self.copies + d, to_s * self.copies + to_d))
        return lax.ppermute(array, AXES, pairs)

    def steps(self, axis):
        return range((self.seqs if axis == "seq" else self.ring).bit_length() - 1)

    def place(self, m):
        return self.z ^ jnp.where(self.c == 0, m, flipped(m, self.ring))

    def around(self, block, axis, start=0, stop=None):
        for step in self.steps(axis)[start:stop]:
            block = join([block, self.hop(block, axis, step)])[0]
        return block

    def ring_block(self, block):
        _, rows, half = block.shape
        if rows % 16 == 0:
            return block
        placed = jnp.zeros_like(block)
        for m in range(self.ring):
            placed = lax.dynamic_update_slice(
                placed, block[m : m + 1], (self.place(m), jnp.int32(0), jnp.int32(0))
            )
        return placed.reshape(1, self.ring * rows, half)

    def both_cores(self, blocks):
        return blocks + [self.swap(one, core=1) for one in blocks]

    def finish(self, block, axis):
        return self.both_cores([block, self.hop(block, axis, self.steps(axis)[-1])])

    def ring_terms(self, terms):
        terms = [term[0] for term in terms]
        if terms[0].shape[0] > 1:
            return terms
        total = terms[0][0].astype(f32)
        for term in terms[1:]:
            total = total + term[0].astype(f32)
        total = total.reshape(self.ring, total.shape[0] // self.ring, total.shape[1])
        units = []
        for m in range(self.ring):
            at = self.z ^ jnp.where(self.c == 0, flipped(m, self.ring), m)
            units.append(lax.dynamic_index_in_dim(total, at, 0, keepdims=False))
        return [jnp.stack(units).astype(bf16)]


def shards(
    inputs,
    masked_positions,
    masked_grads,
    kernel_paths,
    attn_weight,
    out_weight,
    point_weight,
    depth_weight,
    gains,
    shifts,
    first_attn,
    first_out,
    first_point,
    first_depth,
    first_gains,
    first_shifts,
    second_attn,
    second_out,
    second_point,
    second_depth,
    second_gains,
    second_shifts,
):
    seq_count, part_tokens, width = inputs.shape
    seqs, copies = lax.axis_size("seq"), lax.axis_size("dp")
    devices = seqs * copies
    tokens = seqs * part_tokens
    blocks, rows, _ = attn_weight.shape
    taps = depth_weight.shape[1]
    scale = (width // HEADS) ** (-0.5)
    links = Links(seqs, copies)
    aligned = (2 * rows) % 16 == 0
    subs = links.ring if aligned else 1
    part_rows = width // (seqs * subs)
    half = 3 * width // 2
    place = links.s
    mine = jnp.minimum(place, seq_count - 1)
    live = (place < seq_count).astype(jnp.int32)
    own_paths = lax.dynamic_index_in_dim(kernel_paths, mine, 0, keepdims=False)
    meta = jnp.concatenate(
        [
            jnp.stack([place, links.z if subs > 1 else jnp.zeros_like(links.z), links.c]),
            own_paths,
            live[None],
        ]
    ).astype(jnp.int32)
    cut = width // 2
    ends = [half + LANES, half + LANES + width]
    ends += [ends[1] + half, ends[1] + half + width]

    def shape(*dims, dtype=f32):
        return jax.ShapeDtypeStruct(dims, dtype)

    dma = pltpu.SemaphoreType.DMA
    square = (width, width)
    wide = (width, 3 * width)

    def attend(b, parts, pieces, table, after=()):
        near = b == blocks - 1
        outs = (
            Stored(wide, bf16),
            Stored((width, tokens), bf16),
            Stored((tokens, 3 * width), bf16),
            shape(tokens, width, dtype=bf16),
            shape(width, tokens, dtype=bf16) if near else Stored((width, tokens), bf16),
            Stored((LANES, tokens), f32),
        )
        scratch = [
            pltpu.VMEM(wide, bf16),
            pltpu.VMEM((width, tokens), bf16),
            pltpu.VMEM((tokens, 3 * width), bf16),
            pltpu.VMEM((LANES, tokens), f32),
            dma((7,)),
        ]
        if not near:
            scratch = [pltpu.VMEM((width, tokens), bf16)] + scratch
        if b == 0:
            outs = (shape(blocks * SLOT, width), shape(tokens, width, dtype=bf16)) + outs
            scratch += [pltpu.VMEM((2, width, LANES), bf16)]
        return call(
            partial(attend_kernel, b, near, len(parts), scale),
            outs,
            [smem_spec()] + [vmem_spec()] * ((1 if b else 0) + len(parts) + len(pieces)),
            [meta] + ([table] if b else []) + list(parts) + list(pieces),
            scratch,
            11 * 10**9,
            f"attend_{b}",
            after,
        )

    def mix(b, table, x, o, pieces, after=()):
        final = b == blocks - 1
        kept = (
            ((tokens, width), f32),
            ((tokens, width), f32),
            ((width, tokens), bf16),
            ((tokens, LANES), f32),
            (square, bf16),
            (square, bf16),
        )
        if final:
            outs = (shape(1, part_tokens, width, dtype=bf16),) * seqs
            outs += tuple(jax.ShapeDtypeStruct(*one) for one in kept)
        else:
            outs = (shape(tokens, width), shape(tokens, width, dtype=bf16))
            outs += tuple(Stored(*one) for one in kept)
        return call(
            partial(
                mix_kernel, b, len(pieces), final and aligned, taps, final, seqs if final else 0
            ),
            outs,
            [smem_spec()] + [vmem_spec()] * (3 + len(pieces)),
            [meta, table, x, o, *pieces],
            ([] if final else [pltpu.VMEM(*one) for one in kept])
            + [
                pltpu.VMEM((tokens, width), f32),
                pltpu.VMEM((tokens, width), f32),
                pltpu.VMEM((tokens + 2 * PAD, width), f32),
                pltpu.VMEM((tokens, width), bf16),
                dma((10,)),
            ],
            7 * 10**9,
            f"mix_{b}",
            after,
        )

    def unmix(b, table, upstream, saved, after=(), fetch=()):
        last = b == blocks - 1
        parts = shape(seqs, subs, part_rows, width, dtype=bf16)
        return call(
            partial(unmix_kernel, b, taps, last),
            (
                shape(tokens, width),
                shape(tokens, width, dtype=bf16),
                shape(SLOT, width),
                shape(SLOT, tokens),
                parts,
                parts,
            ),
            [smem_spec()] + [vmem_spec()] * (len(upstream) + 1 + len(saved)),
            [meta, table, *upstream, *saved],
            [
                pltpu.VMEM((tokens, width), f32),
                pltpu.VMEM((tokens, width), bf16),
                pltpu.VMEM((tokens + 2 * PAD, width), f32),
                pltpu.VMEM((tokens + 2 * PAD, width), f32),
            ],
            10 * 10**9,
            f"unmix_{b}",
            after,
            fetch,
        )

    def unattend(b, qkv, do, lse, inner, after=(), fetch=()):
        return call(
            partial(unattend_kernel, scale),
            (shape(tokens, 3 * width, dtype=bf16), shape(1, width)),
            [smem_spec()] + [vmem_spec()] * 4,
            [meta, qkv, do, lse, inner],
            [],
            11 * 10**9,
            f"unattend_{b}",
            after,
            fetch,
        )

    def attn_grad(b, keep, dqkv, xt, tables, after=()):
        span = half + (0 if b else LANES)
        return call(
            partial(attn_grad_kernel, len(tables) // 2, keep),
            (shape(seqs, subs, part_rows, span, dtype=bf16), TOKEN),
            [smem_spec()] + [vmem_spec()] * (2 + len(tables)),
            [meta, dqkv, xt, *tables],
            [pltpu.VMEM((LANES, width), f32)] if tables else [],
            10**8,
            f"attn_grad_{b}",
            after,
        )

    def unproject(b, dqkv, dr1, weight, after=(), fetch=()):
        return call(
            partial(unproject_kernel, 0 if b else seqs),
            (shape(tokens, width),) if b else (shape(1, part_tokens, width, dtype=bf16),) * seqs,
            [smem_spec()] + [vmem_spec()] * 3,
            [meta, dqkv, dr1, weight],
            [pltpu.VMEM((tokens, width), f32)],
            4 * 10**9,
            f"unproject_{b}",
            after,
            fetch,
        )

    def settle(parts, dtype, after=()):
        return call(
            partial(settle_kernel, seqs),
            (shape(seq_count, part_tokens, width, dtype=dtype), TOKEN),
            [smem_spec()] + [vmem_spec()] * len(parts),
            [meta, *parts],
            [pltpu.VMEM((seqs, part_tokens, width), bf16)],
            10**8,
            "settle",
            after,
        )

    def end(kept, got, after=()):
        span = kept.shape[-1]
        own, other = call(
            end_kernel,
            (shape(rows, span), shape(rows, span, dtype=bf16)),
            [smem_spec(), vmem_spec(), vmem_spec()],
            [meta, kept, got],
            [pltpu.VMEM((2 * rows, span), f32)],
            10**8,
            "end",
            after,
        )
        return own, links.swap(other, core=1)

    def adam(places, rates, smalls, grads, states, fetch=()):
        outs = []
        for state in states:
            outs += [shape(*state[0].shape)] * 3 + [shape(*state[0].shape, dtype=bf16)]
        flat = [array for state in states for array in state]
        results = call(
            partial(adam_kernel, places, rates, smalls),
            (*outs, TOKEN),
            [smem_spec()] + [vmem_spec()] * (len(grads) + len(flat)),
            [meta, *grads, *flat],
            [pltpu.VMEM((LANES, LANES), f32)],
            10**8,
            "adam",
            (),
            fetch,
        )
        results, near = results if fetch else (results, ())
        return [results[4 * n : 4 * n + 4] for n in range(len(states))], results[-1], near

    depth_rows = [jnp.swapaxes(a, 0, 1) for a in (depth_weight, first_depth, second_depth)]
    shift_rows = [jnp.swapaxes(a, 0, 1) for a in (shifts, first_shifts, second_shifts)]
    own, other, *x_parts = call(
        partial(prepare_kernel, ends),
        (shape(rows, ends[3], dtype=bf16),) * 2
        + (shape(part_tokens, width, dtype=bf16),) * seqs,
        [smem_spec()] + [hbm_spec()] * 7,
        [meta, inputs, attn_weight, out_weight, point_weight, depth_rows[0], gains, shift_rows[0]],
        [pltpu.VMEM((LANES, LANES), f32)]
        + [
            pltpu.VMEM(array.shape, array.dtype)
            for array in (inputs, attn_weight, out_weight, point_weight)
            + (depth_rows[0], gains, shift_rows[0])
        ]
        + [dma((7,))],
        10**8,
        "prepare",
    )
    given = links.swap(other, core=1)
    widths = (ends[0], ends[2] - ends[0], width)
    unit_a0, unit_mid, unit_m1 = call(
        pair_kernel,
        tuple(shape(1, 2 * rows, span, dtype=bf16) for span in widths),
        [smem_spec(), vmem_spec(), vmem_spec()],
        [meta, own, given],
        [pltpu.VMEM((2 * rows, ends[3]), f32)],
        10**8,
        "pair",
    )
    x_parts = [x_parts[0]] + [links.swap(x_parts[k], seq=k) for k in range(1, seqs)]
    last_seq, last_ring = links.steps("seq")[-1], links.steps("ring")[-1]
    block_a0 = links.around(unit_a0, "ring", stop=-1)
    got_a0 = links.hop(block_a0, "ring", last_ring)
    plane_m1, marks = unit_m1, [*x_parts[1:]]
    if aligned:
        plane_m1, done = join([unit_m1, links.hop(unit_m1, "seq", 0)])
        marks.append(done)
    ring_a0, done = join([block_a0, got_a0], after=marks)
    ring_a0 = links.ring_block(ring_a0)
    got_a0 = links.hop(ring_a0[None], "seq", 0)
    unit_mid, _ = join([unit_mid], after=(done,))
    got_mid = links.hop(unit_mid, "ring", 0)
    part_mid, done = join([unit_mid, got_mid])
    marks = [done]
    if aligned:
        plane_m1, done = join([plane_m1, links.hop(plane_m1, "seq", last_seq)])
        marks.append(done)
    plane_a0, _ = join([ring_a0[None], got_a0], after=marks)
    pieces_a0 = links.finish(plane_a0, "seq")
    ring_mid = links.ring_block(links.around(part_mid, "ring", 1))
    ring_m0, ring_a1 = ring_mid[..., :width], ring_mid[..., width:]
    got_m0 = [links.swap(ring_m0[None], seq=k) for k in range(1, seqs)]
    got_a1 = links.hop(ring_a1[None], "seq", 0)
    parts = [got_m0, [ring_a1[None], got_a1]]
    if aligned:
        parts.append([plane_m1[None], links.hop(plane_m1[None], "ring", 0)])
    table, x16, w_0, xt_0, qkv_0, o_0, ot_0, lse_0 = attend(
        0, x_parts, pieces_a0, None, after=(ring_m0, ring_a1)
    )
    got_m0, plane_a1, *plane_m1, done = joins(parts, after=(table,))
    pieces_m0 = links.both_cores([ring_m0[None], got_m0])
    parts = [[links.hop(plane_a1, "seq", last_seq)]]
    if aligned:
        parts.append([links.hop(plane_m1[0], "ring", last_ring)])
    y_0, x_1, *saved_0 = mix(0, table, x16, o_0, pieces_m0, after=(done,))
    got_a1, *got_m1, _ = joins(parts, after=(x_1,))
    pieces_a1 = links.both_cores([plane_a1, got_a1])
    w_1, xt_1, qkv_1, o_1, ot_1, lse_1 = attend(1, [x_1], pieces_a1, table)
    if aligned:
        pieces_m1 = links.both_cores([*plane_m1, *got_m1])
    else:
        ring_m1 = links.ring_block(links.around(unit_m1, "ring"))
        pieces_m1 = links.finish(links.around(ring_m1[None], "seq", stop=-1), "seq")
    outs_1 = mix(1, table, y_0, o_1, pieces_m1)
    y_1, saved_1 = outs_1[:seqs], outs_1[seqs:]

    y_back = [links.swap(y_1[k], seq=k) for k in range(1, seqs)]
    places = masked_positions[:, None, :]
    (dr1, do, sums_1, inner, keep, send), near = unmix(
        1, table, (places, masked_grads), (*saved_1, ot_1), fetch=(qkv_1, lse_1)
    )
    y_back, done = join(y_back, after=(sums_1,))
    given_m1 = links.swap(send, core=1)
    terms_m1 = [keep, given_m1]
    (dqkv, bias_1), (xt, weight) = unattend(
        1, near[0], do, near[1], inner, after=(done,), fetch=(xt_1, w_1)
    )
    send, done = attn_grad(1, False, dqkv, xt, ())
    given_a1 = links.swap(send, core=1)
    keep, _ = attn_grad(1, True, dqkv, xt, (), after=(done,))
    late, sent, done = fold([terms_m1, [keep, given_a1]])
    got = links.hop(sent, "seq", 0)
    (dy,), near = unproject(1, dqkv, dr1, weight, after=(done,), fetch=(*saved_0, ot_0))
    (dr1, do, sums_0, inner, keep, send), near = unmix(0, table, (dy,), near, fetch=(qkv_0, lse_0))
    late, sent, done = fold([[late, got]], after=(sums_0,))
    got = links.hop(sent, "seq", 1)
    mixed, sent, done_mixed = fold([[keep, links.swap(send, core=1)]], after=(done,))
    got_mixed = links.hop(sent, "seq", 0)
    (dqkv, bias_0), (xt, weight) = unattend(
        0, near[0], do, near[1], inner, after=(done, done_mixed), fetch=(xt_0, w_0)
    )
    mixed, sent, done_mixed = fold([[mixed, got_mixed]], after=(bias_0,))
    got_mixed = links.hop(sent, "seq", 1)
    late, sent, done = fold([links.ring_terms([late, got])], after=(bias_0,))
    got = links.hop(sent, "ring", 0)
    tables = (sums_0, bias_0, sums_1, bias_1)
    send, done = attn_grad(0, False, dqkv, xt, tables, after=(done, done_mixed))
    given = links.swap(send, core=1)
    keep, _ = attn_grad(0, True, dqkv, xt, tables, after=(done,))
    final, sent, done = fold([[keep, given]])
    got_final = links.hop(sent, "seq", 0)
    dx = unproject(0, dqkv, dr1, weight, after=(done, touch(got_mixed, got)))
    for step in links.steps("ring")[1:]:
        late, sent, done = fold([[late, got]], after=(dx[0],))
        got = links.hop(sent, "ring", step)
    mixed, sent, done_mixed = fold([links.ring_terms([mixed, got_mixed])], after=(dx[0], done))
    got_mixed = links.hop(sent, "ring", 0)
    final, sent, done = fold([[final, got_final]], after=(done_mixed,))
    got_final = links.hop(sent, "seq", 1)
    for step in links.steps("ring")[1:]:
        mixed, sent, done_mixed = fold([[mixed, got_mixed]], after=(done,))
        got_mixed = links.hop(sent, "ring", step)
    result, done_y = settle([y_1[0], y_back], bf16)
    final, sent, done = fold(
        [links.ring_terms([final, got_final])], after=(done_mixed, touch(got), done_y)
    )
    got_final = links.hop(sent, "ring", 0)
    *dx_sent, _ = joins([[one] for one in dx[1:]], after=(done,))
    x_back = [links.swap(dx_sent[k - 1], seq=k) for k in range(1, seqs)]
    for step in links.steps("ring")[1:]:
        final, sent, _ = fold([[final, got_final]], after=(touch(got_mixed),))
        got_final = links.hop(sent, "ring", step)
    x_back, _ = join(x_back)
    input_grad, done_x = settle([dx[0], x_back], f32)
    grads = end(late, got) + end(mixed, got_mixed)
    (new_out, new_point), done_mix, states = adam(
        (((1, 0), (0, 0)), ((1, cut), (0, cut))),
        (rate_out, rate_point),
        (),
        grads,
        (
            (out_weight, first_out, second_out),
            (point_weight, first_point, second_point),
        ),
        fetch=(attn_weight, first_attn, second_attn),
    )
    (new_attn, new_depth, new_gains, new_shifts), _, _ = adam(
        (((0, 0), (1, width)),),
        (rate_attn,),
        ((0, True, rate_depth), (GAIN, False, rate_gain), (SHIFT, True, rate_vector)),
        end(final, got_final, (done_x, done_mix)) + grads[:2],
        (states, depth_rows, (gains, first_gains, second_gains), shift_rows),
    )
    new_depth, new_shifts = (
        [jnp.swapaxes(a, 0, 1) for a in new] for new in (new_depth, new_shifts)
    )
    updates = (new_attn, new_out, new_point, new_depth, new_gains, new_shifts)
    return (
        (result, input_grad)
        + tuple((entry[0] for entry in updates))
        + tuple((entry[1] for entry in updates))
        + tuple((entry[2] for entry in updates))
        + tuple((entry[3] for entry in updates))
    )


def solution(mesh):
    sequence = P("dp", "seq", None)
    matrix = P(None, AXES, None)
    vector = P(None, None, AXES)
    weights = (matrix,) * 3 + (vector,) * 3
    return jax.shard_map(
        shards,
        mesh=mesh,
        in_specs=(sequence, P("dp", None), P("dp", None, None), P("dp", None)) + weights * 3,
        out_specs=(sequence, sequence) + weights * 4,
        check_vma=False,
    )
```

```python
from functools import partial

import jax
import jax.numpy as jnp
from jax import lax
from jax.experimental import pallas as pl
from jax.experimental.pallas import tpu as pltpu
from jax.sharding import PartitionSpec as P

HEADS = 12
STEP = 10

norm_eps = 1e-05
beta_first = 0.5
beta_second = 0.5
adam_eps = 1e-08
weight_decay = 0.01
rate_attn = 0.03
rate_out = 0.25
rate_point = 0.03
rate_depth = 0.3
rate_gain = 0.45
rate_vector = 0.2

f32 = jnp.float32
bf16 = jnp.bfloat16
AXES = ("seq", "dp")
VMEM_BYTES = 24 * 2**20
GROUP = 256
ROWS = 64
PAD = 8

GAIN = 7
SHIFT = 9
SMALL = 14
SLOT = 16
LANES = 128


def dot_nn(a, b):
    return lax.dot_general(a, b, (((1,), (0,)), ((), ())), preferred_element_type=f32)


def dot_nt(a, b):
    return lax.dot_general(a, b, (((1,), (1,)), ((), ())), preferred_element_type=f32)


def dot_tn(a, b):
    return lax.dot_general(a, b, (((0,), (0,)), ((), ())), preferred_element_type=f32)


def vmem_spec():
    return pl.BlockSpec(memory_space=pltpu.VMEM)


def smem_spec():
    return pl.BlockSpec(memory_space=pltpu.SMEM)


def any_spec():
    return pl.BlockSpec(memory_space=pl.ANY)


def hbm_spec():
    return pl.BlockSpec(memory_space=pltpu.HBM)


class Stored(jax.ShapeDtypeStruct):
    pass


class Position:
    def __init__(self, ring):
        self.ring = ring

    def read(self):
        place = lax.axis_index("dp")
        ring = place // 2 if self.ring else jnp.zeros_like(place)
        return [lax.axis_index("seq"), ring, place % 2]


def call(body, outs, in_specs, args, scratch, cost, name, after=(), fetch=()):
    position = args[0] if isinstance(args[0], Position) else None
    if position:
        in_specs, args = in_specs[1:], args[1:]
    n_in, n_after, n_out, n_fetch = len(in_specs), len(after), len(outs), len(fetch)

    def kernel(*refs):
        first = n_in + n_after
        far, refs = refs[first : first + n_fetch], refs[:n_in] + refs[first + n_fetch :]
        near = refs[n_in + n_out : n_in + n_out + n_fetch]
        refs = refs[: n_in + n_out] + refs[n_in + n_out + n_fetch :]
        copies = []
        if n_fetch:
            for n in range(n_fetch):
                count = 4 if far[n].shape[0] % 64 == 0 else 1
                copies += chunk_copies(far[n], near[n], refs[-1].at[n], count)
            refs = refs[:-1]
        for copy in copies:
            copy.start()
        body(*([position.read()] if position else []), *refs)
        for copy in copies:
            copy.wait()

    args = [
        pltpu.with_memory_space_constraint(arg, pltpu.HBM)
        if spec.memory_space == pltpu.HBM
        else arg
        for arg, spec in zip(args, in_specs, strict=True)
    ]
    fetch = [pltpu.with_memory_space_constraint(arg, pltpu.HBM) for arg in fetch]
    results = pl.pallas_call(
        kernel,
        out_shape=tuple(
            pltpu.HBM(out.shape, out.dtype) if isinstance(out, Stored) else out for out in outs
        )
        + tuple(jax.ShapeDtypeStruct(a.shape, a.dtype) for a in fetch),
        in_specs=list(in_specs) + [vmem_spec()] * n_after + [hbm_spec()] * n_fetch,
        out_specs=tuple(hbm_spec() if isinstance(out, Stored) else vmem_spec() for out in outs)
        + (vmem_spec(),) * n_fetch,
        scratch_shapes=list(scratch) + ([pltpu.SemaphoreType.DMA((n_fetch,))] if fetch else []),
        compiler_params=pltpu.CompilerParams(vmem_limit_bytes=VMEM_BYTES),
        cost_estimate=pl.CostEstimate(flops=cost, bytes_accessed=2**18, transcendentals=0),
        name=name,
    )(*args, *after, *fetch)
    return (results[:n_out], results[n_out:]) if n_fetch else results


TOKEN = jax.ShapeDtypeStruct((8, 128), f32)


def small_call(body, outs, args, name, after=(), scratch=()):
    specs = [vmem_spec()] * len(args)
    return call(body, outs, specs, args, list(scratch), 10**8, name, after)


def joins(groups, after=(), mark=False):
    def kernel(*refs):
        used = 0
        for group, out in zip(groups, refs[sum(map(len, groups)) :]):
            start = 0
            for part in refs[used : used + len(group)]:
                count = part.shape[0]
                out[start : start + count] = part[...]
                start += count
            used += len(group)
        if mark:
            refs[-1][...] = jnp.zeros_like(refs[-1])

    outs = [
        jax.ShapeDtypeStruct((sum(p.shape[0] for p in group),) + group[0].shape[1:], group[0].dtype)
        for group in groups
    ]
    parts = [part for group in groups for part in group]
    return small_call(kernel, (*outs, TOKEN) if mark else outs, parts, "join", after)


def join(parts, after=()):
    return joins([parts], after)[0]


def join_mark(parts, after=()):
    return joins([parts], after, True)


def fold(groups, after=(), mark=True):
    terms = [term for group in groups for term in group]
    widths = [group[0].shape[-1] for group in groups]
    lead = terms[0].shape[:-2]
    rows, half = terms[0].shape[-2], lead[0] // 2

    def kernel(*refs):
        ins, (kept, sent, *marks) = refs[: len(terms)], refs[len(terms) :]

        def block(out, to, at):
            start, used = 0, 0
            for group, width in zip(groups, widths, strict=True):
                total = ins[used][at].astype(f32)
                for term in ins[used + 1 : used + len(group)]:
                    total = total + term[at].astype(f32)
                out[(*to, slice(None), slice(start, start + width))] = total.astype(bf16)
                start, used = start + width, used + len(group)

        for n in range(half):
            if len(lead) == 1:
                block(kept, (n,), (n,))
                block(sent, (n,), (half + n,))
            else:

                def step(m, carry, n=n):
                    block(kept, (n, m), (n, m))
                    block(sent, (n, m), (half + n, m))
                    return carry

                lax.fori_loop(0, lead[1], step, 0)
        for one in marks:
            one[...] = jnp.zeros_like(one)

    out = jax.ShapeDtypeStruct((half,) + lead[1:] + (rows, sum(widths)), bf16)
    return small_call(kernel, (out, out, TOKEN) if mark else (out, out), terms, "fold", after)


def touch(*arrays):
    def kernel(*refs):
        refs[-1][...] = jnp.zeros_like(refs[-1])

    return small_call(kernel, (TOKEN,), arrays, "touch")[0]


def chunk_copies(source, dest, sem, count=4):
    rows = source.shape[0] // count
    return [
        pltpu.make_async_copy(
            source.at[pl.ds(n * rows, rows)], dest.at[pl.ds(n * rows, rows)], sem
        )
        for n in range(count)
    ]


def group_loop(width, body):
    def step(g, carry):
        first = pl.multiple_of(g * GROUP, GROUP)
        return body(g, [pl.ds(part * width + first, GROUP) for part in range(3)], carry)

    return partial(lax.fori_loop, 0, width // GROUP, step)


def strip_loop(width, body):
    def step(n, carry):
        body(pl.ds(pl.multiple_of(n * LANES, LANES), LANES))
        return carry

    lax.fori_loop(0, width // LANES, step, 0)


def row_loop(total, body, rows=ROWS):
    def step(i, carry):
        body(pl.multiple_of(i * rows, rows))
        return carry

    lax.fori_loop(0, total // rows, step, 0, unroll=True)


def flipped(index, count):
    bits, out = count.bit_length() - 1, 0
    for bit in range(bits):
        out = out | (((index >> bit) & 1) << (bits - 1 - bit))
    return out


def weight_copies(meta, pieces, dest, sem, first, half, ring_last=False, whole=False):
    s, z, c = meta[0], meta[1], meta[2]
    copies, first_late = [], pieces[0].shape[0]
    late_count = first_late + pieces[1].shape[0]
    for n, piece in enumerate(pieces):
        late, early, rows, width = piece.shape
        core = (n // 2) ^ c
        for a in range(late):
            for b in range(early):
                outer, inner = (n % 2) * first_late + a, b
                if 2 * first_late == late_count:
                    outer = jnp.where(core == 0, outer, flipped(outer, late_count))
                inner = jnp.where(core == 0, inner, flipped(inner, early))
                if ring_last:
                    row = ((inner ^ s) * late_count + (outer ^ z)) * rows
                else:
                    row = ((outer ^ s) * early + (inner ^ z)) * rows
                row = pl.multiple_of(row, rows)
                source = piece.at[a, b]
                if (first, half) != (0, width):
                    source = piece.at[a, b, :, pl.ds(first, half)]
                if whole:
                    target = dest.at[core, pl.ds(row, rows)]
                else:
                    col = pl.multiple_of(core * half, 128)
                    target = dest.at[pl.ds(row, rows), pl.ds(col, half)]
                copies.append(pltpu.make_async_copy(source, target, sem))
    return copies


def head_masks(scale):
    lane = lax.broadcasted_iota(jnp.int32, (1, GROUP), 1) // (GROUP // 4)
    return [jnp.where(lane == h, f32(scale), f32(0)).astype(bf16) for h in range(4)]


def attend_kernel(block, near, x_parts, scale, meta, *refs):
    if block:
        table, refs = refs[0], refs[1:]
    x_refs, pieces = refs[:x_parts], refs[x_parts : x_parts + 4]
    refs = refs[x_parts + 4 :]
    if block == 0:
        table, x, refs = refs[0], refs[1], refs[2:]
    w_far, xt_far, qkv_far, o_out, ot_far, lse_far, *refs = refs
    if near:
        ot = ot_far
    else:
        ot, refs = refs[0], refs[1:]
    weight, xt, qkv, lse, sems = refs[:5]
    half = weight.shape[1] // 2
    if block == 0:
        (extra,) = refs[5:]
        smalls = weight_copies(meta, pieces, extra, sems.at[0], half, LANES, whole=True)
        for copy in smalls:
            copy.start()
        part_rows = x_refs[0].shape[0]
        x_copies = [
            pltpu.make_async_copy(
                x_refs[k],
                x.at[pl.ds(pl.multiple_of((k ^ meta[0]) * part_rows, part_rows), part_rows)],
                sems.at[1],
            )
            for k in range(x_parts)
        ]
        for copy in x_copies:
            copy.start()
    else:
        x = x_refs[0]
    copies = weight_copies(meta, pieces, weight, sems.at[2], 0, half)
    for copy in copies:
        copy.start()
    if block == 0:
        for copy in x_copies:
            copy.wait()
        for copy in smalls:
            copy.wait()
        table[...] = extra[0].astype(f32).T[: table.shape[0]]
    small = table.at[pl.ds(SLOT * block, SLOT)]
    xt[...] = x[...].T
    xt_store = pltpu.make_async_copy(xt, xt_far, sems.at[3])
    xt_store.start()
    for copy in copies:
        copy.wait()
    w_stores = chunk_copies(weight, w_far, sems.at[2])
    for copy in w_stores:
        copy.start()
    tokens, width = x.shape
    scaled, plain = head_masks(scale), head_masks(1.0)
    lane = lax.broadcasted_iota(jnp.int32, (tokens, 128), 1)
    sums = jnp.zeros((tokens, 128), f32)
    for g in range(width // GROUP):
        cols = slice(g * GROUP, (g + 1) * GROUP)
        cols_k = slice(width + g * GROUP, width + (g + 1) * GROUP)
        cols_v = slice(2 * width + g * GROUP, 2 * width + (g + 1) * GROUP)
        bias = small[SHIFT + 2 : SHIFT + 3, cols]
        qkv[:, cols] = (dot_nn(x[...], weight[:, cols]) + bias).astype(bf16)
        qkv[:, cols_k] = dot_nn(x[...], weight[:, cols_k]).astype(bf16)
        qkv[:, cols_v] = dot_nn(x[...], weight[:, cols_v]).astype(bf16)
        for part in (cols, cols_k, cols_v):
            pltpu.make_async_copy(qkv.at[:, part], qkv_far.at[:, part], sems.at[4]).start()
        mixed = jnp.zeros((tokens, GROUP), f32)
        for h in range(4):
            scores = dot_nt(qkv[:, cols] * scaled[h], qkv[:, cols_k])
            top = jnp.max(scores, axis=-1, keepdims=True)
            weights = jnp.exp(scores - top)
            total = jnp.sum(weights, axis=-1, keepdims=True)
            part = dot_nn(weights.astype(bf16), qkv[:, cols_v] * plain[h])
            mixed = mixed + part * (1.0 / total)
            sums = jnp.where(lane == g * 4 + h, top + jnp.log(total), sums)
        o_out[:, cols] = mixed.astype(bf16)
        ot[cols, :] = o_out[:, cols].T
        if not near:
            pltpu.make_async_copy(ot.at[cols], ot_far.at[cols], sems.at[5]).start()
    lse[...] = sums.T
    lse_store = pltpu.make_async_copy(lse, lse_far, sems.at[6])
    lse_store.start()
    for copy in w_stores + [lse_store]:
        copy.wait()
    xt_store.wait()
    pltpu.make_async_copy(qkv, qkv_far, sems.at[4]).wait()
    if not near:
        pltpu.make_async_copy(ot, ot_far, sems.at[5]).wait()


def tap_rows(meta, small, block, taps, lanes):
    path = meta[3 + block]
    half = taps // 2
    return [
        small[j : j + 1, lanes] * jnp.where(path + 1 >= abs(j - half), f32(1), f32(0))
        for j in range(taps)
    ]


def norm_rows(r, gain, shift):
    center = r - jnp.mean(r, axis=-1, keepdims=True)
    inverse = lax.rsqrt(jnp.mean(center * center, axis=-1, keepdims=True) + norm_eps)
    normed = center * inverse
    return normed * gain + shift, normed, inverse


def mix_kernel(block, count, ring_last, taps, near, relative, meta, table, x, o_ref, *refs):
    pieces = refs[:count]
    refs = refs[count:]
    y_out, refs = (None, refs) if relative else (refs[0], refs[1:])
    *refs, acc, y1, zpad, hc, sems = refs
    if near:
        outs, kept = refs[:-6], refs[-6:]
    else:
        outs, far, kept = refs[:-12], refs[-12:-6], refs[-6:]
    xh1, xh2, hct, stats, w_out, w_point = kept
    y_low = outs[0]
    stores = []

    def store(n, rows=None):
        if not near:
            source, target = kept[n], far[n]
            if rows is not None:
                source, target = source.at[rows], target.at[rows]
            copy = pltpu.make_async_copy(source, target, sems.at[4 + n])
            copy.start()
            if rows is None:
                stores.append(copy)

    small = table.at[pl.ds(SLOT * block, SLOT)]
    tokens, width = o_ref.shape
    half = width // 2
    copies = weight_copies(meta, pieces, w_out, sems.at[0], 0, half, ring_last)
    late_copies = weight_copies(meta, pieces, w_point, sems.at[1], half, half, ring_last)
    for copy in copies + late_copies:
        copy.start()
    zpad[0:PAD, :] = jnp.zeros((PAD, width), f32)
    zpad[tokens + PAD :, :] = jnp.zeros((PAD, width), f32)
    for copy in copies:
        copy.wait()
    store(4)
    for n in range(width // GROUP):
        cols = slice(n * GROUP, (n + 1) * GROUP)
        acc[:, cols] = dot_nn(o_ref[...], w_out[:, cols])

    def first_norm(row):
        rows = pl.ds(row, ROWS)
        stream = x[rows, :].astype(f32) + (acc[rows, :] + small[SHIFT + 3 : SHIFT + 4, :])
        out, normed, inverse = norm_rows(
            stream, small[GAIN : GAIN + 1, :], small[SHIFT : SHIFT + 1, :]
        )
        y1[rows, :] = out
        xh1[rows, :] = normed
        stats[rows, 0:1] = inverse
        zpad[pl.ds(row + PAD, ROWS), :] = out.astype(bf16).astype(f32)

    row_loop(tokens, first_norm)
    store(0)
    reach = taps // 2

    weights = tap_rows(meta, small, block, taps, slice(None))

    def convolve(row):
        window = zpad[pl.ds(row, ROWS + 2 * PAD), :]
        total = jnp.zeros((ROWS, width), f32)
        for j in range(taps):
            start = PAD - reach + j
            total = total + weights[j] * window[start : start + ROWS]
        hc[pl.ds(row, ROWS), :] = total.astype(bf16)

    row_loop(tokens, convolve)
    hct[...] = hc[...].T
    store(2)
    for copy in late_copies:
        copy.wait()
    store(5)
    for n in range(width // GROUP):
        cols = slice(n * GROUP, (n + 1) * GROUP)
        acc[:, cols] = dot_nn(hc[...], w_point[:, cols])

    def second_norm(row):
        rows = pl.ds(row, ROWS)
        stream = y1[rows, :] + (acc[rows, :] + small[SHIFT + 4 : SHIFT + 5, :])
        out, normed, inverse = norm_rows(
            stream, small[GAIN + 1 : GAIN + 2, :], small[SHIFT + 1 : SHIFT + 2, :]
        )
        xh2[rows, :] = normed
        stats[rows, 1:2] = inverse
        store(1, rows)
        if not relative:
            y_out[rows, :] = out
            y_low[rows, :] = out.astype(bf16)
        else:
            y1[rows, :] = out

    row_loop(tokens, second_norm)
    store(3)
    for k in range(relative):
        part = tokens // relative
        first = pl.multiple_of((k ^ meta[0]) * part, part)
        outs[k][0] = y1[pl.ds(first, part), :].astype(bf16)
    for copy in stores:
        copy.wait()
    if not near:
        pltpu.make_async_copy(xh2, far[1], sems.at[5]).wait()


def norm_rows_back(upstream, normed, inverse, gain):
    scaled = upstream * gain
    inner = (
        scaled
        - jnp.mean(scaled, axis=-1, keepdims=True)
        - normed * jnp.mean(scaled * normed, axis=-1, keepdims=True)
    )
    return inverse * inner


def column_sum(a):
    return jnp.sum(a, axis=0, keepdims=True)


def store_parts(out, columns, value, meta, core):
    seqs, subs, rows, _ = out.shape
    for k in range(seqs):
        for m in range(subs):
            start = (k * subs + m) * rows
            seq, ring = k ^ meta[0], m ^ meta[1]
            seq = jnp.where(core == 0, flipped(seq, seqs), seq)
            ring = jnp.where(core == 0, flipped(ring, subs), ring)
            out[seq, ring, :, columns] = value[start : start + rows].astype(bf16)


def unmix_kernel(block, taps, last, meta, table, *refs):
    small = table.at[pl.ds(SLOT * block, SLOT)]
    if last:
        places, grads = refs[:2]
        refs = refs[2:]
    else:
        dy_ref = refs[0]
        refs = refs[1:]
    xh1, xh2, hct, stats, w_out, w_point, ot, *refs = refs
    dr1, do_out, sums, inner, keep, send, dr2, du, dpad, zpad = refs
    tokens, width = dr1.shape
    half = width // 2
    sums[...] = jnp.zeros_like(sums)
    if last:
        mine = jnp.minimum(meta[0], places.shape[0] - 1)
        picked = places.shape[2]
        token = lax.broadcasted_iota(jnp.int32, (tokens, picked), 0)
        live = jnp.where(meta[5] > 0, f32(1), f32(0))
        picks = jnp.where(token == places[mine], live, f32(0)).astype(bf16)
        dr2[...] = dot_nn(picks, grads[mine])
    for pad in (dpad, zpad):
        pad[0:PAD, :] = jnp.zeros((PAD, width), f32)
        pad[tokens + PAD :, :] = jnp.zeros((PAD, width), f32)

    def second_norm(row):
        rows = pl.ds(row, ROWS)
        dy = dr2[rows, :] if last else dy_ref[rows, :]
        normed = xh2[rows, :]
        back = norm_rows_back(dy, normed, stats[rows, 1:2], small[GAIN + 1 : GAIN + 2, :])
        low = back.astype(bf16)
        dr2[rows, :] = back
        du[rows, :] = low
        sums[GAIN + 1 : GAIN + 2, :] += column_sum(dy * normed)
        sums[SHIFT + 1 : SHIFT + 2, :] += column_sum(dy)
        sums[SHIFT + 4 : SHIFT + 5, :] += column_sum(low.astype(f32))
        z = xh1[rows, :] * small[GAIN : GAIN + 1, :] + small[SHIFT : SHIFT + 1, :]
        zpad[pl.ds(row + PAD, ROWS), :] = z.astype(bf16).astype(f32)

    row_loop(tokens, second_norm)
    c = meta[2]
    mine = pl.ds(pl.multiple_of(c * half, 128), half)
    other = pl.ds(pl.multiple_of((1 - c) * half, 128), half)
    point_cols, out_cols = slice(half, width), slice(0, half)
    for n in range(width // GROUP):
        cols = slice(n * GROUP, (n + 1) * GROUP)
        back = dot_nt(du[...], w_point[cols, :])
        dpad[PAD : PAD + tokens, cols] = back.astype(bf16).astype(f32)
    store_parts(send, point_cols, dot_nn(hct[...], du[:, other]), meta, 1 - c)
    store_parts(keep, point_cols, dot_nn(hct[...], du[:, mine]), meta, c)
    path = meta[3 + block]
    reach = taps // 2

    def unconvolve(lanes):
        weights = tap_rows(meta, small, block, taps, lanes)
        tap_sums = [jnp.zeros((8, LANES), f32)] * taps
        for row in range(0, tokens, ROWS):
            window = dpad[row : row + ROWS + 2 * PAD, lanes]
            z_window = zpad[row : row + ROWS + 2 * PAD, lanes]
            here = window[PAD : PAD + ROWS]
            total = dr2[row : row + ROWS, lanes]
            for j in range(taps):
                start = PAD + reach - j
                total = total + weights[j] * window[start : start + ROWS]
                z_start = PAD - reach + j
                product = here * z_window[z_start : z_start + ROWS]
                tap_sums[j] = tap_sums[j] + jnp.sum(product.reshape(-1, 8, LANES), axis=0)
            dr2[row : row + ROWS, lanes] = total
        for j in range(taps):
            used = jnp.where(path + 1 >= abs(j - reach), f32(1), f32(0))
            sums[j : j + 1, lanes] = column_sum(tap_sums[j]) * used

    strip_loop(width, unconvolve)

    def first_norm(row):
        rows = pl.ds(row, ROWS)
        total = dr2[rows, :]
        normed = xh1[rows, :]
        back = norm_rows_back(total, normed, stats[rows, 0:1], small[GAIN : GAIN + 1, :])
        low = back.astype(bf16)
        dr1[rows, :] = back
        du[rows, :] = low
        sums[GAIN : GAIN + 1, :] += column_sum(total * normed)
        sums[SHIFT : SHIFT + 1, :] += column_sum(total)
        sums[SHIFT + 3 : SHIFT + 4, :] += column_sum(low.astype(f32))

    row_loop(tokens, first_norm)
    for n in range(width // GROUP):
        cols = slice(n * GROUP, (n + 1) * GROUP)
        do_out[:, cols] = dot_nt(du[...], w_out[cols, :]).astype(bf16)
        both = do_out[:, cols].T.astype(f32) * ot[cols, :].astype(f32)
        for h in range(4):
            size = GROUP // 4
            inner[n * 4 + h : n * 4 + h + 1, :] = column_sum(both[h * size : (h + 1) * size])
    store_parts(send, out_cols, dot_nn(ot[...], du[:, other]), meta, 1 - c)
    store_parts(keep, out_cols, dot_nn(ot[...], du[:, mine]), meta, c)


def unattend_kernel(scale, meta, qkv, do_ref, lse, inner, dqkv, bias):
    tokens, width = do_ref.shape
    scaled, plain = head_masks(scale), head_masks(1.0)

    def unattend_group(g, columns, carry):
        cols, cols_k, cols_v = columns
        dq = jnp.zeros((tokens, GROUP), f32)
        dk = jnp.zeros((tokens, GROUP), f32)
        dv = jnp.zeros((tokens, GROUP), f32)
        for h in range(4):
            row = pl.ds(g * 4 + h, 1)
            q = qkv[:, cols] * scaled[h]
            do = do_ref[:, cols] * plain[h]
            scores = dot_nt(qkv[:, cols_k], q)
            probs = jnp.exp(scores - lse[row, :])
            dp = dot_nt(qkv[:, cols_v], do)
            ds = (probs * (dp - inner[row, :])).astype(bf16)
            dv = dv + dot_nn(probs.astype(bf16), do)
            dk = dk + dot_nn(ds, q)
            dq = dq + dot_tn(ds, qkv[:, cols_k] * scaled[h])
        low = dq.astype(bf16)
        dqkv[:, cols] = low
        bias[:, cols] = column_sum(low.astype(f32))
        dqkv[:, cols_k] = dk.astype(bf16)
        dqkv[:, cols_v] = dv.astype(bf16)
        return carry

    group_loop(width, unattend_group)(0)


def attn_grad_kernel(blocks, keep, meta, dqkv, xt, *refs):
    tables, (out, *refs) = refs[: 2 * blocks], refs[2 * blocks :]
    if not keep:
        mark, *refs = refs
        mark[...] = jnp.zeros_like(mark)
    width = xt.shape[0]
    half = 3 * width // 2
    part = half // 3
    core = meta[2] if keep else 1 - meta[2]
    for t in range(3):
        cols = pl.ds(pl.multiple_of(core * half + t * part, 128), part)
        value = dot_nn(xt[...], dqkv[:, cols])
        store_parts(out, slice(t * part, (t + 1) * part), value, meta, core)
    if blocks:
        small = refs[0]
        small[...] = jnp.zeros_like(small)
        for b in range(blocks):
            small[b * SLOT : (b + 1) * SLOT, :] = tables[2 * b][...]
            small[b * SLOT + SHIFT + 2 : b * SLOT + SHIFT + 3, :] = tables[2 * b + 1][...]
        extra = small[...].T * (core == 0).astype(f32)
        store_parts(out, slice(half, half + LANES), extra, meta, core)


def unproject_kernel(relative, meta, dqkv, dr1, weight, *refs):
    outs, dx = refs[:-1], refs[-1]
    tokens, width = dr1.shape
    target = dx if relative else outs[0]
    for n in range(width // GROUP):
        cols = slice(n * GROUP, (n + 1) * GROUP)
        target[:, cols] = dr1[:, cols] + dot_nt(dqkv[...], weight[cols, :])
    for k in range(relative):
        part = tokens // relative
        first = pl.multiple_of((k ^ meta[0]) * part, part)
        outs[k][0] = dx[pl.ds(first, part), :].astype(bf16)


def prepare_kernel(ends, meta, *refs):
    fars, (own, other, *refs) = refs[:7], refs[7:]
    *x_parts, table, inputs, attn, out, point, depth, gains, shifts, sems = refs
    nears = (inputs, attn, out, point, depth, gains, shifts)
    copies = [
        pltpu.make_async_copy(fars[n].at[m], nears[n].at[m], sems.at[n])
        for n in range(4)
        for m in range(nears[n].shape[0])
    ]
    copies += [pltpu.make_async_copy(fars[n], nears[n], sems.at[n]) for n in range(4, 7)]
    for copy in copies:
        copy.start()
    seq_count, blocks = inputs.shape[0], attn.shape[0]
    rows, half, cut = attn.shape[1], attn.shape[2] // 2, out.shape[2] // 2
    table[...] = jnp.zeros_like(table)
    for copy in copies:
        copy.wait()
    for b in range(blocks):
        start = b * SLOT
        for j in range(depth.shape[0]):
            table[start + j : start + j + 1, :rows] = depth[j, b : b + 1, :]
        table[start + GAIN : start + SHIFT, :rows] = gains[b]
        for j in range(shifts.shape[0]):
            at = start + SHIFT + j
            table[at : at + 1, :rows] = shifts[j, b : b + 1, :]
    small = table[...].T[:rows]
    for k, part in enumerate(x_parts):
        part[...] = inputs[jnp.minimum(meta[0] ^ k, seq_count - 1)]
    for to, core in ((own, meta[2]), (other, 1 - meta[2])):
        wide = pl.ds(pl.multiple_of(core * half, 128), half)
        narrow = pl.ds(pl.multiple_of(core * cut, 128), cut)
        to[:, half : half + LANES] = (small * (core == 0).astype(f32)).astype(bf16)
        for b in range(blocks):
            start = 0 if b == 0 else ends[2 * b - 1]
            to[:, start : start + half] = attn[b, :, wide].astype(bf16)
            start = ends[2 * b]
            to[:, start : start + cut] = out[b, :, narrow].astype(bf16)
            to[:, start + cut : start + 2 * cut] = point[b, :, narrow].astype(bf16)


def pair_kernel(meta, own, given, *refs):
    outs, (rows_ref,) = refs[:-1], refs[-1:]
    rows = own.shape[0]
    mine, theirs = own[...].astype(f32), given[...].astype(f32)
    rows_ref[0:rows, :] = jnp.where(meta[2] == 0, mine, theirs)
    rows_ref[rows : 2 * rows, :] = jnp.where(meta[2] == 0, theirs, mine)
    start = 0
    for out in outs:
        stop = start + out.shape[-1]
        out[0] = rows_ref[:, start:stop].astype(bf16)
        start = stop


def end_kernel(meta, kept, got, own, other, rows_ref):
    rows = own.shape[0]
    rows_ref[...] = kept[0].astype(f32) + got[0].astype(f32)
    first, second = rows_ref[0:rows, :], rows_ref[rows : 2 * rows, :]
    own[...] = jnp.where(meta[2] == 0, first, second)
    other[...] = jnp.where(meta[2] == 0, second, first).astype(bf16)


def settle_kernel(seqs, meta, *refs):
    *parts, out, mark, all_parts = refs
    mark[...] = jnp.zeros_like(mark)
    at = 0
    for part in parts:
        for n in range(part.shape[0]):
            all_parts[at] = part[n]
            at += 1
    for i in range(out.shape[0]):
        out[i] = all_parts[i ^ meta[0]].astype(out.dtype)


def adam_update(master, first, second, gradient, step_rate):
    first_new = beta_first * first + (1.0 - beta_first) * gradient
    second_new = beta_second * second + (1.0 - beta_second) * gradient * gradient
    first_hat = first_new / (1.0 - beta_first**STEP)
    second_hat = second_new / (1.0 - beta_second**STEP)
    updated = master - step_rate * (
        first_hat / (jnp.sqrt(second_hat) + adam_eps) + weight_decay * master
    )
    return (updated, first_new, second_new, updated.astype(jnp.bfloat16))


def adam_kernel(places, rates, smalls, meta, *refs):
    count = 2 * (1 + max(index for spots in places for index, _ in spots))
    grads, refs = refs[:count], refs[count:]
    arrays = len(places) + len(smalls)
    states = [refs[3 * n : 3 * n + 3] for n in range(arrays)]
    outs = [refs[3 * arrays + 4 * n : 3 * arrays + 4 * n + 4] for n in range(arrays)]
    *marks, table = refs[7 * arrays :]
    for mark in marks:
        mark[...] = jnp.zeros_like(mark)

    def pick(index, half, lanes):
        own, given = grads[2 * index][:, lanes], grads[2 * index + 1][:, lanes].astype(f32)
        return jnp.where(meta[2] == half, own, given)

    for spots, state, out, rate in zip(places, states, outs, rates):
        width = state[0].shape[2] // 2
        for b, (index, start) in enumerate(spots):
            for half in range(2):
                cols = slice(half * width, (half + 1) * width)
                gradient = pick(index, half, slice(start, start + width))
                values = adam_update(*[ref[b, :, cols] for ref in state], gradient, rate)
                for ref, value in zip(out, values):
                    ref[b, :, cols] = value
    if smalls:
        index, start = places[0][0]
        start += states[0][0].shape[2] // 2
        rows = grads[2 * index].shape[0]
        table[...] = jnp.zeros_like(table)
        table[:rows, :] = pick(index, 0, slice(start, start + LANES))
        sums = table[...].T
        for n, (row, rows_first, rate) in enumerate(smalls):
            state, out = states[len(places) + n], outs[len(places) + n]
            for i in range(state[0].shape[0]):
                if rows_first:
                    parts = [sums[b * SLOT + row + i :][:1] for b in range(state[0].shape[1])]
                    gradient = jnp.concatenate(parts)[:, :rows]
                else:
                    first = i * SLOT + row
                    gradient = sums[first : first + state[0].shape[1], :rows]
                values = adam_update(*[ref[i] for ref in state], gradient, rate)
                for ref, value in zip(out, values):
                    ref[i] = value


class Links:
    def __init__(self, seqs, copies):
        self.seqs, self.copies, self.ring = seqs, copies, copies // 2
        self.s = lax.axis_index("seq")
        position = lax.axis_index("dp")
        self.z, self.c = position // 2, position % 2

    def swap(self, array, seq=0, ring=0, core=0):
        pairs = [
            (s * self.copies + d, (s ^ seq) * self.copies + (d ^ (2 * ring + core)))
            for s in range(self.seqs)
            for d in range(self.copies)
        ]
        return lax.ppermute(array, AXES, pairs)

    def hop(self, array, axis, step):
        count = self.seqs if axis == "seq" else self.ring
        last = count.bit_length() - 2
        pairs = []
        for s in range(self.seqs):
            for d in range(self.copies):
                bit = 1 << (step if d % 2 == 0 else last - step)
                to_s, to_d = (s ^ bit, d) if axis == "seq" else (s, d ^ (2 * bit))
                pairs.append((s * self.copies + d, to_s * self.copies + to_d))
        return lax.ppermute(array, AXES, pairs)

    def steps(self, axis):
        return range((self.seqs if axis == "seq" else self.ring).bit_length() - 1)

    def place(self, m):
        return self.z ^ jnp.where(self.c == 0, m, flipped(m, self.ring))

    def around(self, block, axis, start=0, stop=None):
        for step in self.steps(axis)[start:stop]:
            block = join([block, self.hop(block, axis, step)])
        return block

    def ring_block(self, block):
        _, rows, half = block.shape
        if rows % 16 == 0:
            return block
        placed = jnp.zeros_like(block)
        for m in range(self.ring):
            placed = lax.dynamic_update_slice(
                placed, block[m : m + 1], (self.place(m), jnp.int32(0), jnp.int32(0))
            )
        return placed.reshape(1, self.ring * rows, half)

    def both_cores(self, blocks):
        return blocks + [self.swap(one, core=1) for one in blocks]

    def finish(self, block, axis):
        return self.both_cores([block, self.hop(block, axis, self.steps(axis)[-1])])

    def ring_terms(self, terms):
        terms = [term[0] for term in terms]
        if terms[0].shape[0] > 1:
            return terms
        total = terms[0][0].astype(f32)
        for term in terms[1:]:
            total = total + term[0].astype(f32)
        total = total.reshape(self.ring, total.shape[0] // self.ring, total.shape[1])
        units = []
        for m in range(self.ring):
            at = self.z ^ jnp.where(self.c == 0, flipped(m, self.ring), m)
            units.append(lax.dynamic_index_in_dim(total, at, 0, keepdims=False))
        return [jnp.stack(units).astype(bf16)]


def shards(
    inputs,
    masked_positions,
    masked_grads,
    kernel_paths,
    attn_weight,
    out_weight,
    point_weight,
    depth_weight,
    gains,
    shifts,
    first_attn,
    first_out,
    first_point,
    first_depth,
    first_gains,
    first_shifts,
    second_attn,
    second_out,
    second_point,
    second_depth,
    second_gains,
    second_shifts,
):
    seq_count, part_tokens, width = inputs.shape
    seqs, copies = lax.axis_size("seq"), lax.axis_size("dp")
    devices = seqs * copies
    tokens = seqs * part_tokens
    blocks, rows, _ = attn_weight.shape
    taps = depth_weight.shape[1]
    scale = (width // HEADS) ** (-0.5)
    links = Links(seqs, copies)
    aligned = (2 * rows) % 16 == 0
    subs = links.ring if aligned else 1
    part_rows = width // (seqs * subs)
    half = 3 * width // 2
    place = links.s
    mine = jnp.minimum(place, seq_count - 1)
    live = (place < seq_count).astype(jnp.int32)
    own_paths = lax.dynamic_index_in_dim(kernel_paths, mine, 0, keepdims=False)
    meta = jnp.concatenate(
        [
            jnp.stack([place, links.z if subs > 1 else jnp.zeros_like(links.z), links.c]),
            own_paths,
            live[None],
        ]
    ).astype(jnp.int32)
    full, meta = meta, Position(aligned)
    cut = width // 2
    ends = [half + LANES, half + LANES + width]
    ends += [ends[1] + half, ends[1] + half + width]

    def shape(*dims, dtype=f32):
        return jax.ShapeDtypeStruct(dims, dtype)

    dma = pltpu.SemaphoreType.DMA
    square = (width, width)
    wide = (width, 3 * width)

    def attend(b, parts, pieces, table, after=()):
        near = b == blocks - 1
        outs = (
            Stored(wide, bf16),
            Stored((width, tokens), bf16),
            Stored((tokens, 3 * width), bf16),
            shape(tokens, width, dtype=bf16),
            shape(width, tokens, dtype=bf16) if near else Stored((width, tokens), bf16),
            Stored((LANES, tokens), f32),
        )
        scratch = [
            pltpu.VMEM(wide, bf16),
            pltpu.VMEM((width, tokens), bf16),
            pltpu.VMEM((tokens, 3 * width), bf16),
            pltpu.VMEM((LANES, tokens), f32),
            dma((7,)),
        ]
        if not near:
            scratch = [pltpu.VMEM((width, tokens), bf16)] + scratch
        if b == 0:
            outs = (shape(blocks * SLOT, width), shape(tokens, width, dtype=bf16)) + outs
            scratch += [pltpu.VMEM((2, width, LANES), bf16)]
        return call(
            partial(attend_kernel, b, near, len(parts), scale),
            outs,
            [smem_spec()] + [vmem_spec()] * ((1 if b else 0) + len(parts) + len(pieces)),
            [full] + ([table] if b else []) + list(parts) + list(pieces),
            scratch,
            11 * 10**9,
            f"attend_{b}",
            after,
        )

    def mix(b, table, x, o, pieces, after=()):
        final = b == blocks - 1
        kept = (
            ((tokens, width), f32),
            ((tokens, width), f32),
            ((width, tokens), bf16),
            ((tokens, LANES), f32),
            (square, bf16),
            (square, bf16),
        )
        if final:
            outs = (shape(1, part_tokens, width, dtype=bf16),) * seqs
            outs += tuple(jax.ShapeDtypeStruct(*one) for one in kept)
        else:
            outs = (shape(tokens, width), shape(tokens, width, dtype=bf16))
            outs += tuple(Stored(*one) for one in kept)
        return call(
            partial(
                mix_kernel, b, len(pieces), final and aligned, taps, final, seqs if final else 0
            ),
            outs,
            [smem_spec()] + [vmem_spec()] * (3 + len(pieces)),
            [full, table, x, o, *pieces],
            ([] if final else [pltpu.VMEM(*one) for one in kept])
            + [
                pltpu.VMEM((tokens, width), f32),
                pltpu.VMEM((tokens, width), f32),
                pltpu.VMEM((tokens + 2 * PAD, width), f32),
                pltpu.VMEM((tokens, width), bf16),
                dma((10,)),
            ],
            10**9,
            f"mix_{b}",
            after,
        )

    def unmix(b, table, upstream, saved, after=(), fetch=()):
        last = b == blocks - 1
        parts = shape(seqs, subs, part_rows, width, dtype=bf16)
        return call(
            partial(unmix_kernel, b, taps, last),
            (
                shape(tokens, width),
                shape(tokens, width, dtype=bf16),
                shape(SLOT, width),
                shape(SLOT, tokens),
                parts,
                parts,
            ),
            [smem_spec()] + [vmem_spec()] * (len(upstream) + 1 + len(saved)),
            [full, table, *upstream, *saved],
            [
                pltpu.VMEM((tokens, width), f32),
                pltpu.VMEM((tokens, width), bf16),
                pltpu.VMEM((tokens + 2 * PAD, width), f32),
                pltpu.VMEM((tokens + 2 * PAD, width), f32),
            ],
            10 * 10**9,
            f"unmix_{b}",
            after,
            fetch,
        )

    def unattend(b, qkv, do, lse, inner, after=(), fetch=()):
        return call(
            partial(unattend_kernel, scale),
            (shape(tokens, 3 * width, dtype=bf16), shape(1, width)),
            [smem_spec()] + [vmem_spec()] * 4,
            [meta, qkv, do, lse, inner],
            [],
            11 * 10**9,
            f"unattend_{b}",
            after,
            fetch,
        )

    def attn_grad(b, keep, dqkv, xt, tables, after=()):
        span = half + (0 if b else LANES)
        return call(
            partial(attn_grad_kernel, len(tables) // 2, keep),
            (shape(seqs, subs, part_rows, span, dtype=bf16),) + (() if keep else (TOKEN,)),
            [smem_spec()] + [vmem_spec()] * (2 + len(tables)),
            [meta, dqkv, xt, *tables],
            [pltpu.VMEM((LANES, width), f32)] if tables else [],
            10**8,
            f"attn_grad_{b}",
            after,
        )

    def unproject(b, dqkv, dr1, weight, after=(), fetch=()):
        return call(
            partial(unproject_kernel, 0 if b else seqs),
            (shape(tokens, width),) if b else (shape(1, part_tokens, width, dtype=bf16),) * seqs,
            [smem_spec()] + [vmem_spec()] * 3,
            [meta, dqkv, dr1, weight],
            [pltpu.VMEM((tokens, width), f32)],
            4 * 10**9,
            f"unproject_{b}",
            after,
            fetch,
        )

    def settle(parts, dtype, after=()):
        return call(
            partial(settle_kernel, seqs),
            (shape(seq_count, part_tokens, width, dtype=dtype), TOKEN),
            [smem_spec()] + [vmem_spec()] * len(parts),
            [meta, *parts],
            [pltpu.VMEM((seqs, part_tokens, width), bf16)],
            10**8,
            "settle",
            after,
        )

    def end(kept, got, after=()):
        span = kept.shape[-1]
        own, other = call(
            end_kernel,
            (shape(rows, span), shape(rows, span, dtype=bf16)),
            [smem_spec(), vmem_spec(), vmem_spec()],
            [meta, kept, got],
            [pltpu.VMEM((2 * rows, span), f32)],
            10**8,
            "end",
            after,
        )
        return own, links.swap(other, core=1)

    def adam(places, rates, smalls, grads, states, fetch=()):
        outs = []
        for state in states:
            outs += [shape(*state[0].shape)] * 3 + [shape(*state[0].shape, dtype=bf16)]
        flat = [array for state in states for array in state]
        results = call(
            partial(adam_kernel, places, rates, smalls),
            (*outs, TOKEN) if fetch else outs,
            [smem_spec()] + [vmem_spec()] * (len(grads) + len(flat)),
            [meta, *grads, *flat],
            [pltpu.VMEM((LANES, LANES), f32)],
            10**8,
            "adam",
            (),
            fetch,
        )
        results, near = results if fetch else (results, ())
        return [results[4 * n : 4 * n + 4] for n in range(len(states))], results[-1], near

    depth_rows = [jnp.swapaxes(a, 0, 1) for a in (depth_weight, first_depth, second_depth)]
    shift_rows = [jnp.swapaxes(a, 0, 1) for a in (shifts, first_shifts, second_shifts)]
    own, other, *x_parts = call(
        partial(prepare_kernel, ends),
        (shape(rows, ends[3], dtype=bf16),) * 2
        + (shape(part_tokens, width, dtype=bf16),) * seqs,
        [smem_spec()] + [hbm_spec()] * 7,
        [meta, inputs, attn_weight, out_weight, point_weight, depth_rows[0], gains, shift_rows[0]],
        [pltpu.VMEM((LANES, LANES), f32)]
        + [
            pltpu.VMEM(array.shape, array.dtype)
            for array in (inputs, attn_weight, out_weight, point_weight)
            + (depth_rows[0], gains, shift_rows[0])
        ]
        + [dma((7,))],
        10**8,
        "prepare",
    )
    given = links.swap(other, core=1)
    widths = (ends[0], ends[2] - ends[0], width)
    unit_a0, unit_mid, unit_m1 = call(
        pair_kernel,
        tuple(shape(1, 2 * rows, span, dtype=bf16) for span in widths),
        [smem_spec(), vmem_spec(), vmem_spec()],
        [meta, own, given],
        [pltpu.VMEM((2 * rows, ends[3]), f32)],
        10**8,
        "pair",
    )
    x_parts = [x_parts[0]] + [links.swap(x_parts[k], seq=k) for k in range(1, seqs)]
    last_seq, last_ring = links.steps("seq")[-1], links.steps("ring")[-1]
    block_a0 = links.around(unit_a0, "ring", stop=-1)
    got_a0 = links.hop(block_a0, "ring", last_ring)
    plane_m1, marks = unit_m1, [*x_parts[1:]]
    if aligned:
        plane_m1, done = join_mark([unit_m1, links.hop(unit_m1, "seq", 0)])
        marks.append(done)
    ring_a0, done = join_mark([block_a0, got_a0], after=marks)
    ring_a0 = links.ring_block(ring_a0)
    got_a0 = links.hop(ring_a0[None], "seq", 0)
    unit_mid = join([unit_mid], after=(done,))
    got_mid = links.hop(unit_mid, "ring", 0)
    part_mid, done = join_mark([unit_mid, got_mid])
    marks = [done]
    if aligned:
        plane_m1, done = join_mark([plane_m1, links.hop(plane_m1, "seq", last_seq)])
        marks.append(done)
    plane_a0 = join([ring_a0[None], got_a0], after=marks)
    pieces_a0 = links.finish(plane_a0, "seq")
    ring_mid = links.ring_block(links.around(part_mid, "ring", 1))
    ring_m0, ring_a1 = ring_mid[..., :width], ring_mid[..., width:]
    got_m0 = [links.swap(ring_m0[None], seq=k) for k in range(1, seqs)]
    got_a1 = links.hop(ring_a1[None], "seq", 0)
    if aligned:
        got_m1 = links.hop(plane_m1[None], "ring", 0)
    table, x16, w_0, xt_0, qkv_0, o_0, ot_0, lse_0 = attend(
        0, x_parts, pieces_a0, None, after=(ring_m0, ring_a1)
    )
    marks = [table]
    if aligned:
        plane_m1, done = join_mark([plane_m1[None], got_m1], after=marks)
        marks.append(done)
    plane_a1, done = join_mark([ring_a1[None], got_a1], after=marks)
    got_m0, done = join_mark(got_m0, after=(done,))
    pieces_m0 = links.both_cores([ring_m0[None], got_m0])
    parts = [[links.hop(plane_a1, "seq", last_seq)]]
    if aligned:
        parts.append([links.hop(plane_m1, "ring", last_ring)])
    y_0, x_1, *saved_0 = mix(0, table, x16, o_0, pieces_m0, after=(done,))
    got_a1, *got_m1 = joins(parts, after=(x_1,))
    pieces_a1 = links.both_cores([plane_a1, got_a1])
    w_1, xt_1, qkv_1, o_1, ot_1, lse_1 = attend(1, [x_1], pieces_a1, table)
    if aligned:
        pieces_m1 = links.both_cores([plane_m1, *got_m1])
    else:
        ring_m1 = links.ring_block(links.around(unit_m1, "ring"))
        pieces_m1 = links.finish(links.around(ring_m1[None], "seq", stop=-1), "seq")
    outs_1 = mix(1, table, y_0, o_1, pieces_m1)
    y_1, saved_1 = outs_1[:seqs], outs_1[seqs:]

    y_back = [links.swap(y_1[k], seq=k) for k in range(1, seqs)]
    places = masked_positions[:, None, :]
    (dr1, do, sums_1, inner, keep, send), near = unmix(
        1, table, (places, masked_grads), (*saved_1, ot_1), fetch=(qkv_1, lse_1)
    )
    y_back, done = join_mark(y_back, after=(sums_1,))
    given_m1 = links.swap(send, core=1)
    terms_m1 = [keep, given_m1]
    (dqkv, bias_1), (xt, weight) = unattend(
        1, near[0], do, near[1], inner, after=(done,), fetch=(xt_1, w_1)
    )
    send, done = attn_grad(1, False, dqkv, xt, ())
    given_a1 = links.swap(send, core=1)
    (keep,) = attn_grad(1, True, dqkv, xt, (), after=(done,))
    late, sent, done = fold([terms_m1, [keep, given_a1]])
    got = links.hop(sent, "seq", 0)
    (dy,), near = unproject(1, dqkv, dr1, weight, after=(done,), fetch=(*saved_0, ot_0))
    (dr1, do, sums_0, inner, keep, send), near = unmix(0, table, (dy,), near, fetch=(qkv_0, lse_0))
    late, sent, done = fold([[late, got]], after=(sums_0,))
    got = links.hop(sent, "seq", 1)
    mixed, sent, done_mixed = fold([[keep, links.swap(send, core=1)]], after=(done,))
    got_mixed = links.hop(sent, "seq", 0)
    (dqkv, bias_0), (xt, weight) = unattend(
        0, near[0], do, near[1], inner, after=(done, done_mixed), fetch=(xt_0, w_0)
    )
    mixed, sent, done_mixed = fold([[mixed, got_mixed]], after=(bias_0,))
    got_mixed = links.hop(sent, "seq", 1)
    late, sent, done = fold([links.ring_terms([late, got])], after=(bias_0,))
    got = links.hop(sent, "ring", 0)
    tables = (sums_0, bias_0, sums_1, bias_1)
    send, done = attn_grad(0, False, dqkv, xt, tables, after=(done, done_mixed))
    given = links.swap(send, core=1)
    (keep,) = attn_grad(0, True, dqkv, xt, tables, after=(done,))
    final, sent, done = fold([[keep, given]], after=(touch(got_mixed),))
    got_final = links.hop(sent, "seq", 0)
    dx = unproject(0, dqkv, dr1, weight, after=(done, touch(got)))
    for step in links.steps("ring")[1:]:
        late, sent, done = fold([[late, got]], after=(dx[0],))
        got = links.hop(sent, "ring", step)
    mixed, sent, done_mixed = fold([links.ring_terms([mixed, got_mixed])], after=(dx[0], done))
    got_mixed = links.hop(sent, "ring", 0)
    final, sent, done = fold([[final, got_final]], after=(done_mixed,))
    got_final = links.hop(sent, "seq", 1)
    for step in links.steps("ring")[1:]:
        mixed, sent, done_mixed = fold([[mixed, got_mixed]], after=(done,))
        got_mixed = links.hop(sent, "ring", step)
    result, done_y = settle([y_1[0], y_back], bf16)
    final, sent, done = fold(
        [links.ring_terms([final, got_final])], after=(done_mixed, touch(got), done_y)
    )
    got_final = links.hop(sent, "ring", 0)
    dx_sent = joins([[one] for one in dx[1:]], after=(done,))
    x_back = [links.swap(dx_sent[k - 1], seq=k) for k in range(1, seqs)]
    for step in links.steps("ring")[1:]:
        final, sent = fold([[final, got_final]], after=(touch(got_mixed),), mark=False)
        got_final = links.hop(sent, "ring", step)
    x_back = join(x_back)
    input_grad, done_x = settle([dx[0], x_back], f32)
    grads = end(late, got) + end(mixed, got_mixed)
    (new_out, new_point), done_mix, states = adam(
        (((1, 0), (0, 0)), ((1, cut), (0, cut))),
        (rate_out, rate_point),
        (),
        grads,
        (
            (out_weight, first_out, second_out),
            (point_weight, first_point, second_point),
        ),
        fetch=(attn_weight, first_attn, second_attn),
    )
    (new_attn, new_depth, new_gains, new_shifts), _, _ = adam(
        (((0, 0), (1, width)),),
        (rate_attn,),
        ((0, True, rate_depth), (GAIN, False, rate_gain), (SHIFT, True, rate_vector)),
        end(final, got_final, (done_x, done_mix)) + grads[:2],
        (states, depth_rows, (gains, first_gains, second_gains), shift_rows),
    )
    new_depth, new_shifts = (
        [jnp.swapaxes(a, 0, 1) for a in new] for new in (new_depth, new_shifts)
    )
    updates = (new_attn, new_out, new_point, new_depth, new_gains, new_shifts)
    return (
        (result, input_grad)
        + tuple((entry[0] for entry in updates))
        + tuple((entry[1] for entry in updates))
        + tuple((entry[2] for entry in updates))
        + tuple((entry[3] for entry in updates))
    )


def solution(mesh):
    sequence = P("dp", "seq", None)
    matrix = P(None, AXES, None)
    vector = P(None, None, AXES)
    weights = (matrix,) * 3 + (vector,) * 3
    return jax.shard_map(
        shards,
        mesh=mesh,
        in_specs=(sequence, P("dp", None), P("dp", None, None), P("dp", None)) + weights * 3,
        out_specs=(sequence, sequence) + weights * 4,
        check_vma=False,
    )
```

```python
from functools import partial

import jax
import jax.numpy as jnp
from jax import lax
from jax.experimental import pallas as pl
from jax.experimental.pallas import tpu as pltpu
from jax.sharding import PartitionSpec as P

HEADS = 12
STEP = 10

norm_eps = 1e-05
beta_first = 0.5
beta_second = 0.5
adam_eps = 1e-08
weight_decay = 0.01
rate_attn = 0.03
rate_out = 0.25
rate_point = 0.03
rate_depth = 0.3
rate_gain = 0.45
rate_vector = 0.2

f32 = jnp.float32
bf16 = jnp.bfloat16
AXES = ("seq", "dp")
VMEM_BYTES = 24 * 2**20
GROUP = 256
ROWS = 64
PAD = 8

GAIN = 7
SHIFT = 9
SMALL = 14
SLOT = 16
LANES = 128


def dot_nn(a, b):
    return lax.dot_general(a, b, (((1,), (0,)), ((), ())), preferred_element_type=f32)


def dot_nt(a, b):
    return lax.dot_general(a, b, (((1,), (1,)), ((), ())), preferred_element_type=f32)


def dot_tn(a, b):
    return lax.dot_general(a, b, (((0,), (0,)), ((), ())), preferred_element_type=f32)


def vmem_spec():
    return pl.BlockSpec(memory_space=pltpu.VMEM)


def smem_spec():
    return pl.BlockSpec(memory_space=pltpu.SMEM)


def any_spec():
    return pl.BlockSpec(memory_space=pl.ANY)


def hbm_spec():
    return pl.BlockSpec(memory_space=pltpu.HBM)


class Stored(jax.ShapeDtypeStruct):
    pass


class Position:
    def __init__(self, ring):
        self.ring = ring

    def read(self):
        place = lax.axis_index("dp")
        ring = place // 2 if self.ring else jnp.zeros_like(place)
        return [lax.axis_index("seq"), ring, place % 2]


def call(body, outs, in_specs, args, scratch, cost, name, after=(), fetch=()):
    position = args[0] if isinstance(args[0], Position) else None
    if position:
        in_specs, args = in_specs[1:], args[1:]
    n_in, n_after, n_out, n_fetch = len(in_specs), len(after), len(outs), len(fetch)

    def kernel(*refs):
        first = n_in + n_after
        far, refs = refs[first : first + n_fetch], refs[:n_in] + refs[first + n_fetch :]
        near = refs[n_in + n_out : n_in + n_out + n_fetch]
        refs = refs[: n_in + n_out] + refs[n_in + n_out + n_fetch :]
        copies = []
        if n_fetch:
            for n in range(n_fetch):
                count = 4 if far[n].shape[0] % 64 == 0 else 1
                copies += chunk_copies(far[n], near[n], refs[-1].at[n], count)
            refs = refs[:-1]
        for copy in copies:
            copy.start()
        body(*([position.read()] if position else []), *refs)
        for copy in copies:
            copy.wait()

    args = [
        pltpu.with_memory_space_constraint(arg, pltpu.HBM)
        if spec.memory_space == pltpu.HBM
        else arg
        for arg, spec in zip(args, in_specs, strict=True)
    ]
    fetch = [pltpu.with_memory_space_constraint(arg, pltpu.HBM) for arg in fetch]
    results = pl.pallas_call(
        kernel,
        out_shape=tuple(
            pltpu.HBM(out.shape, out.dtype) if isinstance(out, Stored) else out for out in outs
        )
        + tuple(jax.ShapeDtypeStruct(a.shape, a.dtype) for a in fetch),
        in_specs=list(in_specs) + [vmem_spec()] * n_after + [hbm_spec()] * n_fetch,
        out_specs=tuple(hbm_spec() if isinstance(out, Stored) else vmem_spec() for out in outs)
        + (vmem_spec(),) * n_fetch,
        scratch_shapes=list(scratch) + ([pltpu.SemaphoreType.DMA((n_fetch,))] if fetch else []),
        compiler_params=pltpu.CompilerParams(vmem_limit_bytes=VMEM_BYTES),
        cost_estimate=pl.CostEstimate(flops=cost, bytes_accessed=2**18, transcendentals=0),
        name=name,
    )(*args, *after, *fetch)
    return (results[:n_out], results[n_out:]) if n_fetch else results


TOKEN = jax.ShapeDtypeStruct((8, 128), f32)


def small_call(body, outs, args, name, after=(), scratch=()):
    specs = [vmem_spec()] * len(args)
    return call(body, outs, specs, args, list(scratch), 10**8, name, after)


def joins(groups, after=(), mark=False):
    def kernel(*refs):
        used = 0
        for group, out in zip(groups, refs[sum(map(len, groups)) :]):
            start = 0
            for part in refs[used : used + len(group)]:
                count = part.shape[0]
                out[start : start + count] = part[...]
                start += count
            used += len(group)
        if mark:
            refs[-1][...] = jnp.zeros_like(refs[-1])

    outs = [
        jax.ShapeDtypeStruct((sum(p.shape[0] for p in group),) + group[0].shape[1:], group[0].dtype)
        for group in groups
    ]
    parts = [part for group in groups for part in group]
    return small_call(kernel, (*outs, TOKEN) if mark else outs, parts, "join", after)


def join(parts, after=()):
    return joins([parts], after)[0]


def join_mark(parts, after=()):
    return joins([parts], after, True)


def fold(groups, after=(), mark=True):
    terms = [term for group in groups for term in group]
    widths = [group[0].shape[-1] for group in groups]
    lead = terms[0].shape[:-2]
    rows, half = terms[0].shape[-2], lead[0] // 2

    def kernel(*refs):
        ins, (kept, sent, *marks) = refs[: len(terms)], refs[len(terms) :]

        def block(out, to, at):
            start, used = 0, 0
            for group, width in zip(groups, widths, strict=True):
                total = ins[used][at].astype(f32)
                for term in ins[used + 1 : used + len(group)]:
                    total = total + term[at].astype(f32)
                out[(*to, slice(None), slice(start, start + width))] = total.astype(bf16)
                start, used = start + width, used + len(group)

        for n in range(half):
            if len(lead) == 1:
                block(kept, (n,), (n,))
                block(sent, (n,), (half + n,))
            else:

                def step(m, carry, n=n):
                    block(kept, (n, m), (n, m))
                    block(sent, (n, m), (half + n, m))
                    return carry

                lax.fori_loop(0, lead[1], step, 0)
        for one in marks:
            one[...] = jnp.zeros_like(one)

    out = jax.ShapeDtypeStruct((half,) + lead[1:] + (rows, sum(widths)), bf16)
    return small_call(kernel, (out, out, TOKEN) if mark else (out, out), terms, "fold", after)


def touch(*arrays):
    def kernel(*refs):
        refs[-1][...] = jnp.zeros_like(refs[-1])

    return small_call(kernel, (TOKEN,), arrays, "touch")[0]


def chunk_copies(source, dest, sem, count=4):
    rows = source.shape[0] // count
    return [
        pltpu.make_async_copy(
            source.at[pl.ds(n * rows, rows)], dest.at[pl.ds(n * rows, rows)], sem
        )
        for n in range(count)
    ]


def group_loop(width, body):
    def step(g, carry):
        first = pl.multiple_of(g * GROUP, GROUP)
        return body(g, [pl.ds(part * width + first, GROUP) for part in range(3)], carry)

    return partial(lax.fori_loop, 0, width // GROUP, step)


def strip_loop(width, body):
    def step(n, carry):
        body(pl.ds(pl.multiple_of(n * LANES, LANES), LANES))
        return carry

    lax.fori_loop(0, width // LANES, step, 0)


def row_loop(total, body, rows=ROWS):
    def step(i, carry):
        body(pl.multiple_of(i * rows, rows))
        return carry

    lax.fori_loop(0, total // rows, step, 0, unroll=True)


def flipped(index, count):
    bits, out = count.bit_length() - 1, 0
    for bit in range(bits):
        out = out | (((index >> bit) & 1) << (bits - 1 - bit))
    return out


def weight_copies(meta, pieces, dest, sem, first, half, ring_last=False, whole=False):
    s, z, c = meta[0], meta[1], meta[2]
    copies, first_late = [], pieces[0].shape[0]
    late_count = first_late + pieces[1].shape[0]
    for n, piece in enumerate(pieces):
        late, early, rows, width = piece.shape
        core = (n // 2) ^ c
        for a in range(late):
            for b in range(early):
                outer, inner = (n % 2) * first_late + a, b
                if 2 * first_late == late_count:
                    outer = jnp.where(core == 0, outer, flipped(outer, late_count))
                inner = jnp.where(core == 0, inner, flipped(inner, early))
                if ring_last:
                    row = ((inner ^ s) * late_count + (outer ^ z)) * rows
                else:
                    row = ((outer ^ s) * early + (inner ^ z)) * rows
                row = pl.multiple_of(row, rows)
                source = piece.at[a, b]
                if (first, half) != (0, width):
                    source = piece.at[a, b, :, pl.ds(first, half)]
                if whole:
                    target = dest.at[core, pl.ds(row, rows)]
                else:
                    col = pl.multiple_of(core * half, 128)
                    target = dest.at[pl.ds(row, rows), pl.ds(col, half)]
                copies.append(pltpu.make_async_copy(source, target, sem))
    return copies


def head_masks(scale):
    lane = lax.broadcasted_iota(jnp.int32, (1, GROUP), 1) // (GROUP // 4)
    return [jnp.where(lane == h, f32(scale), f32(0)).astype(bf16) for h in range(4)]


def attend_kernel(block, near, x_parts, scale, meta, *refs):
    if block:
        table, refs = refs[0], refs[1:]
    x_refs, pieces = refs[:x_parts], refs[x_parts : x_parts + 4]
    refs = refs[x_parts + 4 :]
    if block == 0:
        table, x, refs = refs[0], refs[1], refs[2:]
    w_far, xt_far, qkv_far, o_out, ot_far, lse_far, *refs = refs
    if near:
        ot = ot_far
    else:
        ot, refs = refs[0], refs[1:]
    weight, xt, qkv, lse, sems = refs[:5]
    half = weight.shape[1] // 2
    if block == 0:
        (extra,) = refs[5:]
        smalls = weight_copies(meta, pieces, extra, sems.at[0], half, LANES, whole=True)
        for copy in smalls:
            copy.start()
        part_rows = x_refs[0].shape[0]
        x_copies = [
            pltpu.make_async_copy(
                x_refs[k],
                x.at[pl.ds(pl.multiple_of((k ^ meta[0]) * part_rows, part_rows), part_rows)],
                sems.at[1],
            )
            for k in range(x_parts)
        ]
        for copy in x_copies:
            copy.start()
    else:
        x = x_refs[0]
    copies = weight_copies(meta, pieces, weight, sems.at[2], 0, half)
    for copy in copies:
        copy.start()
    if block == 0:
        for copy in x_copies:
            copy.wait()
        for copy in smalls:
            copy.wait()
        table[...] = extra[0].astype(f32).T[: table.shape[0]]
        for b in range(table.shape[0] // SLOT):
            for reach in (2, 3):
                row = b * SLOT + SMALL + reach - 2
                on = jnp.where(meta[3 + b] + 1 >= reach, f32(1), f32(0))
                table[row : row + 1, :] = jnp.zeros((1, table.shape[1]), f32) + on
    small = table.at[pl.ds(SLOT * block, SLOT)]
    xt[...] = x[...].T
    xt_store = pltpu.make_async_copy(xt, xt_far, sems.at[3])
    xt_store.start()
    for copy in copies:
        copy.wait()
    w_stores = chunk_copies(weight, w_far, sems.at[2])
    for copy in w_stores:
        copy.start()
    tokens, width = x.shape
    scaled, plain = head_masks(scale), head_masks(1.0)
    lane = lax.broadcasted_iota(jnp.int32, (tokens, 128), 1)
    sums = jnp.zeros((tokens, 128), f32)
    for g in range(width // GROUP):
        cols = slice(g * GROUP, (g + 1) * GROUP)
        cols_k = slice(width + g * GROUP, width + (g + 1) * GROUP)
        cols_v = slice(2 * width + g * GROUP, 2 * width + (g + 1) * GROUP)
        bias = small[SHIFT + 2 : SHIFT + 3, cols]
        qkv[:, cols] = (dot_nn(x[...], weight[:, cols]) + bias).astype(bf16)
        qkv[:, cols_k] = dot_nn(x[...], weight[:, cols_k]).astype(bf16)
        qkv[:, cols_v] = dot_nn(x[...], weight[:, cols_v]).astype(bf16)
        for part in (cols, cols_k, cols_v):
            pltpu.make_async_copy(qkv.at[:, part], qkv_far.at[:, part], sems.at[4]).start()
        mixed = jnp.zeros((tokens, GROUP), f32)
        for h in range(4):
            scores = dot_nt(qkv[:, cols] * scaled[h], qkv[:, cols_k])
            top = jnp.max(scores, axis=-1, keepdims=True)
            weights = jnp.exp(scores - top)
            total = jnp.sum(weights, axis=-1, keepdims=True)
            part = dot_nn(weights.astype(bf16), qkv[:, cols_v] * plain[h])
            mixed = mixed + part * (1.0 / total)
            sums = jnp.where(lane == g * 4 + h, top + jnp.log(total), sums)
        o_out[:, cols] = mixed.astype(bf16)
        ot[cols, :] = o_out[:, cols].T
        if not near:
            pltpu.make_async_copy(ot.at[cols], ot_far.at[cols], sems.at[5]).start()
    lse[...] = sums.T
    lse_store = pltpu.make_async_copy(lse, lse_far, sems.at[6])
    lse_store.start()
    for copy in w_stores + [lse_store]:
        copy.wait()
    xt_store.wait()
    pltpu.make_async_copy(qkv, qkv_far, sems.at[4]).wait()
    if not near:
        pltpu.make_async_copy(ot, ot_far, sems.at[5]).wait()


def tap_flags(small, taps, lanes):
    one = jnp.ones_like(small[SMALL : SMALL + 1, lanes])
    flags = [one, one, small[SMALL : SMALL + 1, lanes], small[SMALL + 1 : SMALL + 2, lanes]]
    return [flags[abs(j - taps // 2)] for j in range(taps)]


def tap_rows(small, taps, lanes):
    flags = tap_flags(small, taps, lanes)
    return [small[j : j + 1, lanes] * flags[j] for j in range(taps)]


def norm_rows(r, gain, shift):
    center = r - jnp.mean(r, axis=-1, keepdims=True)
    inverse = lax.rsqrt(jnp.mean(center * center, axis=-1, keepdims=True) + norm_eps)
    normed = center * inverse
    return normed * gain + shift, normed, inverse


def mix_kernel(block, count, ring_last, taps, near, relative, meta, table, x, o_ref, *refs):
    pieces = refs[:count]
    refs = refs[count:]
    y_out, refs = (None, refs) if relative else (refs[0], refs[1:])
    *refs, acc, y1, zpad, hc, sems = refs
    if near:
        outs, kept = refs[:-6], refs[-6:]
    else:
        outs, far, kept = refs[:-12], refs[-12:-6], refs[-6:]
    xh1, xh2, hct, stats, w_out, w_point = kept
    y_low = outs[0]
    stores = []

    def store(n, rows=None):
        if not near:
            source, target = kept[n], far[n]
            if rows is not None:
                source, target = source.at[rows], target.at[rows]
            copy = pltpu.make_async_copy(source, target, sems.at[4 + n])
            copy.start()
            if rows is None:
                stores.append(copy)

    small = table.at[pl.ds(SLOT * block, SLOT)]
    tokens, width = o_ref.shape
    half = width // 2
    copies = weight_copies(meta, pieces, w_out, sems.at[0], 0, half, ring_last)
    late_copies = weight_copies(meta, pieces, w_point, sems.at[1], half, half, ring_last)
    for copy in copies + late_copies:
        copy.start()
    zpad[0:PAD, :] = jnp.zeros((PAD, width), f32)
    zpad[tokens + PAD :, :] = jnp.zeros((PAD, width), f32)
    for copy in copies:
        copy.wait()
    store(4)
    for n in range(width // GROUP):
        cols = slice(n * GROUP, (n + 1) * GROUP)
        acc[:, cols] = dot_nn(o_ref[...], w_out[:, cols])

    def first_norm(row):
        rows = pl.ds(row, ROWS)
        stream = x[rows, :].astype(f32) + (acc[rows, :] + small[SHIFT + 3 : SHIFT + 4, :])
        out, normed, inverse = norm_rows(
            stream, small[GAIN : GAIN + 1, :], small[SHIFT : SHIFT + 1, :]
        )
        y1[rows, :] = out
        xh1[rows, :] = normed
        stats[rows, 0:1] = inverse
        zpad[pl.ds(row + PAD, ROWS), :] = out.astype(bf16).astype(f32)

    row_loop(tokens, first_norm)
    store(0)
    reach = taps // 2

    weights = tap_rows(small, taps, slice(None))

    def convolve(row):
        window = zpad[pl.ds(row, ROWS + 2 * PAD), :]
        total = jnp.zeros((ROWS, width), f32)
        for j in range(taps):
            start = PAD - reach + j
            total = total + weights[j] * window[start : start + ROWS]
        hc[pl.ds(row, ROWS), :] = total.astype(bf16)

    row_loop(tokens, convolve)
    hct[...] = hc[...].T
    store(2)
    for copy in late_copies:
        copy.wait()
    store(5)
    for n in range(width // GROUP):
        cols = slice(n * GROUP, (n + 1) * GROUP)
        acc[:, cols] = dot_nn(hc[...], w_point[:, cols])

    def second_norm(row):
        rows = pl.ds(row, ROWS)
        stream = y1[rows, :] + (acc[rows, :] + small[SHIFT + 4 : SHIFT + 5, :])
        out, normed, inverse = norm_rows(
            stream, small[GAIN + 1 : GAIN + 2, :], small[SHIFT + 1 : SHIFT + 2, :]
        )
        xh2[rows, :] = normed
        stats[rows, 1:2] = inverse
        store(1, rows)
        if not relative:
            y_out[rows, :] = out
            y_low[rows, :] = out.astype(bf16)
        else:
            y1[rows, :] = out

    row_loop(tokens, second_norm)
    store(3)
    for k in range(relative):
        part = tokens // relative
        first = pl.multiple_of((k ^ meta[0]) * part, part)
        outs[k][0] = y1[pl.ds(first, part), :].astype(bf16)
    for copy in stores:
        copy.wait()
    if not near:
        pltpu.make_async_copy(xh2, far[1], sems.at[5]).wait()


def norm_rows_back(upstream, normed, inverse, gain):
    scaled = upstream * gain
    inner = (
        scaled
        - jnp.mean(scaled, axis=-1, keepdims=True)
        - normed * jnp.mean(scaled * normed, axis=-1, keepdims=True)
    )
    return inverse * inner


def column_sum(a):
    return jnp.sum(a, axis=0, keepdims=True)


def store_parts(out, columns, value, meta, core):
    seqs, subs, rows, _ = out.shape
    for k in range(seqs):
        for m in range(subs):
            start = (k * subs + m) * rows
            seq, ring = k ^ meta[0], m ^ meta[1]
            seq = jnp.where(core == 0, flipped(seq, seqs), seq)
            ring = jnp.where(core == 0, flipped(ring, subs), ring)
            out[seq, ring, :, columns] = value[start : start + rows].astype(bf16)


def unmix_kernel(block, taps, last, meta, table, *refs):
    small = table.at[pl.ds(SLOT * block, SLOT)]
    if last:
        places, grads = refs[:2]
        refs = refs[2:]
    else:
        dy_ref = refs[0]
        refs = refs[1:]
    xh1, xh2, hct, stats, w_out, w_point, ot, *refs = refs
    dr1, do_out, sums, inner, keep, send, dr2, du, dpad, zpad = refs
    tokens, width = dr1.shape
    half = width // 2
    sums[...] = jnp.zeros_like(sums)
    if last:
        mine = jnp.minimum(meta[0], places.shape[0] - 1)
        picked = places.shape[2]
        token = lax.broadcasted_iota(jnp.int32, (tokens, picked), 0)
        live = jnp.where(meta[0] < places.shape[0], f32(1), f32(0))
        picks = jnp.where(token == places[mine], live, f32(0)).astype(bf16)
        dr2[...] = dot_nn(picks, grads[mine])
    for pad in (dpad, zpad):
        pad[0:PAD, :] = jnp.zeros((PAD, width), f32)
        pad[tokens + PAD :, :] = jnp.zeros((PAD, width), f32)

    def second_norm(row):
        rows = pl.ds(row, ROWS)
        dy = dr2[rows, :] if last else dy_ref[rows, :]
        normed = xh2[rows, :]
        back = norm_rows_back(dy, normed, stats[rows, 1:2], small[GAIN + 1 : GAIN + 2, :])
        low = back.astype(bf16)
        dr2[rows, :] = back
        du[rows, :] = low
        sums[GAIN + 1 : GAIN + 2, :] += column_sum(dy * normed)
        sums[SHIFT + 1 : SHIFT + 2, :] += column_sum(dy)
        sums[SHIFT + 4 : SHIFT + 5, :] += column_sum(low.astype(f32))
        z = xh1[rows, :] * small[GAIN : GAIN + 1, :] + small[SHIFT : SHIFT + 1, :]
        zpad[pl.ds(row + PAD, ROWS), :] = z.astype(bf16).astype(f32)

    row_loop(tokens, second_norm)
    c = meta[2]
    mine = pl.ds(pl.multiple_of(c * half, 128), half)
    other = pl.ds(pl.multiple_of((1 - c) * half, 128), half)
    point_cols, out_cols = slice(half, width), slice(0, half)
    for n in range(width // GROUP):
        cols = slice(n * GROUP, (n + 1) * GROUP)
        back = dot_nt(du[...], w_point[cols, :])
        dpad[PAD : PAD + tokens, cols] = back.astype(bf16).astype(f32)
    store_parts(send, point_cols, dot_nn(hct[...], du[:, other]), meta, 1 - c)
    store_parts(keep, point_cols, dot_nn(hct[...], du[:, mine]), meta, c)
    reach = taps // 2

    def unconvolve(lanes):
        weights = tap_rows(small, taps, lanes)
        flags = tap_flags(small, taps, lanes)
        tap_sums = [jnp.zeros((8, LANES), f32)] * taps
        for row in range(0, tokens, ROWS):
            window = dpad[row : row + ROWS + 2 * PAD, lanes]
            z_window = zpad[row : row + ROWS + 2 * PAD, lanes]
            here = window[PAD : PAD + ROWS]
            total = dr2[row : row + ROWS, lanes]
            for j in range(taps):
                start = PAD + reach - j
                total = total + weights[j] * window[start : start + ROWS]
                z_start = PAD - reach + j
                product = here * z_window[z_start : z_start + ROWS]
                tap_sums[j] = tap_sums[j] + jnp.sum(product.reshape(-1, 8, LANES), axis=0)
            dr2[row : row + ROWS, lanes] = total
        for j in range(taps):
            sums[j : j + 1, lanes] = column_sum(tap_sums[j]) * flags[j]

    strip_loop(width, unconvolve)

    def first_norm(row):
        rows = pl.ds(row, ROWS)
        total = dr2[rows, :]
        normed = xh1[rows, :]
        back = norm_rows_back(total, normed, stats[rows, 0:1], small[GAIN : GAIN + 1, :])
        low = back.astype(bf16)
        dr1[rows, :] = back
        du[rows, :] = low
        sums[GAIN : GAIN + 1, :] += column_sum(total * normed)
        sums[SHIFT : SHIFT + 1, :] += column_sum(total)
        sums[SHIFT + 3 : SHIFT + 4, :] += column_sum(low.astype(f32))

    row_loop(tokens, first_norm)
    for n in range(width // GROUP):
        cols = slice(n * GROUP, (n + 1) * GROUP)
        do_out[:, cols] = dot_nt(du[...], w_out[cols, :]).astype(bf16)
        both = do_out[:, cols].T.astype(f32) * ot[cols, :].astype(f32)
        for h in range(4):
            size = GROUP // 4
            inner[n * 4 + h : n * 4 + h + 1, :] = column_sum(both[h * size : (h + 1) * size])
    store_parts(send, out_cols, dot_nn(ot[...], du[:, other]), meta, 1 - c)
    store_parts(keep, out_cols, dot_nn(ot[...], du[:, mine]), meta, c)


def unattend_kernel(scale, meta, qkv, do_ref, lse, inner, dqkv, bias):
    tokens, width = do_ref.shape
    scaled, plain = head_masks(scale), head_masks(1.0)

    def unattend_group(g, columns, carry):
        cols, cols_k, cols_v = columns
        dq = jnp.zeros((tokens, GROUP), f32)
        dk = jnp.zeros((tokens, GROUP), f32)
        dv = jnp.zeros((tokens, GROUP), f32)
        for h in range(4):
            row = pl.ds(g * 4 + h, 1)
            q = qkv[:, cols] * scaled[h]
            do = do_ref[:, cols] * plain[h]
            scores = dot_nt(qkv[:, cols_k], q)
            probs = jnp.exp(scores - lse[row, :])
            dp = dot_nt(qkv[:, cols_v], do)
            ds = (probs * (dp - inner[row, :])).astype(bf16)
            dv = dv + dot_nn(probs.astype(bf16), do)
            dk = dk + dot_nn(ds, q)
            dq = dq + dot_tn(ds, qkv[:, cols_k] * scaled[h])
        low = dq.astype(bf16)
        dqkv[:, cols] = low
        bias[:, cols] = column_sum(low.astype(f32))
        dqkv[:, cols_k] = dk.astype(bf16)
        dqkv[:, cols_v] = dv.astype(bf16)
        return carry

    group_loop(width, unattend_group)(0)


def attn_grad_kernel(blocks, keep, meta, dqkv, xt, *refs):
    tables, (out, *refs) = refs[: 2 * blocks], refs[2 * blocks :]
    if not keep:
        mark, *refs = refs
        mark[...] = jnp.zeros_like(mark)
    width = xt.shape[0]
    half = 3 * width // 2
    part = half // 3
    core = meta[2] if keep else 1 - meta[2]
    for t in range(3):
        cols = pl.ds(pl.multiple_of(core * half + t * part, 128), part)
        value = dot_nn(xt[...], dqkv[:, cols])
        store_parts(out, slice(t * part, (t + 1) * part), value, meta, core)
    if blocks:
        small = refs[0]
        small[...] = jnp.zeros_like(small)
        for b in range(blocks):
            small[b * SLOT : (b + 1) * SLOT, :] = tables[2 * b][...]
            small[b * SLOT + SHIFT + 2 : b * SLOT + SHIFT + 3, :] = tables[2 * b + 1][...]
        extra = small[...].T * (core == 0).astype(f32)
        store_parts(out, slice(half, half + LANES), extra, meta, core)


def unproject_kernel(relative, meta, dqkv, dr1, weight, *refs):
    outs, dx = refs[:-1], refs[-1]
    tokens, width = dr1.shape
    target = dx if relative else outs[0]
    for n in range(width // GROUP):
        cols = slice(n * GROUP, (n + 1) * GROUP)
        target[:, cols] = dr1[:, cols] + dot_nt(dqkv[...], weight[cols, :])
    for k in range(relative):
        part = tokens // relative
        first = pl.multiple_of((k ^ meta[0]) * part, part)
        outs[k][0] = dx[pl.ds(first, part), :].astype(bf16)


def prepare_kernel(ends, meta, *refs):
    fars, (own, other, *refs) = refs[:7], refs[7:]
    *x_parts, table, inputs, attn, out, point, depth, gains, shifts, sems = refs
    nears = (inputs, attn, out, point, depth, gains, shifts)
    copies = [
        pltpu.make_async_copy(fars[n].at[m], nears[n].at[m], sems.at[n])
        for n in range(4)
        for m in range(nears[n].shape[0])
    ]
    copies += [pltpu.make_async_copy(fars[n], nears[n], sems.at[n]) for n in range(4, 7)]
    for copy in copies:
        copy.start()
    seq_count, blocks = inputs.shape[0], attn.shape[0]
    rows, half, cut = attn.shape[1], attn.shape[2] // 2, out.shape[2] // 2
    table[...] = jnp.zeros_like(table)
    for copy in copies:
        copy.wait()
    for b in range(blocks):
        start = b * SLOT
        for j in range(depth.shape[0]):
            table[start + j : start + j + 1, :rows] = depth[j, b : b + 1, :]
        table[start + GAIN : start + SHIFT, :rows] = gains[b]
        for j in range(shifts.shape[0]):
            at = start + SHIFT + j
            table[at : at + 1, :rows] = shifts[j, b : b + 1, :]
    small = table[...].T[:rows]
    for k, part in enumerate(x_parts):
        part[...] = inputs[jnp.minimum(meta[0] ^ k, seq_count - 1)]
    for to, core in ((own, meta[2]), (other, 1 - meta[2])):
        wide = pl.ds(pl.multiple_of(core * half, 128), half)
        narrow = pl.ds(pl.multiple_of(core * cut, 128), cut)
        to[:, half : half + LANES] = (small * (core == 0).astype(f32)).astype(bf16)
        for b in range(blocks):
            start = 0 if b == 0 else ends[2 * b - 1]
            to[:, start : start + half] = attn[b, :, wide].astype(bf16)
            start = ends[2 * b]
            to[:, start : start + cut] = out[b, :, narrow].astype(bf16)
            to[:, start + cut : start + 2 * cut] = point[b, :, narrow].astype(bf16)


def pair_kernel(meta, own, given, *refs):
    outs, (rows_ref,) = refs[:-1], refs[-1:]
    rows = own.shape[0]
    mine, theirs = own[...].astype(f32), given[...].astype(f32)
    rows_ref[0:rows, :] = jnp.where(meta[2] == 0, mine, theirs)
    rows_ref[rows : 2 * rows, :] = jnp.where(meta[2] == 0, theirs, mine)
    start = 0
    for out in outs:
        stop = start + out.shape[-1]
        out[0] = rows_ref[:, start:stop].astype(bf16)
        start = stop


def end_kernel(meta, kept, got, own, other, rows_ref):
    rows = own.shape[0]
    rows_ref[...] = kept[0].astype(f32) + got[0].astype(f32)
    first, second = rows_ref[0:rows, :], rows_ref[rows : 2 * rows, :]
    own[...] = jnp.where(meta[2] == 0, first, second)
    other[...] = jnp.where(meta[2] == 0, second, first).astype(bf16)


def settle_kernel(seqs, meta, *refs):
    *parts, out, mark, all_parts = refs
    mark[...] = jnp.zeros_like(mark)
    at = 0
    for part in parts:
        for n in range(part.shape[0]):
            all_parts[at] = part[n]
            at += 1
    for i in range(out.shape[0]):
        out[i] = all_parts[i ^ meta[0]].astype(out.dtype)


def adam_update(master, first, second, gradient, step_rate):
    first_new = beta_first * first + (1.0 - beta_first) * gradient
    second_new = beta_second * second + (1.0 - beta_second) * gradient * gradient
    first_hat = first_new / (1.0 - beta_first**STEP)
    second_hat = second_new / (1.0 - beta_second**STEP)
    updated = master - step_rate * (
        first_hat / (jnp.sqrt(second_hat) + adam_eps) + weight_decay * master
    )
    return (updated, first_new, second_new, updated.astype(jnp.bfloat16))


def adam_kernel(places, rates, smalls, meta, *refs):
    count = 2 * (1 + max(index for spots in places for index, _ in spots))
    grads, refs = refs[:count], refs[count:]
    arrays = len(places) + len(smalls)
    states = [refs[3 * n : 3 * n + 3] for n in range(arrays)]
    outs = [refs[3 * arrays + 4 * n : 3 * arrays + 4 * n + 4] for n in range(arrays)]
    *marks, table = refs[7 * arrays :]
    for mark in marks:
        mark[...] = jnp.zeros_like(mark)

    def pick(index, half, lanes):
        own, given = grads[2 * index][:, lanes], grads[2 * index + 1][:, lanes].astype(f32)
        return jnp.where(meta[2] == half, own, given)

    for spots, state, out, rate in zip(places, states, outs, rates):
        width = state[0].shape[2] // 2
        for b, (index, start) in enumerate(spots):
            for half in range(2):
                cols = slice(half * width, (half + 1) * width)
                gradient = pick(index, half, slice(start, start + width))
                values = adam_update(*[ref[b, :, cols] for ref in state], gradient, rate)
                for ref, value in zip(out, values):
                    ref[b, :, cols] = value
    if smalls:
        index, start = places[0][0]
        start += states[0][0].shape[2] // 2
        rows = grads[2 * index].shape[0]
        table[...] = jnp.zeros_like(table)
        table[:rows, :] = pick(index, 0, slice(start, start + LANES))
        sums = table[...].T
        for n, (row, rows_first, rate) in enumerate(smalls):
            state, out = states[len(places) + n], outs[len(places) + n]
            for i in range(state[0].shape[0]):
                if rows_first:
                    parts = [sums[b * SLOT + row + i :][:1] for b in range(state[0].shape[1])]
                    gradient = jnp.concatenate(parts)[:, :rows]
                else:
                    first = i * SLOT + row
                    gradient = sums[first : first + state[0].shape[1], :rows]
                values = adam_update(*[ref[i] for ref in state], gradient, rate)
                for ref, value in zip(out, values):
                    ref[i] = value


class Links:
    def __init__(self, seqs, copies):
        self.seqs, self.copies, self.ring = seqs, copies, copies // 2
        self.s = lax.axis_index("seq")
        position = lax.axis_index("dp")
        self.z, self.c = position // 2, position % 2

    def swap(self, array, seq=0, ring=0, core=0):
        pairs = [
            (s * self.copies + d, (s ^ seq) * self.copies + (d ^ (2 * ring + core)))
            for s in range(self.seqs)
            for d in range(self.copies)
        ]
        return lax.ppermute(array, AXES, pairs)

    def hop(self, array, axis, step):
        count = self.seqs if axis == "seq" else self.ring
        last = count.bit_length() - 2
        pairs = []
        for s in range(self.seqs):
            for d in range(self.copies):
                bit = 1 << (step if d % 2 == 0 else last - step)
                to_s, to_d = (s ^ bit, d) if axis == "seq" else (s, d ^ (2 * bit))
                pairs.append((s * self.copies + d, to_s * self.copies + to_d))
        return lax.ppermute(array, AXES, pairs)

    def steps(self, axis):
        return range((self.seqs if axis == "seq" else self.ring).bit_length() - 1)

    def place(self, m):
        return self.z ^ jnp.where(self.c == 0, m, flipped(m, self.ring))

    def around(self, block, axis, start=0, stop=None):
        for step in self.steps(axis)[start:stop]:
            block = join([block, self.hop(block, axis, step)])
        return block

    def ring_block(self, block):
        _, rows, half = block.shape
        if rows % 16 == 0:
            return block
        placed = jnp.zeros_like(block)
        for m in range(self.ring):
            placed = lax.dynamic_update_slice(
                placed, block[m : m + 1], (self.place(m), jnp.int32(0), jnp.int32(0))
            )
        return placed.reshape(1, self.ring * rows, half)

    def both_cores(self, blocks):
        return blocks + [self.swap(one, core=1) for one in blocks]

    def finish(self, block, axis):
        return self.both_cores([block, self.hop(block, axis, self.steps(axis)[-1])])

    def ring_terms(self, terms):
        terms = [term[0] for term in terms]
        if terms[0].shape[0] > 1:
            return terms
        total = terms[0][0].astype(f32)
        for term in terms[1:]:
            total = total + term[0].astype(f32)
        total = total.reshape(self.ring, total.shape[0] // self.ring, total.shape[1])
        units = []
        for m in range(self.ring):
            at = self.z ^ jnp.where(self.c == 0, flipped(m, self.ring), m)
            units.append(lax.dynamic_index_in_dim(total, at, 0, keepdims=False))
        return [jnp.stack(units).astype(bf16)]


def shards(
    inputs,
    masked_positions,
    masked_grads,
    kernel_paths,
    attn_weight,
    out_weight,
    point_weight,
    depth_weight,
    gains,
    shifts,
    first_attn,
    first_out,
    first_point,
    first_depth,
    first_gains,
    first_shifts,
    second_attn,
    second_out,
    second_point,
    second_depth,
    second_gains,
    second_shifts,
):
    seq_count, part_tokens, width = inputs.shape
    seqs, copies = lax.axis_size("seq"), lax.axis_size("dp")
    devices = seqs * copies
    tokens = seqs * part_tokens
    blocks, rows, _ = attn_weight.shape
    taps = depth_weight.shape[1]
    scale = (width // HEADS) ** (-0.5)
    links = Links(seqs, copies)
    aligned = (2 * rows) % 16 == 0
    subs = links.ring if aligned else 1
    part_rows = width // (seqs * subs)
    half = 3 * width // 2
    place = links.s
    mine = jnp.minimum(place, seq_count - 1)
    live = (place < seq_count).astype(jnp.int32)
    own_paths = lax.dynamic_index_in_dim(kernel_paths, mine, 0, keepdims=False)
    meta = jnp.concatenate(
        [
            jnp.stack([place, links.z if subs > 1 else jnp.zeros_like(links.z), links.c]),
            own_paths,
            live[None],
        ]
    ).astype(jnp.int32)
    full, meta = meta, Position(aligned)
    cut = width // 2
    ends = [half + LANES, half + LANES + width]
    ends += [ends[1] + half, ends[1] + half + width]

    def shape(*dims, dtype=f32):
        return jax.ShapeDtypeStruct(dims, dtype)

    dma = pltpu.SemaphoreType.DMA
    square = (width, width)
    wide = (width, 3 * width)

    def attend(b, parts, pieces, table, after=()):
        near = b == blocks - 1
        outs = (
            Stored(wide, bf16),
            Stored((width, tokens), bf16),
            Stored((tokens, 3 * width), bf16),
            shape(tokens, width, dtype=bf16),
            shape(width, tokens, dtype=bf16) if near else Stored((width, tokens), bf16),
            Stored((LANES, tokens), f32),
        )
        scratch = [
            pltpu.VMEM(wide, bf16),
            pltpu.VMEM((width, tokens), bf16),
            pltpu.VMEM((tokens, 3 * width), bf16),
            pltpu.VMEM((LANES, tokens), f32),
            dma((7,)),
        ]
        if not near:
            scratch = [pltpu.VMEM((width, tokens), bf16)] + scratch
        if b == 0:
            outs = (shape(blocks * SLOT, width), shape(tokens, width, dtype=bf16)) + outs
            scratch += [pltpu.VMEM((2, width, LANES), bf16)]
        return call(
            partial(attend_kernel, b, near, len(parts), scale),
            outs,
            [smem_spec()] + [vmem_spec()] * ((1 if b else 0) + len(parts) + len(pieces)),
            [full] + ([table] if b else []) + list(parts) + list(pieces),
            scratch,
            11 * 10**9,
            f"attend_{b}",
            after,
        )

    def mix(b, table, x, o, pieces, after=()):
        final = b == blocks - 1
        kept = (
            ((tokens, width), f32),
            ((tokens, width), f32),
            ((width, tokens), bf16),
            ((tokens, LANES), f32),
            (square, bf16),
            (square, bf16),
        )
        if final:
            outs = (shape(1, part_tokens, width, dtype=bf16),) * seqs
            outs += tuple(jax.ShapeDtypeStruct(*one) for one in kept)
        else:
            outs = (shape(tokens, width), shape(tokens, width, dtype=bf16))
            outs += tuple(Stored(*one) for one in kept)
        return call(
            partial(
                mix_kernel, b, len(pieces), final and aligned, taps, final, seqs if final else 0
            ),
            outs,
            [smem_spec()] + [vmem_spec()] * (3 + len(pieces)),
            [meta, table, x, o, *pieces],
            ([] if final else [pltpu.VMEM(*one) for one in kept])
            + [
                pltpu.VMEM((tokens, width), f32),
                pltpu.VMEM((tokens, width), f32),
                pltpu.VMEM((tokens + 2 * PAD, width), f32),
                pltpu.VMEM((tokens, width), bf16),
                dma((10,)),
            ],
            10**9,
            f"mix_{b}",
            after,
        )

    def unmix(b, table, upstream, saved, after=(), fetch=()):
        last = b == blocks - 1
        parts = shape(seqs, subs, part_rows, width, dtype=bf16)
        return call(
            partial(unmix_kernel, b, taps, last),
            (
                shape(tokens, width),
                shape(tokens, width, dtype=bf16),
                shape(SLOT, width),
                shape(SLOT, tokens),
                parts,
                parts,
            ),
            [smem_spec()] + [vmem_spec()] * (len(upstream) + 1 + len(saved)),
            [meta, table, *upstream, *saved],
            [
                pltpu.VMEM((tokens, width), f32),
                pltpu.VMEM((tokens, width), bf16),
                pltpu.VMEM((tokens + 2 * PAD, width), f32),
                pltpu.VMEM((tokens + 2 * PAD, width), f32),
            ],
            10 * 10**9,
            f"unmix_{b}",
            after,
            fetch,
        )

    def unattend(b, qkv, do, lse, inner, after=(), fetch=()):
        return call(
            partial(unattend_kernel, scale),
            (shape(tokens, 3 * width, dtype=bf16), shape(1, width)),
            [smem_spec()] + [vmem_spec()] * 4,
            [meta, qkv, do, lse, inner],
            [],
            11 * 10**9,
            f"unattend_{b}",
            after,
            fetch,
        )

    def attn_grad(b, keep, dqkv, xt, tables, after=()):
        span = half + (0 if b else LANES)
        return call(
            partial(attn_grad_kernel, len(tables) // 2, keep),
            (shape(seqs, subs, part_rows, span, dtype=bf16),) + (() if keep else (TOKEN,)),
            [smem_spec()] + [vmem_spec()] * (2 + len(tables)),
            [meta, dqkv, xt, *tables],
            [pltpu.VMEM((LANES, width), f32)] if tables else [],
            10**8,
            f"attn_grad_{b}",
            after,
        )

    def unproject(b, dqkv, dr1, weight, after=(), fetch=()):
        return call(
            partial(unproject_kernel, 0 if b else seqs),
            (shape(tokens, width),) if b else (shape(1, part_tokens, width, dtype=bf16),) * seqs,
            [smem_spec()] + [vmem_spec()] * 3,
            [meta, dqkv, dr1, weight],
            [pltpu.VMEM((tokens, width), f32)],
            4 * 10**9,
            f"unproject_{b}",
            after,
            fetch,
        )

    def settle(parts, dtype, after=()):
        return call(
            partial(settle_kernel, seqs),
            (shape(seq_count, part_tokens, width, dtype=dtype), TOKEN),
            [smem_spec()] + [vmem_spec()] * len(parts),
            [meta, *parts],
            [pltpu.VMEM((seqs, part_tokens, width), bf16)],
            10**8,
            "settle",
            after,
        )

    def end(kept, got, after=()):
        span = kept.shape[-1]
        own, other = call(
            end_kernel,
            (shape(rows, span), shape(rows, span, dtype=bf16)),
            [smem_spec(), vmem_spec(), vmem_spec()],
            [meta, kept, got],
            [pltpu.VMEM((2 * rows, span), f32)],
            10**8,
            "end",
            after,
        )
        return own, links.swap(other, core=1)

    def adam(places, rates, smalls, grads, states, fetch=()):
        outs = []
        for state in states:
            outs += [shape(*state[0].shape)] * 3 + [shape(*state[0].shape, dtype=bf16)]
        flat = [array for state in states for array in state]
        results = call(
            partial(adam_kernel, places, rates, smalls),
            (*outs, TOKEN) if fetch else outs,
            [smem_spec()] + [vmem_spec()] * (len(grads) + len(flat)),
            [meta, *grads, *flat],
            [pltpu.VMEM((LANES, LANES), f32)],
            10**8,
            "adam",
            (),
            fetch,
        )
        results, near = results if fetch else (results, ())
        return [results[4 * n : 4 * n + 4] for n in range(len(states))], results[-1], near

    depth_rows = [jnp.swapaxes(a, 0, 1) for a in (depth_weight, first_depth, second_depth)]
    shift_rows = [jnp.swapaxes(a, 0, 1) for a in (shifts, first_shifts, second_shifts)]
    own, other, *x_parts = call(
        partial(prepare_kernel, ends),
        (shape(rows, ends[3], dtype=bf16),) * 2
        + (shape(part_tokens, width, dtype=bf16),) * seqs,
        [smem_spec()] + [hbm_spec()] * 7,
        [meta, inputs, attn_weight, out_weight, point_weight, depth_rows[0], gains, shift_rows[0]],
        [pltpu.VMEM((LANES, LANES), f32)]
        + [
            pltpu.VMEM(array.shape, array.dtype)
            for array in (inputs, attn_weight, out_weight, point_weight)
            + (depth_rows[0], gains, shift_rows[0])
        ]
        + [dma((7,))],
        10**8,
        "prepare",
    )
    given = links.swap(other, core=1)
    widths = (ends[0], ends[2] - ends[0], width)
    unit_a0, unit_mid, unit_m1 = call(
        pair_kernel,
        tuple(shape(1, 2 * rows, span, dtype=bf16) for span in widths),
        [smem_spec(), vmem_spec(), vmem_spec()],
        [meta, own, given],
        [pltpu.VMEM((2 * rows, ends[3]), f32)],
        10**8,
        "pair",
    )
    x_parts = [x_parts[0]] + [links.swap(x_parts[k], seq=k) for k in range(1, seqs)]
    last_seq, last_ring = links.steps("seq")[-1], links.steps("ring")[-1]
    block_a0 = links.around(unit_a0, "ring", stop=-1)
    got_a0 = links.hop(block_a0, "ring", last_ring)
    plane_m1, marks = unit_m1, [*x_parts[1:]]
    if aligned:
        plane_m1, done = join_mark([unit_m1, links.hop(unit_m1, "seq", 0)])
        marks.append(done)
    ring_a0, done = join_mark([block_a0, got_a0], after=marks)
    ring_a0 = links.ring_block(ring_a0)
    got_a0 = links.hop(ring_a0[None], "seq", 0)
    unit_mid = join([unit_mid], after=(done,))
    got_mid = links.hop(unit_mid, "ring", 0)
    part_mid, done = join_mark([unit_mid, got_mid])
    marks = [done]
    if aligned:
        plane_m1, done = join_mark([plane_m1, links.hop(plane_m1, "seq", last_seq)])
        marks.append(done)
    plane_a0 = join([ring_a0[None], got_a0], after=marks)
    pieces_a0 = links.finish(plane_a0, "seq")
    ring_mid = links.ring_block(links.around(part_mid, "ring", 1))
    ring_m0, ring_a1 = ring_mid[..., :width], ring_mid[..., width:]
    got_m0 = [links.swap(ring_m0[None], seq=k) for k in range(1, seqs)]
    got_a1 = links.hop(ring_a1[None], "seq", 0)
    if aligned:
        got_m1 = links.hop(plane_m1[None], "ring", 0)
    table, x16, w_0, xt_0, qkv_0, o_0, ot_0, lse_0 = attend(
        0, x_parts, pieces_a0, None, after=(ring_m0, ring_a1)
    )
    marks = [table]
    if aligned:
        plane_m1, done = join_mark([plane_m1[None], got_m1], after=marks)
        marks.append(done)
    plane_a1, done = join_mark([ring_a1[None], got_a1], after=marks)
    got_m0, done = join_mark(got_m0, after=(done,))
    pieces_m0 = links.both_cores([ring_m0[None], got_m0])
    parts = [[links.hop(plane_a1, "seq", last_seq)]]
    if aligned:
        parts.append([links.hop(plane_m1, "ring", last_ring)])
    y_0, x_1, *saved_0 = mix(0, table, x16, o_0, pieces_m0, after=(done,))
    got_a1, *got_m1 = joins(parts, after=(x_1,))
    pieces_a1 = links.both_cores([plane_a1, got_a1])
    w_1, xt_1, qkv_1, o_1, ot_1, lse_1 = attend(1, [x_1], pieces_a1, table)
    if aligned:
        pieces_m1 = links.both_cores([plane_m1, *got_m1])
    else:
        ring_m1 = links.ring_block(links.around(unit_m1, "ring"))
        pieces_m1 = links.finish(links.around(ring_m1[None], "seq", stop=-1), "seq")
    outs_1 = mix(1, table, y_0, o_1, pieces_m1)
    y_1, saved_1 = outs_1[:seqs], outs_1[seqs:]

    y_back = [links.swap(y_1[k], seq=k) for k in range(1, seqs)]
    places = masked_positions[:, None, :]
    (dr1, do, sums_1, inner, keep, send), near = unmix(
        1, table, (places, masked_grads), (*saved_1, ot_1), fetch=(qkv_1, lse_1)
    )
    y_back, done = join_mark(y_back, after=(sums_1,))
    given_m1 = links.swap(send, core=1)
    terms_m1 = [keep, given_m1]
    (dqkv, bias_1), (xt, weight) = unattend(
        1, near[0], do, near[1], inner, after=(done,), fetch=(xt_1, w_1)
    )
    send, done = attn_grad(1, False, dqkv, xt, ())
    given_a1 = links.swap(send, core=1)
    (keep,) = attn_grad(1, True, dqkv, xt, (), after=(done,))
    late, sent, done = fold([terms_m1, [keep, given_a1]])
    got = links.hop(sent, "seq", 0)
    (dy,), near = unproject(1, dqkv, dr1, weight, after=(done,), fetch=(*saved_0, ot_0))
    (dr1, do, sums_0, inner, keep, send), near = unmix(0, table, (dy,), near, fetch=(qkv_0, lse_0))
    late, sent, done = fold([[late, got]], after=(sums_0,))
    got = links.hop(sent, "seq", 1)
    mixed, sent, done_mixed = fold([[keep, links.swap(send, core=1)]], after=(done,))
    got_mixed = links.hop(sent, "seq", 0)
    (dqkv, bias_0), (xt, weight) = unattend(
        0, near[0], do, near[1], inner, after=(done, done_mixed), fetch=(xt_0, w_0)
    )
    mixed, sent, done_mixed = fold([[mixed, got_mixed]], after=(bias_0,))
    got_mixed = links.hop(sent, "seq", 1)
    late, sent, done = fold([links.ring_terms([late, got])], after=(bias_0,))
    got = links.hop(sent, "ring", 0)
    tables = (sums_0, bias_0, sums_1, bias_1)
    send, done = attn_grad(0, False, dqkv, xt, tables, after=(done, done_mixed))
    given = links.swap(send, core=1)
    (keep,) = attn_grad(0, True, dqkv, xt, tables, after=(done,))
    final, sent, done = fold([[keep, given]], after=(touch(got_mixed),))
    got_final = links.hop(sent, "seq", 0)
    dx = unproject(0, dqkv, dr1, weight, after=(done, touch(got)))
    for step in links.steps("ring")[1:]:
        late, sent, done = fold([[late, got]], after=(dx[0],))
        got = links.hop(sent, "ring", step)
    mixed, sent, done_mixed = fold([links.ring_terms([mixed, got_mixed])], after=(dx[0], done))
    got_mixed = links.hop(sent, "ring", 0)
    final, sent, done = fold([[final, got_final]], after=(done_mixed,))
    got_final = links.hop(sent, "seq", 1)
    for step in links.steps("ring")[1:]:
        mixed, sent, done_mixed = fold([[mixed, got_mixed]], after=(done,))
        got_mixed = links.hop(sent, "ring", step)
    result, done_y = settle([y_1[0], y_back], bf16)
    final, sent, done = fold(
        [links.ring_terms([final, got_final])], after=(done_mixed, touch(got), done_y)
    )
    got_final = links.hop(sent, "ring", 0)
    dx_sent = joins([[one] for one in dx[1:]], after=(done,))
    x_back = [links.swap(dx_sent[k - 1], seq=k) for k in range(1, seqs)]
    for step in links.steps("ring")[1:]:
        final, sent = fold([[final, got_final]], after=(touch(got_mixed),), mark=False)
        got_final = links.hop(sent, "ring", step)
    x_back = join(x_back)
    input_grad, done_x = settle([dx[0], x_back], f32)
    grads = end(late, got) + end(mixed, got_mixed)
    (new_out, new_point), done_mix, states = adam(
        (((1, 0), (0, 0)), ((1, cut), (0, cut))),
        (rate_out, rate_point),
        (),
        grads,
        (
            (out_weight, first_out, second_out),
            (point_weight, first_point, second_point),
        ),
        fetch=(attn_weight, first_attn, second_attn),
    )
    (new_attn, new_depth, new_gains, new_shifts), _, _ = adam(
        (((0, 0), (1, width)),),
        (rate_attn,),
        ((0, True, rate_depth), (GAIN, False, rate_gain), (SHIFT, True, rate_vector)),
        end(final, got_final, (done_x, done_mix)) + grads[:2],
        (states, depth_rows, (gains, first_gains, second_gains), shift_rows),
    )
    new_depth, new_shifts = (
        [jnp.swapaxes(a, 0, 1) for a in new] for new in (new_depth, new_shifts)
    )
    updates = (new_attn, new_out, new_point, new_depth, new_gains, new_shifts)
    return (
        (result, input_grad)
        + tuple((entry[0] for entry in updates))
        + tuple((entry[1] for entry in updates))
        + tuple((entry[2] for entry in updates))
        + tuple((entry[3] for entry in updates))
    )


def solution(mesh):
    sequence = P("dp", "seq", None)
    matrix = P(None, AXES, None)
    vector = P(None, None, AXES)
    weights = (matrix,) * 3 + (vector,) * 3
    return jax.shard_map(
        shards,
        mesh=mesh,
        in_specs=(sequence, P("dp", None), P("dp", None, None), P("dp", None)) + weights * 3,
        out_specs=(sequence, sequence) + weights * 4,
        check_vma=False,
    )
```
